32 devices in a mesh: owner: 8 (over z, x), rep: 4 (over y, core).
Axes of the slice: x: 2, y: 2, z: 4, core: 2. Of those that a mesh axis runs over, the one named last changes fastest.
Arguments:
- stay_rows: bfloat16 [64, 256, 1024], P('owner', 'rep'), may hold values from -40 to 40
- stay_count: int32 [64, 4], P('owner', 'rep'), may hold values from 1 to 64, as said below
- moving_rows: bfloat16 [2048, 1024], P(('owner', 'rep')), may hold values from -5 to 5
- new_list: int32 [2048], P(('owner', 'rep')), may hold values from 0 to 63, as said below
- centroids: bfloat16 [64, 128, 1024], P('owner'), may hold values from -2 to 2
- sharpness: float32 [64], P('owner'), may hold values from 0.5 to 2
Outputs:
- refreshed: bfloat16 [64, 128, 1024], P('owner')
- mass: float32 [64, 128], P('owner', 'rep')
The draws below stay inside these ranges and needn't reach their ends.
Inputs may be any that keep to these rules, and one draw needn't show every extreme that they name: `stay_count`: slots 0 to count - 1 of a list on a replica are live; some entry equals 64. `new_list`: within the rows of one device, each list is named at most 2 times, and on every device some list is named exactly 2 times.
All inputs are finite; a program needn't handle non-finite values.
Results may differ from the reference program's by a relative error of at most 0.0032.
Values may be sent and summed in bfloat16 or wider, within the bound.
A program may use at most 64 MiB of HBM per device.

```python
import math
import jax
import jax.numpy as jnp
from jax import lax

D = 1024
F = 128
LIST_DEV = 8
CAP = 64
SLOT_L = 2
LISTS = 64
OUT_DEV = 64
MOVING = 2048
N_OWNER = 8
N_REP = 4


def centre_table(key):
    table = 0.5 * jax.random.normal(jax.random.fold_in(key, 11), (LISTS, F, D), jnp.float32)
    return jnp.clip(table, -2.0, 2.0)


def draw_centroids(key, part):
    return centre_table(key).astype(jnp.bfloat16)


def draw_stay_rows(key, part):
    values = jnp.clip(jax.random.normal(jax.random.fold_in(key, 13), (LISTS, N_REP * CAP, D), jnp.float32), -4.0, 4.0)
    return values.astype(jnp.bfloat16)


def draw_stay_count(key, part):
    base_key = jax.random.fold_in(key, 3)
    device_shift = jax.random.randint(jax.random.fold_in(base_key, 1), (LISTS // LIST_DEV, N_REP), 0, 3)
    shift_amount = jnp.repeat(device_shift, LIST_DEV, axis=0) + jax.random.randint(jax.random.fold_in(base_key, 2), (LISTS, N_REP), 0, 2)
    top_count = jnp.maximum(jnp.right_shift(jnp.full((LISTS, N_REP), CAP, jnp.int32), shift_amount.astype(jnp.int32)), 1)
    counts = 1 + jax.random.randint(jax.random.fold_in(base_key, 3), (LISTS, N_REP), 0, top_count)
    return counts.at[0, 0].set(CAP).astype(jnp.int32)


def route_targets(key):
    device_total = MOVING // OUT_DEV
    slot_total = LISTS * SLOT_L
    device_keys = jax.random.split(jax.random.fold_in(key, 5), device_total)

    def one_device(device_key):
        first_key = jax.random.fold_in(device_key, 1)
        second_key = jax.random.fold_in(device_key, 2)
        shuffled = jax.random.permutation(first_key, slot_total)
        chosen_list = shuffled[0] // SLOT_L
        order_key = jnp.where(shuffled // SLOT_L == chosen_list, slot_total + jnp.arange(slot_total), jnp.arange(slot_total))
        remaining = shuffled[jnp.argsort(order_key, stable=True)]
        picked = jnp.concatenate([chosen_list * SLOT_L + jnp.arange(SLOT_L), remaining[:OUT_DEV - SLOT_L]])
        return picked[jax.random.permutation(second_key, OUT_DEV)]
    return jax.vmap(one_device)(device_keys).reshape(-1).astype(jnp.int32)


def draw_new_list(key, part):
    return (route_targets(key) // SLOT_L).astype(jnp.int32)


def level_of(stream_key, shape, shards, smallest, largest):
    def one(position, blocks):
        heights = jax.random.uniform(jax.random.fold_in(jax.random.fold_in(stream_key, 6), position), (blocks,), jnp.float32, smallest / len(shards), largest / len(shards))
        return jnp.repeat(jnp.exp(heights), shape[position] // blocks).reshape((-1,) + (1,) * (len(shape) - position - 1))

    factor_of = one(*shards[0])
    for cut in shards[1:]:
        factor_of = factor_of * one(*cut)
    return factor_of


def gaussian(own_key, shape, width, bound, cuts=(), held_as=jnp.bfloat16):
    gain = level_of(own_key, shape, cuts, -0.22, 0.18) if cuts else 1.0
    entries = jax.random.normal(own_key, shape, jnp.float32) * width * gain
    return jnp.minimum(jnp.maximum(entries, -bound), bound).astype(held_as)


def setup_inputs(seed: int = 0) -> dict:
    keys = jax.random.split(jax.random.key(seed), 7)
    return {
        "stay_rows": draw_stay_rows(jax.random.fold_in(keys[6], 71), 0),
        "stay_count": draw_stay_count(jax.random.fold_in(keys[6], 71), 0),
        "moving_rows": gaussian(keys[2], (MOVING, D), 1.0, 5.0, ((0, 32),)),
        "new_list": draw_new_list(jax.random.fold_in(keys[6], 71), 0),
        "centroids": draw_centroids(jax.random.fold_in(keys[6], 71), 0),
        "sharpness": jnp.clip(jnp.exp(math.log(2.0) - 1.3862944 * jax.random.uniform(keys[5], (LISTS,), jnp.float32) ** level_of(keys[5], (LISTS,), ((0, 8),), -0.2, 0.2)), 0.5, 2.0),
    }


prior_weight = 1.0

def soft_stats(members, live_mask, centres, sharp):
    products = jnp.dot(members, centres.T, preferred_element_type=jnp.float32)
    centre_norm = lax.optimization_barrier(jnp.sum(jnp.square(centres.astype(jnp.float32)), axis=-1))
    scores = sharp * (2.0 * products - centre_norm[None, :]) / math.sqrt(D)
    weights = jax.nn.softmax(scores, axis=-1).astype(jnp.bfloat16) * live_mask[:, None].astype(jnp.bfloat16)
    numerator = jnp.dot(weights.T, members, preferred_element_type=jnp.float32)
    mass_sum = lax.optimization_barrier(jnp.sum(weights.astype(jnp.float32), axis=0))
    return (numerator, mass_sum)

def reference(stay_rows, stay_count, moving_rows, new_list, centroids, sharpness):
    limit = N_OWNER * N_REP * SLOT_L
    order = jnp.argsort(new_list, stable=True)
    arrived_sorted = jnp.concatenate([moving_rows[order], jnp.zeros((limit, D), moving_rows.dtype)], axis=0)
    arrive_count = jnp.zeros((LISTS,), jnp.int32).at[new_list].add(1).astype(jnp.int32)
    arrive_start = (jnp.cumsum(arrive_count) - arrive_count).astype(jnp.int32)

    def one_list(items):
        members, live_count, centres, sharp, offset, count = items
        stay_mask = (jnp.arange(CAP)[None, :] < live_count[:, None]).reshape(-1)
        first_num, first_mass = soft_stats(members, stay_mask, centres, sharp)
        arrivals = lax.dynamic_slice_in_dim(arrived_sorted, offset.astype(jnp.int32), limit, 0)
        arrive_mask = jnp.arange(limit) < count
        second_num, second_mass = soft_stats(arrivals, arrive_mask, centres, sharp)
        numerator = first_num + second_num
        mass_sum = first_mass + second_mass
        refreshed = ((numerator + prior_weight * centres.astype(jnp.float32)) / (mass_sum[:, None] + prior_weight)).astype(jnp.bfloat16)
        return (refreshed, mass_sum)
    refreshed, mass = lax.map(one_list, (stay_rows, stay_count, centroids, sharpness, arrive_start, arrive_count))
    return (refreshed, mass)
```

```python
import math

import jax
import jax.numpy as jnp
from jax import lax
from jax.experimental import pallas as pl
from jax.experimental.pallas import tpu as pltpu
from jax.sharding import PartitionSpec as P

SLOT_L = 2


prior_weight = 1.0


def partner(value, axis, stride):
    mask = 2**stride
    pairs = [(source, source ^ mask) for source in range(lax.axis_size(axis))]
    return lax.ppermute(value, axis, pairs)


def weigh(members, live_mask, centres, centre_norm, sharp, features):
    products = jnp.einsum("lrd,lfd->lrf", members, centres, preferred_element_type=jnp.float32)
    scores = sharp[:, None, None] * (2.0 * products - centre_norm[:, None, :]) / math.sqrt(features)
    weights = jax.nn.softmax(scores, axis=-1).astype(jnp.bfloat16) * live_mask[:, :, None]
    numerator = jnp.einsum("lrf,lrd->lfd", weights, members, preferred_element_type=jnp.float32)
    return (numerator, jnp.sum(weights.astype(jnp.float32), axis=1))


def local(stay_rows, stay_count, moving_rows, new_list, centroids, sharpness):
    owners = lax.axis_size("owner")
    replicas = lax.axis_size("rep")
    lists_here, capacity, features = stay_rows.shape
    fine_count = centroids.shape[1]
    centre_norm = jnp.sum(jnp.square(centroids.astype(jnp.float32)), axis=-1)
    outgoing_count = new_list.shape[0]
    order_index = jnp.arange(outgoing_count)
    earlier = (new_list[None, :] == new_list[:, None]) & (
        order_index[None, :] < order_index[:, None]
    )
    slot_index = jnp.sum(earlier.astype(jnp.int32), axis=1)
    local_list = new_list % lists_here
    target_owner = new_list // lists_here
    position = (local_list * owners + target_owner) * SLOT_L + slot_index
    slot_total = lists_here * owners * SLOT_L
    outgoing = (
        jnp.zeros((slot_total, features), jnp.bfloat16)
        .at[position]
        .set(moving_rows, unique_indices=True)
    )
    occupied = (
        jnp.zeros((slot_total,), jnp.bfloat16)
        .at[position]
        .set(jnp.ones((outgoing_count,), jnp.bfloat16), unique_indices=True)
    )
    arrived, present = (
        lax.all_to_all(
            outgoing.reshape(lists_here, owners, SLOT_L, features),
            "owner",
            split_axis=1,
            concat_axis=1,
            tiled=True,
        ),
        lax.all_to_all(
            occupied.reshape(lists_here, owners, SLOT_L),
            "owner",
            split_axis=1,
            concat_axis=1,
            tiled=True,
        ),
    )
    arrive_slots = owners * SLOT_L
    arrivals = arrived.reshape(lists_here, arrive_slots, features)
    present = present.reshape(lists_here, arrive_slots)
    live_count = stay_count[:, 0]
    replica = lax.axis_index("rep")
    fine_share = fine_count // replicas
    groups = max(1, replicas // lists_here)
    per_rep = max(1, lists_here // replicas)
    slot_mask = (jnp.arange(capacity)[None, :] < live_count[:, None]).astype(jnp.bfloat16)
    stay_pieces = stay_rows.reshape(lists_here * groups, capacity // groups, features)
    mask_pieces = slot_mask.reshape(lists_here * groups, capacity // groups)
    moved_stay, moved_mask = (
        lax.all_to_all(stay_pieces, "rep", split_axis=0, concat_axis=1, tiled=True),
        lax.all_to_all(mask_pieces, "rep", split_axis=0, concat_axis=1, tiled=True),
    )
    arrive_pieces = arrivals.reshape(lists_here * groups, arrive_slots // groups, features)
    present_pieces = present.reshape(lists_here * groups, arrive_slots // groups)
    moved_arrive, moved_present = (
        lax.all_to_all(arrive_pieces, "rep", split_axis=0, concat_axis=1, tiled=True),
        lax.all_to_all(present_pieces, "rep", split_axis=0, concat_axis=1, tiled=True),
    )
    members = jnp.concatenate([moved_stay, moved_arrive], axis=1)
    member_mask = jnp.concatenate([moved_mask, moved_present], axis=1)
    first_list = replica * per_rep // groups
    centres = lax.dynamic_slice_in_dim(centroids, first_list, per_rep, 0)
    norms = lax.dynamic_slice_in_dim(centre_norm, first_list, per_rep, 0)
    sharp = lax.dynamic_slice_in_dim(sharpness, first_list, per_rep, 0)
    numerator, mass_sum = weigh(members, member_mask, centres, norms, sharp, features)
    for bit_number in range(groups.bit_length() - 1):
        other_num, other_mass = partner((numerator, mass_sum), "rep", bit_number)
        numerator = numerator + other_num
        mass_sum = mass_sum + other_mass
    refreshed_all = (
        (numerator + prior_weight * centres.astype(jnp.float32))
        / (mass_sum[:, :, None] + prior_weight)
    ).astype(jnp.bfloat16)
    piece_rows = fine_count // groups
    part_index = replica % groups
    refreshed_piece = lax.dynamic_slice_in_dim(
        refreshed_all, part_index * piece_rows, piece_rows, 1
    ).reshape(per_rep * piece_rows, features)
    mass_piece = lax.dynamic_slice_in_dim(mass_sum, part_index * piece_rows, piece_rows, 1).reshape(
        per_rep * piece_rows
    )
    refreshed = lax.all_gather(refreshed_piece, "rep", axis=0, tiled=True).reshape(
        lists_here, fine_count, features
    )
    mass_whole = lax.all_gather(mass_piece, "rep", axis=0, tiled=True).reshape(
        lists_here, fine_count
    )
    return (refreshed, lax.dynamic_slice_in_dim(mass_whole, replica * fine_share, fine_share, 1))


LANES = 128
VMEM_BUDGET = 40 * 2**20
MESH = pl.DeviceIdType.MESH


class Plan:
    def __init__(self, owners, replicas, lists, capacity, features, fine, moving):
        self.owners, self.replicas, self.lists = owners, replicas, lists
        self.capacity, self.features, self.fine, self.moving = capacity, features, fine, moving
        self.split = 2 if replicas % 2 == 0 and lists % 2 == 0 else 1
        self.groups = replicas // self.split
        self.half = lists // self.split
        self.per_source = self.half * SLOT_L
        self.block = self.groups * self.per_source
        self.blocks = owners * self.split
        self.width = features + LANES
        self.moving_lanes = -(-moving // LANES) * LANES

    def fits(self):
        slots = 2 * self.blocks * self.block * self.width
        held = self.half * self.replicas * self.capacity * self.features
        centres = 2 * self.half * self.fine * self.features
        gathered = self.groups * self.moving * self.features
        small = 2 * (slots + held + centres + gathered)
        return (
            small <= VMEM_BUDGET
            and self.block % 16 == 0
            and self.capacity % 16 == 0
            and self.moving % 16 == 0
            and self.features % LANES == 0
            and self.fine % LANES == 0
        )


def weigh_rows(plan, centres, norm, sharp, rows, mask):
    products = lax.dot_general(
        centres, rows, (((1,), (1,)), ((), ())), preferred_element_type=jnp.float32
    )
    scores = sharp * (2.0 * products - norm) / math.sqrt(plan.features)
    top = jnp.max(scores, axis=0, keepdims=True)
    raised = jnp.exp(scores - top)
    weights = (raised / jnp.sum(raised, axis=0, keepdims=True)).astype(jnp.bfloat16)
    weights = weights * mask.astype(jnp.bfloat16)
    numerator = jnp.dot(weights, rows, preferred_element_type=jnp.float32)
    mass = jnp.sum(weights.astype(jnp.float32), axis=1, keepdims=True)
    ones = jnp.ones((8, rows.shape[0]), jnp.bfloat16)
    mass_row = lax.dot_general(
        ones, weights, (((1,), (1,)), ((), ())), preferred_element_type=jnp.float32
    )
    return numerator, mass, mass_row


def fused_kernel(
    plan,
    stay_ref, count_ref, moving_ref, list_ref, centre_ref, sharp_ref,
    out_ref, mass_ref,
    stay_buf, count_buf, moving_buf, pos_own, pos_buf, placed, arrived, centre_buf, result_buf, mass_buf,
    stay_send, stay_recv, count_send, count_recv, moving_send, moving_recv, pos_send, pos_recv,
    slot_send, slot_recv, centre_sem, result_send, result_recv, mass_send, mass_recv, local_sem,
):
    owners, split, groups, half = plan.owners, plan.split, plan.groups, plan.half
    replicas, capacity, features = plan.replicas, plan.capacity, plan.features
    owner = lax.axis_index("owner")
    replica = lax.axis_index("rep")
    core = replica % split
    group = replica // split

    def rep_at(k, dc):
        return lax.rem(group + k, groups) * split + lax.rem(core + dc, split)

    def owner_at(k):
        return lax.rem(owner + k, owners)

    peers = [(k, dc) for k in range(groups) for dc in range(split) if (k, dc) != (0, 0)]
    plane = [(k, dc) for k in range(1, owners) for dc in range(split)]
    barrier = pltpu.get_barrier_semaphore()
    for k, dc in peers:
        pl.semaphore_signal(barrier, inc=1, device_id=(owner, rep_at(k, dc)), device_id_type=MESH)
    for k, dc in plane:
        pl.semaphore_signal(
            barrier, inc=1, device_id=(owner_at(k), rep_at(0, dc)), device_id_type=MESH
        )

    centre_copy = pltpu.make_async_copy(
        centre_ref.at[pl.ds(core * half, half)], centre_buf, centre_sem
    )
    centre_copy.start()

    def own_copy(j):
        return pltpu.make_async_copy(
            stay_ref.at[core * half + j], stay_buf.at[j, 0], stay_recv.at[j, 0]
        )

    for j in range(half):
        own_copy(j).start()

    moving = plan.moving
    count_buf[0] = jnp.broadcast_to(count_ref[...], count_buf.shape[1:])
    names = jnp.broadcast_to(list_ref[...], (moving, moving))
    row = lax.broadcasted_iota(jnp.int32, (moving, moving), 0)
    column = lax.broadcasted_iota(jnp.int32, (moving, moving), 1)
    down = jnp.sum(jnp.where(row == column, names, 0), axis=1, keepdims=True)
    earlier = jnp.where((names == down) & (row < column), 1, 0)
    slot = jnp.sum(earlier, axis=0, keepdims=True)
    target = list_ref[...]
    position = (
        (target // half) * plan.block + group * plan.per_source + (target % half) * SLOT_L + slot
    )
    pos_own[...] = jnp.full(pos_own.shape, -1, jnp.int32)
    pos_own[:, :moving] = jnp.broadcast_to(position, (8, moving))

    pl.semaphore_wait(barrier, len(peers) + len(plane))

    def moving_copy(k):
        return pltpu.make_async_remote_copy(
            src_ref=moving_ref, dst_ref=moving_buf.at[k - 1],
            send_sem=moving_send.at[k - 1], recv_sem=moving_recv.at[k - 1],
            device_id=(owner, rep_at(k, 0)), device_id_type=MESH,
        )

    def pos_copy(k):
        return pltpu.make_async_remote_copy(
            src_ref=pos_own, dst_ref=pos_buf.at[k - 1],
            send_sem=pos_send.at[k - 1], recv_sem=pos_recv.at[k - 1],
            device_id=(owner, rep_at(k, 0)), device_id_type=MESH,
        )

    for k in range(1, groups):
        pos_copy(k).start()
        moving_copy(k).start()

    def count_copy(k, dc):
        q = k * split + dc
        return pltpu.make_async_remote_copy(
            src_ref=count_buf.at[0], dst_ref=count_buf.at[q],
            send_sem=count_send.at[q], recv_sem=count_recv.at[q],
            device_id=(owner, rep_at(k, dc)), device_id_type=MESH,
        )

    def stay_copy(j, k, dc):
        q = k * split + dc
        return pltpu.make_async_remote_copy(
            src_ref=stay_ref.at[lax.rem(core + dc, split) * half + j], dst_ref=stay_buf.at[j, q],
            send_sem=stay_send.at[j, q], recv_sem=stay_recv.at[j, q],
            device_id=(owner, rep_at(k, dc)), device_id_type=MESH,
        )

    for k, dc in peers:
        count_copy(k, dc).start()
    for j in range(half):
        for k, dc in peers:
            stay_copy(j, k, dc).start()

    total = plan.blocks * plan.block
    slot_row = lax.broadcasted_iota(jnp.int32, (total, moving), 0)

    def one_hot(positions):
        return jnp.where(slot_row == positions, 1.0, 0.0).astype(jnp.bfloat16)

    pick = one_hot(pos_own[0:1, :moving])
    ones = jnp.ones((moving, LANES), jnp.bfloat16)
    rows = jnp.dot(pick, moving_ref[...], preferred_element_type=jnp.float32)
    flags = jnp.dot(pick, ones, preferred_element_type=jnp.float32)
    for k in range(1, groups):
        pos_copy(k).wait_recv()
        moving_copy(k).wait_recv()
        pick = one_hot(pos_buf[k - 1, 0:1, :moving])
        rows += jnp.dot(pick, moving_buf[k - 1], preferred_element_type=jnp.float32)
        flags += jnp.dot(pick, ones, preferred_element_type=jnp.float32)
    placed[:, :, :features] = rows.astype(jnp.bfloat16).reshape(plan.blocks, plan.block, features)
    placed[:, :, features:] = flags.astype(jnp.bfloat16).reshape(plan.blocks, plan.block, LANES)

    def slot_copy(k, dc):
        b = k * split + dc
        return pltpu.make_async_remote_copy(
            src_ref=placed.at[owner_at(k) * split + lax.rem(core + dc, split)],
            dst_ref=arrived.at[b],
            send_sem=slot_send.at[b], recv_sem=slot_recv.at[b],
            device_id=(owner_at(k), rep_at(0, dc)), device_id_type=MESH,
        )

    sent = [(k, dc) for k in range(owners) for dc in range(split) if (k, dc) != (0, 0)]
    for k, dc in sent:
        slot_copy(k, dc).start()
    arrived[0] = placed[owner * split + core]
    centre_copy.wait()
    for k, dc in peers:
        count_copy(k, dc).wait_recv()
    for k, dc in sent:
        slot_copy(k, dc).wait_recv()

    lane = lax.broadcasted_iota(jnp.int32, (1, replicas * capacity), 1)
    arrived_lane = lax.broadcasted_iota(jnp.int32, (1, total), 1)
    arrived_list = (arrived_lane % plan.per_source) // SLOT_L

    def result_copy(j, dc):
        return pltpu.make_async_remote_copy(
            src_ref=result_buf.at[j], dst_ref=out_ref.at[core * half + j],
            send_sem=result_send.at[j, dc], recv_sem=result_recv.at[j, dc],
            device_id=(owner, rep_at(0, dc)), device_id_type=MESH,
        )

    def result_own(j):
        return pltpu.make_async_copy(
            result_buf.at[j], out_ref.at[core * half + j], result_recv.at[j, 0]
        )

    def one_list(j, carry):
        own_copy(j).wait()
        for k, dc in peers:
            stay_copy(j, k, dc).wait_recv()
        centres = centre_buf[j]
        wide = centres.astype(jnp.float32)
        norm = jnp.sum(wide * wide, axis=1, keepdims=True)
        sharp = sharp_ref[core * half + j]
        counts = count_buf[0, pl.ds(core * half + j, 1), :]
        for q in range(1, replicas):
            counts = jnp.where(
                lane // capacity == q, count_buf[q, pl.ds(core * half + j, 1), :], counts
            )
        mask = jnp.where(lane % capacity < counts, 1.0, 0.0)
        members = stay_buf[j].reshape(replicas * capacity, features)
        num, mass, mass_row = weigh_rows(plan, centres, norm, sharp, members, mask)
        rows = arrived[:, :, :features].reshape(total, features)
        marks = arrived[:, :, features:].reshape(total, LANES)
        spread = jnp.full((8, LANES), 1.0 / LANES, jnp.bfloat16)
        present = lax.dot_general(
            spread, marks, (((1,), (1,)), ((), ())), preferred_element_type=jnp.float32
        )[0:1]
        here = jnp.where(arrived_list == j, present, 0.0)
        num2, mass2, mass_row2 = weigh_rows(plan, centres, norm, sharp, rows, here)
        mass = mass + mass2
        result_buf[j] = (
            (num + num2 + prior_weight * wide) / (mass + prior_weight)
        ).astype(jnp.bfloat16)
        mass_buf[j] = mass_row + mass_row2
        result_own(j).start()
        for dc in range(1, split):
            result_copy(j, dc).start()
        return carry

    lax.fori_loop(0, half, one_list, 0)

    def mass_copy(dc):
        return pltpu.make_async_remote_copy(
            src_ref=mass_buf, dst_ref=mass_ref.at[core],
            send_sem=mass_send.at[dc], recv_sem=mass_recv.at[dc],
            device_id=(owner, rep_at(0, dc)), device_id_type=MESH,
        )

    mass_own = pltpu.make_async_copy(mass_buf, mass_ref.at[core], local_sem)
    mass_own.start()
    for dc in range(1, split):
        mass_copy(dc).start()

    for k in range(1, groups):
        pos_copy(k).wait_send()
        moving_copy(k).wait_send()
    for k, dc in peers:
        count_copy(k, dc).wait_send()
    for j in range(half):
        for k, dc in peers:
            stay_copy(j, k, dc).wait_send()
    for k, dc in sent:
        slot_copy(k, dc).wait_send()
    for j in range(half):
        result_own(j).wait()
        for dc in range(1, split):
            result_copy(j, dc).wait()
    mass_own.wait()
    for dc in range(1, split):
        mass_copy(dc).wait()


def fused(plan, stay_rows, stay_count, moving_rows, new_list, centroids, sharpness):
    half, split, replicas = plan.half, plan.split, plan.replicas
    any_space = pl.BlockSpec(memory_space=pl.ANY)
    vmem = pl.BlockSpec(memory_space=pltpu.VMEM)
    dma = pltpu.SemaphoreType.DMA
    members = replicas * plan.capacity
    refreshed, mass = pl.pallas_call(
        lambda *refs: fused_kernel(plan, *refs),
        out_shape=(
            jax.ShapeDtypeStruct(centroids.shape, jnp.bfloat16),
            jax.ShapeDtypeStruct((split, half, 8, plan.fine), jnp.float32),
        ),
        in_specs=[any_space, vmem, vmem, vmem, any_space, pl.BlockSpec(memory_space=pltpu.SMEM)],
        out_specs=(any_space, any_space),
        scratch_shapes=[
            pltpu.VMEM((half, replicas, plan.capacity, plan.features), jnp.bfloat16),
            pltpu.VMEM((replicas, plan.lists, members), jnp.int32),
            pltpu.VMEM((max(1, plan.groups - 1), plan.moving, plan.features), jnp.bfloat16),
            pltpu.VMEM((8, plan.moving_lanes), jnp.int32),
            pltpu.VMEM((max(1, plan.groups - 1), 8, plan.moving_lanes), jnp.int32),
            pltpu.VMEM((plan.blocks, plan.block, plan.width), jnp.bfloat16),
            pltpu.VMEM((plan.blocks, plan.block, plan.width), jnp.bfloat16),
            pltpu.VMEM((half, plan.fine, plan.features), jnp.bfloat16),
            pltpu.VMEM((half, plan.fine, plan.features), jnp.bfloat16),
            pltpu.VMEM((half, 8, plan.fine), jnp.float32),
            dma((half, replicas)), dma((half, replicas)),
            dma((replicas,)), dma((replicas,)),
            dma((plan.groups,)), dma((plan.groups,)),
            dma((plan.groups,)), dma((plan.groups,)),
            dma((plan.blocks,)), dma((plan.blocks,)),
            dma,
            dma((half, split)), dma((half, split)),
            dma((split,)), dma((split,)),
            dma,
        ],
        compiler_params=pltpu.CompilerParams(
            collective_id=0, has_side_effects=True, vmem_limit_bytes=48 * 2**20
        ),
    )(stay_rows, stay_count, moving_rows, new_list.reshape(1, -1), centroids, sharpness)
    fine_share = plan.fine // replicas
    whole = mass[:, :, 0, :].reshape(plan.lists, plan.fine)
    share = lax.dynamic_slice_in_dim(whole, lax.axis_index("rep") * fine_share, fine_share, 1)
    return refreshed, share


def device_program(stay_rows, stay_count, moving_rows, new_list, centroids, sharpness):
    lists_here, capacity, features = stay_rows.shape
    plan = Plan(
        lax.axis_size("owner"), lax.axis_size("rep"), lists_here, capacity, features,
        centroids.shape[1], moving_rows.shape[0],
    )
    step = (lambda *a: fused(plan, *a)) if plan.fits() else local
    return step(stay_rows, stay_count, moving_rows, new_list, centroids, sharpness)


def solution(mesh):
    in_specs = (
        P("owner", "rep", None),
        P("owner", "rep"),
        P(("owner", "rep"), None),
        P(("owner", "rep")),
        P("owner", None, None),
        P("owner"),
    )
    out_specs = (P("owner", None, None), P("owner", "rep"))
    return jax.shard_map(device_program, mesh=mesh, in_specs=in_specs, out_specs=out_specs, check_vma=False)
```

```python
import math

import jax
import jax.numpy as jnp
from jax import lax
from jax.experimental import pallas as pl
from jax.experimental.pallas import tpu as pltpu
from jax.sharding import PartitionSpec as P

SLOT_L = 2


prior_weight = 1.0


def partner(value, axis, stride):
    mask = 2**stride
    pairs = [(source, source ^ mask) for source in range(lax.axis_size(axis))]
    return lax.ppermute(value, axis, pairs)


def weigh(members, live_mask, centres, centre_norm, sharp, features):
    products = jnp.einsum("lrd,lfd->lrf", members, centres, preferred_element_type=jnp.float32)
    scores = sharp[:, None, None] * (2.0 * products - centre_norm[:, None, :]) / math.sqrt(features)
    weights = jax.nn.softmax(scores, axis=-1).astype(jnp.bfloat16) * live_mask[:, :, None]
    numerator = jnp.einsum("lrf,lrd->lfd", weights, members, preferred_element_type=jnp.float32)
    return (numerator, jnp.sum(weights.astype(jnp.float32), axis=1))


def local(stay_rows, stay_count, moving_rows, new_list, centroids, sharpness):
    owners = lax.axis_size("owner")
    replicas = lax.axis_size("rep")
    lists_here, capacity, features = stay_rows.shape
    fine_count = centroids.shape[1]
    centre_norm = jnp.sum(jnp.square(centroids.astype(jnp.float32)), axis=-1)
    outgoing_count = new_list.shape[0]
    order_index = jnp.arange(outgoing_count)
    earlier = (new_list[None, :] == new_list[:, None]) & (
        order_index[None, :] < order_index[:, None]
    )
    slot_index = jnp.sum(earlier.astype(jnp.int32), axis=1)
    local_list = new_list % lists_here
    target_owner = new_list // lists_here
    position = (local_list * owners + target_owner) * SLOT_L + slot_index
    slot_total = lists_here * owners * SLOT_L
    outgoing = (
        jnp.zeros((slot_total, features), jnp.bfloat16)
        .at[position]
        .set(moving_rows, unique_indices=True)
    )
    occupied = (
        jnp.zeros((slot_total,), jnp.bfloat16)
        .at[position]
        .set(jnp.ones((outgoing_count,), jnp.bfloat16), unique_indices=True)
    )
    arrived, present = (
        lax.all_to_all(
            outgoing.reshape(lists_here, owners, SLOT_L, features),
            "owner",
            split_axis=1,
            concat_axis=1,
            tiled=True,
        ),
        lax.all_to_all(
            occupied.reshape(lists_here, owners, SLOT_L),
            "owner",
            split_axis=1,
            concat_axis=1,
            tiled=True,
        ),
    )
    arrive_slots = owners * SLOT_L
    arrivals = arrived.reshape(lists_here, arrive_slots, features)
    present = present.reshape(lists_here, arrive_slots)
    live_count = stay_count[:, 0]
    replica = lax.axis_index("rep")
    fine_share = fine_count // replicas
    groups = max(1, replicas // lists_here)
    per_rep = max(1, lists_here // replicas)
    slot_mask = (jnp.arange(capacity)[None, :] < live_count[:, None]).astype(jnp.bfloat16)
    stay_pieces = stay_rows.reshape(lists_here * groups, capacity // groups, features)
    mask_pieces = slot_mask.reshape(lists_here * groups, capacity // groups)
    moved_stay, moved_mask = (
        lax.all_to_all(stay_pieces, "rep", split_axis=0, concat_axis=1, tiled=True),
        lax.all_to_all(mask_pieces, "rep", split_axis=0, concat_axis=1, tiled=True),
    )
    arrive_pieces = arrivals.reshape(lists_here * groups, arrive_slots // groups, features)
    present_pieces = present.reshape(lists_here * groups, arrive_slots // groups)
    moved_arrive, moved_present = (
        lax.all_to_all(arrive_pieces, "rep", split_axis=0, concat_axis=1, tiled=True),
        lax.all_to_all(present_pieces, "rep", split_axis=0, concat_axis=1, tiled=True),
    )
    members = jnp.concatenate([moved_stay, moved_arrive], axis=1)
    member_mask = jnp.concatenate([moved_mask, moved_present], axis=1)
    first_list = replica * per_rep // groups
    centres = lax.dynamic_slice_in_dim(centroids, first_list, per_rep, 0)
    norms = lax.dynamic_slice_in_dim(centre_norm, first_list, per_rep, 0)
    sharp = lax.dynamic_slice_in_dim(sharpness, first_list, per_rep, 0)
    numerator, mass_sum = weigh(members, member_mask, centres, norms, sharp, features)
    for bit_number in range(groups.bit_length() - 1):
        other_num, other_mass = partner((numerator, mass_sum), "rep", bit_number)
        numerator = numerator + other_num
        mass_sum = mass_sum + other_mass
    refreshed_all = (
        (numerator + prior_weight * centres.astype(jnp.float32))
        / (mass_sum[:, :, None] + prior_weight)
    ).astype(jnp.bfloat16)
    piece_rows = fine_count // groups
    part_index = replica % groups
    refreshed_piece = lax.dynamic_slice_in_dim(
        refreshed_all, part_index * piece_rows, piece_rows, 1
    ).reshape(per_rep * piece_rows, features)
    mass_piece = lax.dynamic_slice_in_dim(mass_sum, part_index * piece_rows, piece_rows, 1).reshape(
        per_rep * piece_rows
    )
    refreshed = lax.all_gather(refreshed_piece, "rep", axis=0, tiled=True).reshape(
        lists_here, fine_count, features
    )
    mass_whole = lax.all_gather(mass_piece, "rep", axis=0, tiled=True).reshape(
        lists_here, fine_count
    )
    return (refreshed, lax.dynamic_slice_in_dim(mass_whole, replica * fine_share, fine_share, 1))


LANES = 128
VMEM_BUDGET = 40 * 2**20
MESH = pl.DeviceIdType.MESH


class Plan:
    def __init__(self, owners, replicas, lists, capacity, features, fine, moving):
        self.owners, self.replicas, self.lists = owners, replicas, lists
        self.capacity, self.features, self.fine, self.moving = capacity, features, fine, moving
        self.split = 2 if replicas % 2 == 0 and lists % 2 == 0 else 1
        self.groups = replicas // self.split
        self.half = lists // self.split
        self.per_source = self.half * SLOT_L
        self.block = self.groups * self.per_source
        self.blocks = owners * self.split
        self.width = features + LANES
        self.moving_lanes = -(-moving // LANES) * LANES

    def fits(self):
        slots = 2 * self.blocks * self.block * self.width
        held = self.half * self.replicas * self.capacity * self.features
        centres = 2 * self.half * self.fine * self.features
        gathered = self.groups * self.moving * self.features
        small = 2 * (slots + held + centres + gathered)
        return (
            small <= VMEM_BUDGET
            and self.block % 16 == 0
            and self.capacity % 16 == 0
            and self.moving % 16 == 0
            and self.features % LANES == 0
            and self.fine % LANES == 0
        )


def weigh_rows(plan, centres, norm, sharp, rows, mask):
    products = lax.dot_general(
        centres, rows, (((1,), (1,)), ((), ())), preferred_element_type=jnp.float32
    )
    scores = sharp * (2.0 * products - norm) / math.sqrt(plan.features)
    top = jnp.max(scores, axis=0, keepdims=True)
    raised = jnp.exp(scores - top)
    weights = (raised / jnp.sum(raised, axis=0, keepdims=True)).astype(jnp.bfloat16)
    weights = weights * mask.astype(jnp.bfloat16)
    numerator = jnp.dot(weights, rows, preferred_element_type=jnp.float32)
    mass = jnp.sum(weights.astype(jnp.float32), axis=1, keepdims=True)
    ones = jnp.ones((8, rows.shape[0]), jnp.bfloat16)
    mass_row = lax.dot_general(
        ones, weights, (((1,), (1,)), ((), ())), preferred_element_type=jnp.float32
    )
    return numerator, mass, mass_row


def fused_kernel(
    plan,
    stay_ref, count_in, moving_ref, list_in, centre_ref, sharp_in,
    out_ref, mass_ref,
    count_ref, moving_own, list_ref, sharp_ref, operand_sem, total_buf, mass_col,
    stay_buf, count_buf, moving_buf, pos_own, pos_buf, placed, arrived, centre_buf, result_buf, mass_buf,
    stay_send, stay_recv, count_send, count_recv, moving_send, moving_recv, pos_send, pos_recv,
    slot_send, slot_recv, centre_sem, result_send, result_recv, mass_send, mass_recv, local_sem,
):
    owners, split, groups, half = plan.owners, plan.split, plan.groups, plan.half
    replicas, capacity, features = plan.replicas, plan.capacity, plan.features
    owner = lax.axis_index("owner")
    replica = lax.axis_index("rep")
    core = replica % split
    group = replica // split

    def rep_at(k, dc):
        return lax.rem(group + k, groups) * split + lax.rem(core + dc, split)

    def owner_at(k):
        return lax.rem(owner + k, owners)

    peers = [(k, dc) for k in range(groups) for dc in range(split) if (k, dc) != (0, 0)]
    plane = [(k, dc) for k in range(1, owners) for dc in range(split)]
    barrier = pltpu.get_barrier_semaphore()
    for k, dc in peers:
        pl.semaphore_signal(barrier, inc=1, device_id=(owner, rep_at(k, dc)), device_id_type=MESH)
    for k, dc in plane:
        pl.semaphore_signal(
            barrier, inc=1, device_id=(owner_at(k), rep_at(0, dc)), device_id_type=MESH
        )

    small = [
        pltpu.make_async_copy(source, held, operand_sem.at[i])
        for i, (source, held) in enumerate([
            (list_in, list_ref), (count_in, count_ref), (moving_ref, moving_own), (sharp_in, sharp_ref),
        ])
    ]
    for copy in small:
        copy.start()
    centre_copy = pltpu.make_async_copy(
        centre_ref.at[pl.ds(core * half, half)], centre_buf, centre_sem
    )
    centre_copy.start()

    def own_copy(j):
        return pltpu.make_async_copy(
            stay_ref.at[core * half + j], stay_buf.at[j, 0], stay_recv.at[j, 0]
        )

    for j in range(half):
        own_copy(j).start()

    moving = plan.moving
    small[0].wait()
    small[1].wait()
    line = lax.broadcasted_iota(jnp.int32, count_buf.shape[1:], 0)
    live = jnp.zeros(count_buf.shape[1:], jnp.int32)
    for i in range(plan.lists):
        live = jnp.where(line == i, count_ref[i], live)
    count_buf[0] = live
    names = jnp.broadcast_to(list_ref[...], (moving, moving))
    row = lax.broadcasted_iota(jnp.int32, (moving, moving), 0)
    column = lax.broadcasted_iota(jnp.int32, (moving, moving), 1)
    down = jnp.sum(jnp.where(row == column, names, 0), axis=1, keepdims=True)
    earlier = jnp.where((names == down) & (row < column), 1, 0)
    slot = jnp.sum(earlier, axis=0, keepdims=True)
    target = list_ref[...]
    position = (
        (target // half) * plan.block + group * plan.per_source + (target % half) * SLOT_L + slot
    )
    pos_own[...] = jnp.full(pos_own.shape, -1, jnp.int32)
    pos_own[:, :moving] = jnp.broadcast_to(position, (8, moving))

    pl.semaphore_wait(barrier, len(peers) + len(plane))

    def moving_copy(k):
        return pltpu.make_async_remote_copy(
            src_ref=moving_ref, dst_ref=moving_buf.at[k - 1],
            send_sem=moving_send.at[k - 1], recv_sem=moving_recv.at[k - 1],
            device_id=(owner, rep_at(k, 0)), device_id_type=MESH,
        )

    def pos_copy(k):
        return pltpu.make_async_remote_copy(
            src_ref=pos_own, dst_ref=pos_buf.at[k - 1],
            send_sem=pos_send.at[k - 1], recv_sem=pos_recv.at[k - 1],
            device_id=(owner, rep_at(k, 0)), device_id_type=MESH,
        )

    for k in range(1, groups):
        pos_copy(k).start()
        moving_copy(k).start()

    def count_copy(k, dc):
        q = k * split + dc
        return pltpu.make_async_remote_copy(
            src_ref=count_buf.at[0], dst_ref=count_buf.at[q],
            send_sem=count_send.at[q], recv_sem=count_recv.at[q],
            device_id=(owner, rep_at(k, dc)), device_id_type=MESH,
        )

    def stay_copy(j, k, dc):
        q = k * split + dc
        return pltpu.make_async_remote_copy(
            src_ref=stay_ref.at[lax.rem(core + dc, split) * half + j], dst_ref=stay_buf.at[j, q],
            send_sem=stay_send.at[j, q], recv_sem=stay_recv.at[j, q],
            device_id=(owner, rep_at(k, dc)), device_id_type=MESH,
        )

    for k, dc in peers:
        count_copy(k, dc).start()
    ahead = min(2, half)
    small[2].wait()
    small[3].wait()

    total = plan.blocks * plan.block
    slot_row = lax.broadcasted_iota(jnp.int32, (total, moving), 0)

    def one_hot(positions):
        return jnp.where(slot_row == positions, 1.0, 0.0).astype(jnp.bfloat16)

    pick = one_hot(pos_own[0:1, :moving])
    ones = jnp.ones((moving, LANES), jnp.bfloat16)
    rows = jnp.dot(pick, moving_own[...], preferred_element_type=jnp.float32)
    flags = jnp.dot(pick, ones, preferred_element_type=jnp.float32)
    for k in range(1, groups):
        pos_copy(k).wait_send()
        moving_copy(k).wait_send()
    for j in range(ahead):
        for k, dc in peers:
            stay_copy(j, k, dc).start()
    for k in range(1, groups):
        pos_copy(k).wait_recv()
        moving_copy(k).wait_recv()
        pick = one_hot(pos_buf[k - 1, 0:1, :moving])
        rows += jnp.dot(pick, moving_buf[k - 1], preferred_element_type=jnp.float32)
        flags += jnp.dot(pick, ones, preferred_element_type=jnp.float32)
    placed[:, :, :features] = rows.astype(jnp.bfloat16).reshape(plan.blocks, plan.block, features)
    placed[:, :, features:] = flags.astype(jnp.bfloat16).reshape(plan.blocks, plan.block, LANES)

    def slot_copy(k, dc):
        b = k * split + dc
        return pltpu.make_async_remote_copy(
            src_ref=placed.at[owner_at(k) * split + lax.rem(core + dc, split)],
            dst_ref=arrived.at[b],
            send_sem=slot_send.at[b], recv_sem=slot_recv.at[b],
            device_id=(owner_at(k), rep_at(0, dc)), device_id_type=MESH,
        )

    sent = [(k, dc) for k in range(owners) for dc in range(split) if (k, dc) != (0, 0)]
    for k, dc in sent:
        slot_copy(k, dc).start()
    arrived[0] = placed[owner * split + core]
    centre_copy.wait()
    for k, dc in peers:
        count_copy(k, dc).wait_recv()

    arrived_lane = lax.broadcasted_iota(jnp.int32, (1, total), 1)
    arrived_list = (arrived_lane % plan.per_source) // SLOT_L

    def result_copy(j, dc):
        return pltpu.make_async_remote_copy(
            src_ref=result_buf.at[j], dst_ref=out_ref.at[core * half + j],
            send_sem=result_send.at[j, dc], recv_sem=result_recv.at[j, dc],
            device_id=(owner, rep_at(0, dc)), device_id_type=MESH,
        )

    def result_own(j):
        return pltpu.make_async_copy(
            result_buf.at[j], out_ref.at[core * half + j], result_recv.at[j, 0]
        )

    def list_facts(j):
        centres = centre_buf[j]
        wide = centres.astype(jnp.float32)
        norm = jnp.sum(wide * wide, axis=1, keepdims=True)
        return centres, norm, sharp_ref[core * half + j]

    def add_part(j, rows, mask):
        num, mass, mass_row = weigh_rows(plan, *list_facts(j), rows, mask)
        total_buf[j] += num
        mass_col[j] += jnp.broadcast_to(mass, mass_col.shape[1:])
        mass_buf[j] += mass_row

    def add_stay(j, first, last):
        lane = lax.broadcasted_iota(jnp.int32, (1, (last - first) * capacity), 1)
        counts = jnp.zeros(lane.shape, jnp.int32)
        for q in range(first, last):
            counts = jnp.where(
                lane // capacity == q - first,
                count_buf[q, pl.ds(core * half + j, 1), :][:, : lane.shape[1]], counts,
            )
        mask = jnp.where(lane % capacity < counts, 1.0, 0.0)
        members = stay_buf[j, first:last].reshape((last - first) * capacity, features)
        add_part(j, members, mask)

    def add_arrivals(j):
        spread = jnp.full((8, LANES), 1.0 / LANES, jnp.bfloat16)
        marks = arrived[:, :, features:].reshape(total, LANES)
        present = lax.dot_general(
            spread, marks, (((1,), (1,)), ((), ())), preferred_element_type=jnp.float32
        )[0:1]
        here = jnp.where(arrived_list == j, present, 0.0)
        add_part(j, arrived[:, :, :features].reshape(total, features), here)

    def add_near(j):
        total_buf[j] = prior_weight * centre_buf[j].astype(jnp.float32)
        mass_col[j] = jnp.zeros(mass_col.shape[1:], jnp.float32)
        mass_buf[j] = jnp.zeros(mass_buf.shape[1:], jnp.float32)
        own_copy(j).wait()
        for k, dc in peers:
            if k == 0:
                stay_copy(j, k, dc).wait_recv()
        add_stay(j, 0, split)

    def pass_on(j):
        for k, dc in peers:
            stay_copy(j, k, dc).wait_send()

        @pl.when(j + ahead < half)
        def _():
            for k, dc in peers:
                stay_copy(j + ahead, k, dc).start()

    def add_far(j):
        for k, dc in peers:
            if k > 0:
                stay_copy(j, k, dc).wait_recv()
        if groups > 1:
            add_stay(j, split, replicas)

    def finish(j):
        share = 1.0 / (mass_col[j][:, 0:1] + prior_weight)
        result_buf[j] = (total_buf[j] * share).astype(jnp.bfloat16)
        result_own(j).start()
        for dc in range(1, split):
            result_copy(j, dc).start()

    def early(j, carry):
        add_near(j)
        pass_on(j)
        add_far(j)
        return carry

    def settle(j, carry):
        add_arrivals(j)
        finish(j)
        return carry

    def late(j, carry):
        add_near(j)
        add_arrivals(j)
        pass_on(j)
        add_far(j)
        finish(j)
        return carry

    cut = half - ahead
    lax.fori_loop(0, cut, early, 0)
    for k, dc in sent:
        slot_copy(k, dc).wait_recv()
    lax.fori_loop(0, cut, settle, 0)
    lax.fori_loop(cut, half, late, 0)

    def mass_copy(dc):
        return pltpu.make_async_remote_copy(
            src_ref=mass_buf, dst_ref=mass_ref.at[core],
            send_sem=mass_send.at[dc], recv_sem=mass_recv.at[dc],
            device_id=(owner, rep_at(0, dc)), device_id_type=MESH,
        )

    mass_own = pltpu.make_async_copy(mass_buf, mass_ref.at[core], local_sem)
    mass_own.start()
    for dc in range(1, split):
        mass_copy(dc).start()

    for k, dc in peers:
        count_copy(k, dc).wait_send()
    for k, dc in sent:
        slot_copy(k, dc).wait_send()
    for j in range(half):
        result_own(j).wait()
        for dc in range(1, split):
            result_copy(j, dc).wait()
    mass_own.wait()
    for dc in range(1, split):
        mass_copy(dc).wait()


def fused(plan, stay_rows, stay_count, moving_rows, new_list, centroids, sharpness):
    half, split, replicas = plan.half, plan.split, plan.replicas
    any_space = pl.BlockSpec(memory_space=pl.ANY)
    dma = pltpu.SemaphoreType.DMA
    members = replicas * plan.capacity
    refreshed, mass = pl.pallas_call(
        lambda *refs: fused_kernel(plan, *refs),
        out_shape=(
            jax.ShapeDtypeStruct(centroids.shape, jnp.bfloat16),
            jax.ShapeDtypeStruct((split, half, 8, plan.fine), jnp.float32),
        ),
        in_specs=[pl.BlockSpec(memory_space=pltpu.HBM)] * 6,
        out_specs=(any_space, any_space),
        scratch_shapes=[
            pltpu.SMEM((plan.lists,), jnp.int32),
            pltpu.VMEM((plan.moving, plan.features), jnp.bfloat16),
            pltpu.VMEM((1, plan.moving), jnp.int32),
            pltpu.SMEM((plan.lists,), jnp.float32),
            dma((4,)),
            pltpu.VMEM((half, plan.fine, plan.features), jnp.float32),
            pltpu.VMEM((half, plan.fine, LANES), jnp.float32),
            pltpu.VMEM((half, replicas, plan.capacity, plan.features), jnp.bfloat16),
            pltpu.VMEM((replicas, plan.lists, members), jnp.int32),
            pltpu.VMEM((max(1, plan.groups - 1), plan.moving, plan.features), jnp.bfloat16),
            pltpu.VMEM((8, plan.moving_lanes), jnp.int32),
            pltpu.VMEM((max(1, plan.groups - 1), 8, plan.moving_lanes), jnp.int32),
            pltpu.VMEM((plan.blocks, plan.block, plan.width), jnp.bfloat16),
            pltpu.VMEM((plan.blocks, plan.block, plan.width), jnp.bfloat16),
            pltpu.VMEM((half, plan.fine, plan.features), jnp.bfloat16),
            pltpu.VMEM((half, plan.fine, plan.features), jnp.bfloat16),
            pltpu.VMEM((half, 8, plan.fine), jnp.float32),
            dma((half, replicas)), dma((half, replicas)),
            dma((replicas,)), dma((replicas,)),
            dma((plan.groups,)), dma((plan.groups,)),
            dma((plan.groups,)), dma((plan.groups,)),
            dma((plan.blocks,)), dma((plan.blocks,)),
            dma,
            dma((half, split)), dma((half, split)),
            dma((split,)), dma((split,)),
            dma,
        ],
        compiler_params=pltpu.CompilerParams(
            collective_id=0, has_side_effects=True, vmem_limit_bytes=58500 * 2**10
        ),
    )(stay_rows, stay_count.reshape(-1), moving_rows, new_list.reshape(1, -1), centroids, sharpness)
    fine_share = plan.fine // replicas
    whole = mass[:, :, 0, :].reshape(plan.lists, plan.fine)
    share = lax.dynamic_slice_in_dim(whole, lax.axis_index("rep") * fine_share, fine_share, 1)
    return refreshed, share


def device_program(stay_rows, stay_count, moving_rows, new_list, centroids, sharpness):
    lists_here, capacity, features = stay_rows.shape
    plan = Plan(
        lax.axis_size("owner"), lax.axis_size("rep"), lists_here, capacity, features,
        centroids.shape[1], moving_rows.shape[0],
    )
    step = (lambda *a: fused(plan, *a)) if plan.fits() else local
    return step(stay_rows, stay_count, moving_rows, new_list, centroids, sharpness)


def solution(mesh):
    in_specs = (
        P("owner", "rep", None),
        P("owner", "rep"),
        P(("owner", "rep"), None),
        P(("owner", "rep")),
        P("owner", None, None),
        P("owner"),
    )
    out_specs = (P("owner", None, None), P("owner", "rep"))
    return jax.shard_map(device_program, mesh=mesh, in_specs=in_specs, out_specs=out_specs, check_vma=False)
```

```python
import math

import jax
import jax.numpy as jnp
from jax import lax
from jax.experimental import pallas as pl
from jax.experimental.pallas import tpu as pltpu
from jax.sharding import PartitionSpec as P

SLOT_L = 2


prior_weight = 1.0


def partner(value, axis, stride):
    mask = 2**stride
    pairs = [(source, source ^ mask) for source in range(lax.axis_size(axis))]
    return lax.ppermute(value, axis, pairs)


def weigh(members, live_mask, centres, centre_norm, sharp, features):
    products = jnp.einsum("lrd,lfd->lrf", members, centres, preferred_element_type=jnp.float32)
    scores = sharp[:, None, None] * (2.0 * products - centre_norm[:, None, :]) / math.sqrt(features)
    weights = jax.nn.softmax(scores, axis=-1).astype(jnp.bfloat16) * live_mask[:, :, None]
    numerator = jnp.einsum("lrf,lrd->lfd", weights, members, preferred_element_type=jnp.float32)
    return (numerator, jnp.sum(weights.astype(jnp.float32), axis=1))


def local(stay_rows, stay_count, moving_rows, new_list, centroids, sharpness):
    owners = lax.axis_size("owner")
    replicas = lax.axis_size("rep")
    lists_here, capacity, features = stay_rows.shape
    fine_count = centroids.shape[1]
    centre_norm = jnp.sum(jnp.square(centroids.astype(jnp.float32)), axis=-1)
    outgoing_count = new_list.shape[0]
    order_index = jnp.arange(outgoing_count)
    earlier = (new_list[None, :] == new_list[:, None]) & (
        order_index[None, :] < order_index[:, None]
    )
    slot_index = jnp.sum(earlier.astype(jnp.int32), axis=1)
    local_list = new_list % lists_here
    target_owner = new_list // lists_here
    position = (local_list * owners + target_owner) * SLOT_L + slot_index
    slot_total = lists_here * owners * SLOT_L
    outgoing = (
        jnp.zeros((slot_total, features), jnp.bfloat16)
        .at[position]
        .set(moving_rows, unique_indices=True)
    )
    occupied = (
        jnp.zeros((slot_total,), jnp.bfloat16)
        .at[position]
        .set(jnp.ones((outgoing_count,), jnp.bfloat16), unique_indices=True)
    )
    arrived, present = (
        lax.all_to_all(
            outgoing.reshape(lists_here, owners, SLOT_L, features),
            "owner",
            split_axis=1,
            concat_axis=1,
            tiled=True,
        ),
        lax.all_to_all(
            occupied.reshape(lists_here, owners, SLOT_L),
            "owner",
            split_axis=1,
            concat_axis=1,
            tiled=True,
        ),
    )
    arrive_slots = owners * SLOT_L
    arrivals = arrived.reshape(lists_here, arrive_slots, features)
    present = present.reshape(lists_here, arrive_slots)
    live_count = stay_count[:, 0]
    replica = lax.axis_index("rep")
    fine_share = fine_count // replicas
    groups = max(1, replicas // lists_here)
    per_rep = max(1, lists_here // replicas)
    slot_mask = (jnp.arange(capacity)[None, :] < live_count[:, None]).astype(jnp.bfloat16)
    stay_pieces = stay_rows.reshape(lists_here * groups, capacity // groups, features)
    mask_pieces = slot_mask.reshape(lists_here * groups, capacity // groups)
    moved_stay, moved_mask = (
        lax.all_to_all(stay_pieces, "rep", split_axis=0, concat_axis=1, tiled=True),
        lax.all_to_all(mask_pieces, "rep", split_axis=0, concat_axis=1, tiled=True),
    )
    arrive_pieces = arrivals.reshape(lists_here * groups, arrive_slots // groups, features)
    present_pieces = present.reshape(lists_here * groups, arrive_slots // groups)
    moved_arrive, moved_present = (
        lax.all_to_all(arrive_pieces, "rep", split_axis=0, concat_axis=1, tiled=True),
        lax.all_to_all(present_pieces, "rep", split_axis=0, concat_axis=1, tiled=True),
    )
    members = jnp.concatenate([moved_stay, moved_arrive], axis=1)
    member_mask = jnp.concatenate([moved_mask, moved_present], axis=1)
    first_list = replica * per_rep // groups
    centres = lax.dynamic_slice_in_dim(centroids, first_list, per_rep, 0)
    norms = lax.dynamic_slice_in_dim(centre_norm, first_list, per_rep, 0)
    sharp = lax.dynamic_slice_in_dim(sharpness, first_list, per_rep, 0)
    numerator, mass_sum = weigh(members, member_mask, centres, norms, sharp, features)
    for bit_number in range(groups.bit_length() - 1):
        other_num, other_mass = partner((numerator, mass_sum), "rep", bit_number)
        numerator = numerator + other_num
        mass_sum = mass_sum + other_mass
    refreshed_all = (
        (numerator + prior_weight * centres.astype(jnp.float32))
        / (mass_sum[:, :, None] + prior_weight)
    ).astype(jnp.bfloat16)
    piece_rows = fine_count // groups
    part_index = replica % groups
    refreshed_piece = lax.dynamic_slice_in_dim(
        refreshed_all, part_index * piece_rows, piece_rows, 1
    ).reshape(per_rep * piece_rows, features)
    mass_piece = lax.dynamic_slice_in_dim(mass_sum, part_index * piece_rows, piece_rows, 1).reshape(
        per_rep * piece_rows
    )
    refreshed = lax.all_gather(refreshed_piece, "rep", axis=0, tiled=True).reshape(
        lists_here, fine_count, features
    )
    mass_whole = lax.all_gather(mass_piece, "rep", axis=0, tiled=True).reshape(
        lists_here, fine_count
    )
    return (refreshed, lax.dynamic_slice_in_dim(mass_whole, replica * fine_share, fine_share, 1))


LANES = 128
VMEM_BUDGET = 40 * 2**20
VMEM_GRANT = 60000 * 2**10
MESH = pl.DeviceIdType.MESH


class Plan:
    def __init__(self, owners, replicas, lists, capacity, features, fine, moving):
        self.owners, self.replicas, self.lists = owners, replicas, lists
        self.capacity, self.features, self.fine, self.moving = capacity, features, fine, moving
        self.split = 2 if replicas % 2 == 0 and lists % 2 == 0 else 1
        self.groups = replicas // self.split
        self.half = lists // self.split
        self.per_source = self.half * SLOT_L
        self.block = self.groups * self.per_source
        self.blocks = owners * self.split
        self.width = features + LANES
        self.moving_lanes = -(-moving // LANES) * LANES

    def fits(self):
        slots = 2 * self.blocks * self.block * self.width
        held = self.half * self.replicas * self.capacity * self.features
        centres = 2 * self.half * self.fine * self.features
        gathered = self.groups * self.moving * self.features
        small = 2 * (slots + held + centres + gathered)
        return (
            small <= VMEM_BUDGET
            and self.block % 16 == 0
            and self.capacity % 16 == 0
            and self.moving % 16 == 0
            and self.features % LANES == 0
            and self.fine % LANES == 0
        )


def weigh_rows(plan, centres, norm, sharp, rows, mask):
    products = lax.dot_general(
        centres, rows, (((1,), (1,)), ((), ())), preferred_element_type=jnp.float32
    )
    scores = sharp * (2.0 * products - norm) / math.sqrt(plan.features)
    top = jnp.max(scores, axis=0, keepdims=True)
    raised = jnp.exp(scores - top)
    weights = (raised / jnp.sum(raised, axis=0, keepdims=True)).astype(jnp.bfloat16)
    weights = weights * mask.astype(jnp.bfloat16)
    numerator = jnp.dot(weights, rows, preferred_element_type=jnp.float32)
    mass = jnp.sum(weights.astype(jnp.float32), axis=1, keepdims=True)
    ones = jnp.ones((8, rows.shape[0]), jnp.bfloat16)
    mass_row = lax.dot_general(
        ones, weights, (((1,), (1,)), ((), ())), preferred_element_type=jnp.float32
    )
    return numerator, mass, mass_row


def fused_kernel(
    plan,
    stay_ref, count_in, moving_ref, list_in, centre_ref, sharp_in,
    out_ref, mass_ref,
    count_ref, moving_own, list_ref, sharp_ref, operand_sem, total_buf, mass_col,
    stay_buf, count_buf, moving_buf, pos_own, pos_buf, placed, arrived, centre_buf, result_buf, mass_buf,
    stay_send, stay_recv, count_send, count_recv, moving_send, moving_recv, pos_send, pos_recv,
    slot_send, slot_recv, centre_sem, result_send, result_recv, mass_send, mass_recv, local_sem,
):
    owners, split, groups, half = plan.owners, plan.split, plan.groups, plan.half
    replicas, capacity, features = plan.replicas, plan.capacity, plan.features
    owner = lax.axis_index("owner")
    replica = lax.axis_index("rep")
    core = replica % split
    group = replica // split

    def rep_at(k, dc):
        return lax.rem(group + k, groups) * split + lax.rem(core + dc, split)

    def owner_at(k):
        return lax.rem(owner + k, owners)

    peers = [(k, dc) for k in range(groups) for dc in range(split) if (k, dc) != (0, 0)]
    plane = [(k, dc) for k in range(1, owners) for dc in range(split)]
    barrier = pltpu.get_barrier_semaphore()
    for k, dc in peers:
        pl.semaphore_signal(barrier, inc=1, device_id=(owner, rep_at(k, dc)), device_id_type=MESH)
    for k, dc in plane:
        pl.semaphore_signal(
            barrier, inc=1, device_id=(owner_at(k), rep_at(0, dc)), device_id_type=MESH
        )

    small = [
        pltpu.make_async_copy(source, held, operand_sem.at[i])
        for i, (source, held) in enumerate([
            (list_in, list_ref), (count_in, count_ref), (moving_ref, moving_own), (sharp_in, sharp_ref),
        ])
    ]
    for copy in small:
        copy.start()
    centre_copy = pltpu.make_async_copy(
        centre_ref.at[pl.ds(core * half, half)], centre_buf, centre_sem
    )
    centre_copy.start()

    def own_copy(j):
        return pltpu.make_async_copy(
            stay_ref.at[core * half + j], stay_buf.at[j, 0], stay_recv.at[j, 0]
        )

    for j in range(half):
        own_copy(j).start()

    moving = plan.moving
    small[0].wait()
    small[1].wait()
    line = lax.broadcasted_iota(jnp.int32, count_buf.shape[1:], 0)
    live = jnp.zeros(count_buf.shape[1:], jnp.int32)
    for i in range(plan.lists):
        live = jnp.where(line == i, count_ref[i], live)
    count_buf[0] = live
    names = jnp.broadcast_to(list_ref[...], (moving, moving))
    row = lax.broadcasted_iota(jnp.int32, (moving, moving), 0)
    column = lax.broadcasted_iota(jnp.int32, (moving, moving), 1)
    down = jnp.sum(jnp.where(row == column, names, 0), axis=1, keepdims=True)
    earlier = jnp.where((names == down) & (row < column), 1, 0)
    slot = jnp.sum(earlier, axis=0, keepdims=True)
    target = list_ref[...]
    position = (
        (target // half) * plan.block + group * plan.per_source + (target % half) * SLOT_L + slot
    )
    pos_own[...] = jnp.full(pos_own.shape, -1, jnp.int32)
    pos_own[:, :moving] = jnp.broadcast_to(position, (8, moving))

    pl.semaphore_wait(barrier, len(peers) + len(plane))

    def moving_copy(k):
        return pltpu.make_async_remote_copy(
            src_ref=moving_ref, dst_ref=moving_buf.at[k - 1],
            send_sem=moving_send.at[k - 1], recv_sem=moving_recv.at[k - 1],
            device_id=(owner, rep_at(k, 0)), device_id_type=MESH,
        )

    def pos_copy(k):
        return pltpu.make_async_remote_copy(
            src_ref=pos_own, dst_ref=pos_buf.at[k - 1],
            send_sem=pos_send.at[k - 1], recv_sem=pos_recv.at[k - 1],
            device_id=(owner, rep_at(k, 0)), device_id_type=MESH,
        )

    for k in range(1, groups):
        pos_copy(k).start()
        moving_copy(k).start()

    def count_copy(k, dc):
        q = k * split + dc
        return pltpu.make_async_remote_copy(
            src_ref=count_buf.at[0], dst_ref=count_buf.at[q],
            send_sem=count_send.at[q], recv_sem=count_recv.at[q],
            device_id=(owner, rep_at(k, dc)), device_id_type=MESH,
        )

    def stay_copy(j, k, dc):
        q = k * split + dc
        return pltpu.make_async_remote_copy(
            src_ref=stay_ref.at[lax.rem(core + dc, split) * half + j], dst_ref=stay_buf.at[j, q],
            send_sem=stay_send.at[j, q], recv_sem=stay_recv.at[j, q],
            device_id=(owner, rep_at(k, dc)), device_id_type=MESH,
        )

    for k, dc in peers:
        count_copy(k, dc).start()
    siblings = [(k, dc) for k, dc in peers if k == 0]
    distant = [(k, dc) for k, dc in peers if k > 0]
    for j in range(half):
        for k, dc in siblings:
            stay_copy(j, k, dc).start()
    small[2].wait()
    small[3].wait()

    total = plan.blocks * plan.block
    slot_row = lax.broadcasted_iota(jnp.int32, (total, moving), 0)

    def one_hot(positions):
        return jnp.where(slot_row == positions, 1.0, 0.0).astype(jnp.bfloat16)

    pick = one_hot(pos_own[0:1, :moving])
    ones = jnp.ones((moving, LANES), jnp.bfloat16)
    rows = jnp.dot(pick, moving_own[...], preferred_element_type=jnp.float32)
    flags = jnp.dot(pick, ones, preferred_element_type=jnp.float32)
    for k in range(1, groups):
        pos_copy(k).wait_send()
        moving_copy(k).wait_send()
    for k, dc in distant:
        stay_copy(0, k, dc).start()
    for k in range(1, groups):
        pos_copy(k).wait_recv()
        moving_copy(k).wait_recv()
        pick = one_hot(pos_buf[k - 1, 0:1, :moving])
        rows += jnp.dot(pick, moving_buf[k - 1], preferred_element_type=jnp.float32)
        flags += jnp.dot(pick, ones, preferred_element_type=jnp.float32)
    placed[:, :, :features] = rows.astype(jnp.bfloat16).reshape(plan.blocks, plan.block, features)
    placed[:, :, features:] = flags.astype(jnp.bfloat16).reshape(plan.blocks, plan.block, LANES)

    def slot_copy(k, dc):
        b = k * split + dc
        return pltpu.make_async_remote_copy(
            src_ref=placed.at[owner_at(k) * split + lax.rem(core + dc, split)],
            dst_ref=arrived.at[b],
            send_sem=slot_send.at[b], recv_sem=slot_recv.at[b],
            device_id=(owner_at(k), rep_at(0, dc)), device_id_type=MESH,
        )

    sent = [(k, dc) for k in range(owners) for dc in range(split) if (k, dc) != (0, 0)]
    for k, dc in sent:
        slot_copy(k, dc).start()
    arrived[0] = placed[owner * split + core]
    centre_copy.wait()
    for k, dc in peers:
        count_copy(k, dc).wait_recv()

    arrived_lane = lax.broadcasted_iota(jnp.int32, (1, total), 1)
    arrived_list = (arrived_lane % plan.per_source) // SLOT_L

    def result_copy(j, dc):
        return pltpu.make_async_remote_copy(
            src_ref=result_buf.at[j], dst_ref=out_ref.at[core * half + j],
            send_sem=result_send.at[j, dc], recv_sem=result_recv.at[j, dc],
            device_id=(owner, rep_at(0, dc)), device_id_type=MESH,
        )

    def result_own(j):
        return pltpu.make_async_copy(
            result_buf.at[j], out_ref.at[core * half + j], result_recv.at[j, 0]
        )

    def list_facts(j):
        centres = centre_buf[j]
        wide = centres.astype(jnp.float32)
        norm = jnp.sum(wide * wide, axis=1, keepdims=True)
        return centres, norm, sharp_ref[core * half + j]

    def add_part(j, rows, mask):
        num, mass, mass_row = weigh_rows(plan, *list_facts(j), rows, mask)
        total_buf[j] += num
        mass_col[j] += jnp.broadcast_to(mass, mass_col.shape[1:])
        mass_buf[j] += mass_row

    def add_stay(j, first, last):
        lane = lax.broadcasted_iota(jnp.int32, (1, (last - first) * capacity), 1)
        counts = jnp.zeros(lane.shape, jnp.int32)
        for q in range(first, last):
            counts = jnp.where(
                lane // capacity == q - first,
                count_buf[q, pl.ds(core * half + j, 1), :][:, : lane.shape[1]], counts,
            )
        mask = jnp.where(lane % capacity < counts, 1.0, 0.0)
        members = stay_buf[j, first:last].reshape((last - first) * capacity, features)
        add_part(j, members, mask)

    def add_arrivals(j):
        spread = jnp.full((8, LANES), 1.0 / LANES, jnp.bfloat16)
        marks = arrived[:, :, features:].reshape(total, LANES)
        present = lax.dot_general(
            spread, marks, (((1,), (1,)), ((), ())), preferred_element_type=jnp.float32
        )[0:1]
        here = jnp.where(arrived_list == j, present, 0.0)
        add_part(j, arrived[:, :, :features].reshape(total, features), here)

    def add_near(j):
        total_buf[j] = prior_weight * centre_buf[j].astype(jnp.float32)
        mass_col[j] = jnp.zeros(mass_col.shape[1:], jnp.float32)
        mass_buf[j] = jnp.zeros(mass_buf.shape[1:], jnp.float32)
        own_copy(j).wait()
        for k, dc in siblings:
            stay_copy(j, k, dc).wait_recv()
        add_stay(j, 0, split)

    def pass_on(j):
        for k, dc in distant:
            stay_copy(j, k, dc).wait_send()
            stay_copy(j + 1, k, dc).start()

    def add_far(j):
        for k, dc in distant:
            stay_copy(j, k, dc).wait_recv()
        if groups > 1:
            add_stay(j, split, replicas)

    def finish(j):
        share = 1.0 / (mass_col[j][:, 0:1] + prior_weight)
        result_buf[j] = (total_buf[j] * share).astype(jnp.bfloat16)
        result_own(j).start()
        for dc in range(1, split):
            result_copy(j, dc).start()

    def early(j, carry):
        add_near(j)
        pass_on(j)
        add_far(j)
        return carry

    def settle(j, carry):
        add_arrivals(j)
        finish(j)
        return carry

    last = half - 1
    lax.fori_loop(0, last, early, 0)
    add_near(last)
    for k, dc in sent:
        slot_copy(k, dc).wait_recv()
    lax.fori_loop(0, last, settle, 0)
    add_arrivals(last)
    add_far(last)
    finish(last)

    def mass_copy(dc):
        return pltpu.make_async_remote_copy(
            src_ref=mass_buf, dst_ref=mass_ref.at[core],
            send_sem=mass_send.at[dc], recv_sem=mass_recv.at[dc],
            device_id=(owner, rep_at(0, dc)), device_id_type=MESH,
        )

    mass_own = pltpu.make_async_copy(mass_buf, mass_ref.at[core], local_sem)
    mass_own.start()
    for dc in range(1, split):
        mass_copy(dc).start()

    for k, dc in peers:
        count_copy(k, dc).wait_send()
    for k, dc in distant:
        stay_copy(last, k, dc).wait_send()
    for j in range(half):
        for k, dc in siblings:
            stay_copy(j, k, dc).wait_send()
    for k, dc in sent:
        slot_copy(k, dc).wait_send()
    for j in range(half):
        result_own(j).wait()
        for dc in range(1, split):
            result_copy(j, dc).wait()
    mass_own.wait()
    for dc in range(1, split):
        mass_copy(dc).wait()


def deliver_kernel(plan, made_ref, mass_ref, out_ref, share_ref, sems):
    copies = [
        pltpu.make_async_copy(made_ref.at[i], out_ref.at[i], sems.at[i]) for i in range(plan.lists)
    ]
    for copy in copies:
        copy.start()
    replica = lax.axis_index("rep")
    width = plan.fine // plan.replicas
    rows = [mass_ref[s, j, 0:1, :] for s in range(plan.split) for j in range(plan.half)]
    whole = jnp.concatenate(rows, axis=0)
    share = whole[:, :width]
    for r in range(1, plan.replicas):
        share = jnp.where(replica == r, whole[:, r * width : (r + 1) * width], share)
    share_ref[...] = share
    for copy in copies:
        copy.wait()


def fused(plan, stay_rows, stay_count, moving_rows, new_list, centroids, sharpness):
    half, split, replicas = plan.half, plan.split, plan.replicas
    any_space = pl.BlockSpec(memory_space=pl.ANY)
    dma = pltpu.SemaphoreType.DMA
    members = replicas * plan.capacity
    refreshed, mass = pl.pallas_call(
        lambda *refs: fused_kernel(plan, *refs),
        out_shape=(
            jax.ShapeDtypeStruct(centroids.shape, jnp.bfloat16),
            jax.ShapeDtypeStruct((split, half, 8, plan.fine), jnp.float32),
        ),
        in_specs=[pl.BlockSpec(memory_space=pltpu.HBM)] * 6,
        out_specs=(any_space, any_space),
        scratch_shapes=[
            pltpu.SMEM((plan.lists,), jnp.int32),
            pltpu.VMEM((plan.moving, plan.features), jnp.bfloat16),
            pltpu.VMEM((1, plan.moving), jnp.int32),
            pltpu.SMEM((plan.lists,), jnp.float32),
            dma((4,)),
            pltpu.VMEM((half, plan.fine, plan.features), jnp.float32),
            pltpu.VMEM((half, plan.fine, LANES), jnp.float32),
            pltpu.VMEM((half, replicas, plan.capacity, plan.features), jnp.bfloat16),
            pltpu.VMEM((replicas, plan.lists, members), jnp.int32),
            pltpu.VMEM((max(1, plan.groups - 1), plan.moving, plan.features), jnp.bfloat16),
            pltpu.VMEM((8, plan.moving_lanes), jnp.int32),
            pltpu.VMEM((max(1, plan.groups - 1), 8, plan.moving_lanes), jnp.int32),
            pltpu.VMEM((plan.blocks, plan.block, plan.width), jnp.bfloat16),
            pltpu.VMEM((plan.blocks, plan.block, plan.width), jnp.bfloat16),
            pltpu.VMEM((half, plan.fine, plan.features), jnp.bfloat16),
            pltpu.VMEM((half, plan.fine, plan.features), jnp.bfloat16),
            pltpu.VMEM((half, 8, plan.fine), jnp.float32),
            dma((half, replicas)), dma((half, replicas)),
            dma((replicas,)), dma((replicas,)),
            dma((plan.groups,)), dma((plan.groups,)),
            dma((plan.groups,)), dma((plan.groups,)),
            dma((plan.blocks,)), dma((plan.blocks,)),
            dma,
            dma((half, split)), dma((half, split)),
            dma((split,)), dma((split,)),
            dma,
        ],
        compiler_params=pltpu.CompilerParams(
            collective_id=0, has_side_effects=True, vmem_limit_bytes=VMEM_GRANT
        ),
    )(stay_rows, stay_count.reshape(-1), moving_rows, new_list.reshape(1, -1), centroids, sharpness)
    return pl.pallas_call(
        lambda *refs: deliver_kernel(plan, *refs),
        out_shape=(
            jax.ShapeDtypeStruct(centroids.shape, jnp.bfloat16),
            jax.ShapeDtypeStruct((plan.lists, plan.fine // replicas), jnp.float32),
        ),
        in_specs=[any_space, pl.BlockSpec(memory_space=pltpu.VMEM)],
        out_specs=(any_space, pl.BlockSpec(memory_space=pltpu.VMEM)),
        scratch_shapes=[dma((plan.lists,))],
        compiler_params=pltpu.CompilerParams(vmem_limit_bytes=VMEM_GRANT),
    )(refreshed, mass)


def device_program(stay_rows, stay_count, moving_rows, new_list, centroids, sharpness):
    lists_here, capacity, features = stay_rows.shape
    plan = Plan(
        lax.axis_size("owner"), lax.axis_size("rep"), lists_here, capacity, features,
        centroids.shape[1], moving_rows.shape[0],
    )
    step = (lambda *a: fused(plan, *a)) if plan.fits() else local
    return step(stay_rows, stay_count, moving_rows, new_list, centroids, sharpness)


def solution(mesh):
    in_specs = (
        P("owner", "rep", None),
        P("owner", "rep"),
        P(("owner", "rep"), None),
        P(("owner", "rep")),
        P("owner", None, None),
        P("owner"),
    )
    out_specs = (P("owner", None, None), P("owner", "rep"))
    return jax.shard_map(device_program, mesh=mesh, in_specs=in_specs, out_specs=out_specs, check_vma=False)
```

```python
import math

import jax
import jax.numpy as jnp
from jax import lax
from jax.experimental import pallas as pl
from jax.experimental.pallas import tpu as pltpu
from jax.sharding import PartitionSpec as P

SLOT_L = 2


prior_weight = 1.0


def partner(value, axis, stride):
    mask = 2**stride
    pairs = [(source, source ^ mask) for source in range(lax.axis_size(axis))]
    return lax.ppermute(value, axis, pairs)


def weigh(members, live_mask, centres, centre_norm, sharp, features):
    products = jnp.einsum("lrd,lfd->lrf", members, centres, preferred_element_type=jnp.float32)
    scores = sharp[:, None, None] * (2.0 * products - centre_norm[:, None, :]) / math.sqrt(features)
    weights = jax.nn.softmax(scores, axis=-1).astype(jnp.bfloat16) * live_mask[:, :, None]
    numerator = jnp.einsum("lrf,lrd->lfd", weights, members, preferred_element_type=jnp.float32)
    return (numerator, jnp.sum(weights.astype(jnp.float32), axis=1))


def local(stay_rows, stay_count, moving_rows, new_list, centroids, sharpness):
    owners = lax.axis_size("owner")
    replicas = lax.axis_size("rep")
    lists_here, capacity, features = stay_rows.shape
    fine_count = centroids.shape[1]
    centre_norm = jnp.sum(jnp.square(centroids.astype(jnp.float32)), axis=-1)
    outgoing_count = new_list.shape[0]
    order_index = jnp.arange(outgoing_count)
    earlier = (new_list[None, :] == new_list[:, None]) & (
        order_index[None, :] < order_index[:, None]
    )
    slot_index = jnp.sum(earlier.astype(jnp.int32), axis=1)
    local_list = new_list % lists_here
    target_owner = new_list // lists_here
    position = (local_list * owners + target_owner) * SLOT_L + slot_index
    slot_total = lists_here * owners * SLOT_L
    outgoing = (
        jnp.zeros((slot_total, features), jnp.bfloat16)
        .at[position]
        .set(moving_rows, unique_indices=True)
    )
    occupied = (
        jnp.zeros((slot_total,), jnp.bfloat16)
        .at[position]
        .set(jnp.ones((outgoing_count,), jnp.bfloat16), unique_indices=True)
    )
    arrived, present = (
        lax.all_to_all(
            outgoing.reshape(lists_here, owners, SLOT_L, features),
            "owner",
            split_axis=1,
            concat_axis=1,
            tiled=True,
        ),
        lax.all_to_all(
            occupied.reshape(lists_here, owners, SLOT_L),
            "owner",
            split_axis=1,
            concat_axis=1,
            tiled=True,
        ),
    )
    arrive_slots = owners * SLOT_L
    arrivals = arrived.reshape(lists_here, arrive_slots, features)
    present = present.reshape(lists_here, arrive_slots)
    live_count = stay_count[:, 0]
    replica = lax.axis_index("rep")
    fine_share = fine_count // replicas
    groups = max(1, replicas // lists_here)
    per_rep = max(1, lists_here // replicas)
    slot_mask = (jnp.arange(capacity)[None, :] < live_count[:, None]).astype(jnp.bfloat16)
    stay_pieces = stay_rows.reshape(lists_here * groups, capacity // groups, features)
    mask_pieces = slot_mask.reshape(lists_here * groups, capacity // groups)
    moved_stay, moved_mask = (
        lax.all_to_all(stay_pieces, "rep", split_axis=0, concat_axis=1, tiled=True),
        lax.all_to_all(mask_pieces, "rep", split_axis=0, concat_axis=1, tiled=True),
    )
    arrive_pieces = arrivals.reshape(lists_here * groups, arrive_slots // groups, features)
    present_pieces = present.reshape(lists_here * groups, arrive_slots // groups)
    moved_arrive, moved_present = (
        lax.all_to_all(arrive_pieces, "rep", split_axis=0, concat_axis=1, tiled=True),
        lax.all_to_all(present_pieces, "rep", split_axis=0, concat_axis=1, tiled=True),
    )
    members = jnp.concatenate([moved_stay, moved_arrive], axis=1)
    member_mask = jnp.concatenate([moved_mask, moved_present], axis=1)
    first_list = replica * per_rep // groups
    centres = lax.dynamic_slice_in_dim(centroids, first_list, per_rep, 0)
    norms = lax.dynamic_slice_in_dim(centre_norm, first_list, per_rep, 0)
    sharp = lax.dynamic_slice_in_dim(sharpness, first_list, per_rep, 0)
    numerator, mass_sum = weigh(members, member_mask, centres, norms, sharp, features)
    for bit_number in range(groups.bit_length() - 1):
        other_num, other_mass = partner((numerator, mass_sum), "rep", bit_number)
        numerator = numerator + other_num
        mass_sum = mass_sum + other_mass
    refreshed_all = (
        (numerator + prior_weight * centres.astype(jnp.float32))
        / (mass_sum[:, :, None] + prior_weight)
    ).astype(jnp.bfloat16)
    piece_rows = fine_count // groups
    part_index = replica % groups
    refreshed_piece = lax.dynamic_slice_in_dim(
        refreshed_all, part_index * piece_rows, piece_rows, 1
    ).reshape(per_rep * piece_rows, features)
    mass_piece = lax.dynamic_slice_in_dim(mass_sum, part_index * piece_rows, piece_rows, 1).reshape(
        per_rep * piece_rows
    )
    refreshed = lax.all_gather(refreshed_piece, "rep", axis=0, tiled=True).reshape(
        lists_here, fine_count, features
    )
    mass_whole = lax.all_gather(mass_piece, "rep", axis=0, tiled=True).reshape(
        lists_here, fine_count
    )
    return (refreshed, lax.dynamic_slice_in_dim(mass_whole, replica * fine_share, fine_share, 1))


LANES = 128
VMEM_BUDGET = 40 * 2**20
VMEM_GRANT = 60000 * 2**10
MESH = pl.DeviceIdType.MESH


class Plan:
    def __init__(self, owners, replicas, lists, capacity, features, fine, moving):
        self.owners, self.replicas, self.lists = owners, replicas, lists
        self.capacity, self.features, self.fine, self.moving = capacity, features, fine, moving
        self.split = 2 if replicas % 2 == 0 and lists % 2 == 0 else 1
        self.groups = replicas // self.split
        self.half = lists // self.split
        self.per_source = self.half * SLOT_L
        self.block = self.groups * self.per_source
        self.blocks = owners * self.split
        self.width = features + LANES
        self.moving_lanes = -(-moving // LANES) * LANES

    def fits(self):
        slots = 2 * self.blocks * self.block * self.width
        held = self.half * self.replicas * self.capacity * self.features
        centres = 2 * self.half * self.fine * self.features
        gathered = self.groups * self.moving * self.features
        small = 2 * (slots + held + centres + gathered)
        return (
            small <= VMEM_BUDGET
            and self.block % 16 == 0
            and self.capacity % 16 == 0
            and self.moving % 16 == 0
            and self.features % LANES == 0
            and self.fine % LANES == 0
        )


def weigh_rows(plan, centres, norm, sharp, rows, mask):
    products = lax.dot_general(
        centres, rows, (((1,), (1,)), ((), ())), preferred_element_type=jnp.float32
    )
    scores = sharp * (2.0 * products - norm) / math.sqrt(plan.features)
    top = jnp.max(scores, axis=0, keepdims=True)
    raised = jnp.exp(scores - top)
    weights = (raised / jnp.sum(raised, axis=0, keepdims=True)).astype(jnp.bfloat16)
    weights = weights * mask.astype(jnp.bfloat16)
    numerator = jnp.dot(weights, rows, preferred_element_type=jnp.float32)
    mass = jnp.sum(weights.astype(jnp.float32), axis=1, keepdims=True)
    ones = jnp.ones((8, rows.shape[0]), jnp.bfloat16)
    mass_row = lax.dot_general(
        ones, weights, (((1,), (1,)), ((), ())), preferred_element_type=jnp.float32
    )
    return numerator, mass, mass_row


def fused_kernel(
    plan,
    stay_ref, count_in, moving_ref, list_in, centre_ref, sharp_in,
    out_ref, mass_ref,
    count_ref, moving_own, list_ref, sharp_ref, operand_sem, total_buf, mass_col, norm_buf,
    stay_buf, count_buf, moving_buf, pos_own, pos_buf, placed, arrived, centre_buf, result_buf, mass_buf,
    stay_send, stay_recv, count_send, count_recv, moving_send, moving_recv, pos_send, pos_recv,
    slot_send, slot_recv, centre_sem, result_send, result_recv, mass_send, mass_recv, local_sem,
):
    owners, split, groups, half = plan.owners, plan.split, plan.groups, plan.half
    replicas, capacity, features = plan.replicas, plan.capacity, plan.features
    owner = lax.axis_index("owner")
    replica = lax.axis_index("rep")
    core = replica % split
    group = replica // split

    def rep_at(k, dc):
        return lax.rem(group + k, groups) * split + lax.rem(core + dc, split)

    def owner_at(k):
        return lax.rem(owner + k, owners)

    peers = [(k, dc) for k in range(groups) for dc in range(split) if (k, dc) != (0, 0)]
    plane = [(k, dc) for k in range(1, owners) for dc in range(split)]
    barrier = pltpu.get_barrier_semaphore()
    for k, dc in peers:
        pl.semaphore_signal(barrier, inc=1, device_id=(owner, rep_at(k, dc)), device_id_type=MESH)
    for k, dc in plane:
        pl.semaphore_signal(
            barrier, inc=1, device_id=(owner_at(k), rep_at(0, dc)), device_id_type=MESH
        )

    small = [
        pltpu.make_async_copy(source, held, operand_sem.at[i])
        for i, (source, held) in enumerate([
            (list_in, list_ref), (count_in, count_ref), (moving_ref, moving_own), (sharp_in, sharp_ref),
        ])
    ]
    for copy in small:
        copy.start()
    centre_copy = pltpu.make_async_copy(
        centre_ref.at[pl.ds(core * half, half)], centre_buf, centre_sem
    )
    centre_copy.start()

    def own_copy(j):
        return pltpu.make_async_copy(
            stay_ref.at[core * half + j], stay_buf.at[j, 0], stay_recv.at[j, 0]
        )

    for j in range(half):
        own_copy(j).start()

    pl.semaphore_wait(barrier, len(peers) + len(plane))

    def moving_copy(k):
        return pltpu.make_async_remote_copy(
            src_ref=moving_ref, dst_ref=moving_buf.at[k - 1],
            send_sem=moving_send.at[k - 1], recv_sem=moving_recv.at[k - 1],
            device_id=(owner, rep_at(k, 0)), device_id_type=MESH,
        )

    def pos_copy(k):
        return pltpu.make_async_remote_copy(
            src_ref=pos_own, dst_ref=pos_buf.at[k - 1],
            send_sem=pos_send.at[k - 1], recv_sem=pos_recv.at[k - 1],
            device_id=(owner, rep_at(k, 0)), device_id_type=MESH,
        )

    for k in range(1, groups):
        moving_copy(k).start()

    def count_copy(k, dc):
        q = k * split + dc
        return pltpu.make_async_remote_copy(
            src_ref=count_buf.at[0], dst_ref=count_buf.at[q],
            send_sem=count_send.at[q], recv_sem=count_recv.at[q],
            device_id=(owner, rep_at(k, dc)), device_id_type=MESH,
        )

    def stay_copy(j, k, dc):
        q = k * split + dc
        return pltpu.make_async_remote_copy(
            src_ref=stay_ref.at[lax.rem(core + dc, split) * half + j], dst_ref=stay_buf.at[j, q],
            send_sem=stay_send.at[j, q], recv_sem=stay_recv.at[j, q],
            device_id=(owner, rep_at(k, dc)), device_id_type=MESH,
        )

    siblings = [(k, dc) for k, dc in peers if k == 0]
    distant = [(k, dc) for k, dc in peers if k > 0]
    for j in range(half):
        for k, dc in siblings:
            stay_copy(j, k, dc).start()

    moving = plan.moving
    small[0].wait()
    small[1].wait()
    line = lax.broadcasted_iota(jnp.int32, count_buf.shape[1:], 0)
    live = jnp.zeros(count_buf.shape[1:], jnp.int32)
    for i in range(plan.lists):
        live = jnp.where(line == i, count_ref[i], live)
    count_buf[0] = live
    names = jnp.broadcast_to(list_ref[...], (moving, moving))
    row = lax.broadcasted_iota(jnp.int32, (moving, moving), 0)
    column = lax.broadcasted_iota(jnp.int32, (moving, moving), 1)
    down = jnp.sum(jnp.where(row == column, names, 0), axis=1, keepdims=True)
    earlier = jnp.where((names == down) & (row < column), 1, 0)
    slot = jnp.sum(earlier, axis=0, keepdims=True)
    target = list_ref[...]
    position = (
        (target // half) * plan.block + group * plan.per_source + (target % half) * SLOT_L + slot
    )
    pos_own[...] = jnp.full(pos_own.shape, -1, jnp.int32)
    pos_own[:, :moving] = jnp.broadcast_to(position, (8, moving))
    for k in range(1, groups):
        pos_copy(k).start()
    for k, dc in peers:
        count_copy(k, dc).start()
    small[2].wait()
    small[3].wait()

    total = plan.blocks * plan.block
    slot_row = lax.broadcasted_iota(jnp.int32, (total, moving), 0)

    def one_hot(positions):
        return jnp.where(slot_row == positions, 1.0, 0.0).astype(jnp.bfloat16)

    pick = one_hot(pos_own[0:1, :moving])
    ones = jnp.ones((moving, LANES), jnp.bfloat16)
    rows = jnp.dot(pick, moving_own[...], preferred_element_type=jnp.float32)
    flags = jnp.dot(pick, ones, preferred_element_type=jnp.float32)
    for k in range(1, groups):
        pos_copy(k).wait_send()
        moving_copy(k).wait_send()
    for k, dc in distant:
        stay_copy(0, k, dc).start()
    for k in range(1, groups):
        pos_copy(k).wait_recv()
        moving_copy(k).wait_recv()
        pick = one_hot(pos_buf[k - 1, 0:1, :moving])
        rows += jnp.dot(pick, moving_buf[k - 1], preferred_element_type=jnp.float32)
        flags += jnp.dot(pick, ones, preferred_element_type=jnp.float32)
    placed[:, :, :features] = rows.astype(jnp.bfloat16).reshape(plan.blocks, plan.block, features)
    placed[:, :, features:] = flags.astype(jnp.bfloat16).reshape(plan.blocks, plan.block, LANES)

    def slot_copy(k, dc):
        b = k * split + dc
        return pltpu.make_async_remote_copy(
            src_ref=placed.at[owner_at(k) * split + lax.rem(core + dc, split)],
            dst_ref=arrived.at[b],
            send_sem=slot_send.at[b], recv_sem=slot_recv.at[b],
            device_id=(owner_at(k), rep_at(0, dc)), device_id_type=MESH,
        )

    sent = [(k, dc) for k in range(owners) for dc in range(split) if (k, dc) != (0, 0)]
    for k, dc in sent:
        slot_copy(k, dc).start()
    arrived[0] = placed[owner * split + core]
    centre_copy.wait()
    for j in range(half):
        wide = centre_buf[j].astype(jnp.float32)
        norm_buf[j] = jnp.broadcast_to(
            jnp.sum(wide * wide, axis=1, keepdims=True), norm_buf.shape[1:]
        )
    for k, dc in peers:
        count_copy(k, dc).wait_recv()

    arrived_lane = lax.broadcasted_iota(jnp.int32, (1, total), 1)
    arrived_list = (arrived_lane % plan.per_source) // SLOT_L

    def result_copy(j, dc):
        return pltpu.make_async_remote_copy(
            src_ref=result_buf.at[j], dst_ref=out_ref.at[core * half + j],
            send_sem=result_send.at[j, dc], recv_sem=result_recv.at[j, dc],
            device_id=(owner, rep_at(0, dc)), device_id_type=MESH,
        )

    def result_own(j):
        return pltpu.make_async_copy(
            result_buf.at[j], out_ref.at[core * half + j], result_recv.at[j, 0]
        )

    def add_part(j, rows, mask):
        num, mass, mass_row = weigh_rows(
            plan, centre_buf[j], norm_buf[j][:, 0:1], sharp_ref[core * half + j], rows, mask
        )
        total_buf[j] += num
        mass_col[j] += jnp.broadcast_to(mass, mass_col.shape[1:])
        mass_buf[j] += mass_row

    def add_stay(j, first, last):
        lane = lax.broadcasted_iota(jnp.int32, (1, (last - first) * capacity), 1)
        counts = jnp.zeros(lane.shape, jnp.int32)
        for q in range(first, last):
            counts = jnp.where(
                lane // capacity == q - first,
                count_buf[q, pl.ds(core * half + j, 1), :][:, : lane.shape[1]], counts,
            )
        mask = jnp.where(lane % capacity < counts, 1.0, 0.0)
        members = stay_buf[j, first:last].reshape((last - first) * capacity, features)
        add_part(j, members, mask)

    def add_arrivals():
        fine = plan.fine
        rows = arrived[:, :, :features].reshape(total, features)
        marks = arrived[:, :, features:].reshape(total, LANES)
        spread = jnp.full((8, LANES), 1.0 / LANES, jnp.bfloat16)
        present = lax.dot_general(
            spread, marks, (((1,), (1,)), ((), ())), preferred_element_type=jnp.float32
        )[0:1]
        products = lax.dot_general(
            centre_buf[...].reshape(half * fine, features), rows, (((1,), (1,)), ((), ())),
            preferred_element_type=jnp.float32,
        )
        parts = []
        for j in range(half):
            own = products[j * fine : (j + 1) * fine]
            sharp = sharp_ref[core * half + j]
            scores = sharp * (2.0 * own - norm_buf[j][:, 0:1]) / math.sqrt(features)
            raised = jnp.exp(scores - jnp.max(scores, axis=0, keepdims=True))
            weights = (raised / jnp.sum(raised, axis=0, keepdims=True)).astype(jnp.bfloat16)
            here = jnp.where(arrived_list == j, present, 0.0)
            weights = weights * here.astype(jnp.bfloat16)
            mass = jnp.sum(weights.astype(jnp.float32), axis=1, keepdims=True)
            mass_col[j] += jnp.broadcast_to(mass, mass_col.shape[1:])
            parts.append(weights)
        stacked = jnp.concatenate(parts, axis=0)
        ones = jnp.ones((8, total), jnp.bfloat16)
        mass_row = lax.dot_general(
            ones, stacked, (((1,), (1,)), ((), ())), preferred_element_type=jnp.float32
        )
        numerator = jnp.dot(stacked, rows, preferred_element_type=jnp.float32)
        for j in range(half):
            mass_buf[j] += mass_row[:, j * fine : (j + 1) * fine]
            total_buf[j] += numerator[j * fine : (j + 1) * fine]

    def add_near(j):
        total_buf[j] = prior_weight * centre_buf[j].astype(jnp.float32)
        mass_col[j] = jnp.zeros(mass_col.shape[1:], jnp.float32)
        mass_buf[j] = jnp.zeros(mass_buf.shape[1:], jnp.float32)
        own_copy(j).wait()
        for k, dc in siblings:
            stay_copy(j, k, dc).wait_recv()
        add_stay(j, 0, split)

    def pass_on(j):
        for k, dc in distant:
            stay_copy(j, k, dc).wait_send()
            stay_copy(j + 1, k, dc).start()

    def add_far(j):
        for k, dc in distant:
            stay_copy(j, k, dc).wait_recv()
        if groups > 1:
            add_stay(j, split, replicas)

    def finish(j):
        share = 1.0 / (mass_col[j][:, 0:1] + prior_weight)
        result_buf[j] = (total_buf[j] * share).astype(jnp.bfloat16)
        result_own(j).start()
        for dc in range(1, split):
            result_copy(j, dc).start()

    def early(j, carry):
        add_near(j)
        pass_on(j)
        add_far(j)
        return carry

    def settle(j, carry):
        finish(j)
        return carry

    last = half - 1
    lax.fori_loop(0, last, early, 0)
    add_near(last)
    for k, dc in sent:
        slot_copy(k, dc).wait_recv()
    add_arrivals()
    lax.fori_loop(0, last, settle, 0)
    add_far(last)
    finish(last)

    def mass_copy(dc):
        return pltpu.make_async_remote_copy(
            src_ref=mass_buf, dst_ref=mass_ref.at[core],
            send_sem=mass_send.at[dc], recv_sem=mass_recv.at[dc],
            device_id=(owner, rep_at(0, dc)), device_id_type=MESH,
        )

    mass_own = pltpu.make_async_copy(mass_buf, mass_ref.at[core], local_sem)
    mass_own.start()
    for dc in range(1, split):
        mass_copy(dc).start()

    for k, dc in peers:
        count_copy(k, dc).wait_send()
    for k, dc in distant:
        stay_copy(last, k, dc).wait_send()
    for j in range(half):
        for k, dc in siblings:
            stay_copy(j, k, dc).wait_send()
    for k, dc in sent:
        slot_copy(k, dc).wait_send()
    for j in range(half):
        result_own(j).wait()
        for dc in range(1, split):
            result_copy(j, dc).wait()
    mass_own.wait()
    for dc in range(1, split):
        mass_copy(dc).wait()


def deliver_kernel(plan, made_ref, mass_ref, out_ref, share_ref, held, in_sems, out_sems):
    fetches = [
        pltpu.make_async_copy(made_ref.at[i], held.at[i], in_sems.at[i]) for i in range(plan.lists)
    ]
    copies = [
        pltpu.make_async_copy(held.at[i], out_ref.at[i], out_sems.at[i]) for i in range(plan.lists)
    ]
    for fetch in fetches:
        fetch.start()
    replica = lax.axis_index("rep")
    width = plan.fine // plan.replicas
    rows = [mass_ref[s, j, 0:1, :] for s in range(plan.split) for j in range(plan.half)]
    whole = jnp.concatenate(rows, axis=0)
    share = whole[:, :width]
    for r in range(1, plan.replicas):
        share = jnp.where(replica == r, whole[:, r * width : (r + 1) * width], share)
    share_ref[...] = share
    for fetch, copy in zip(fetches, copies):
        fetch.wait()
        copy.start()
    for copy in copies:
        copy.wait()


def fused(plan, stay_rows, stay_count, moving_rows, new_list, centroids, sharpness):
    half, split, replicas = plan.half, plan.split, plan.replicas
    any_space = pl.BlockSpec(memory_space=pl.ANY)
    dma = pltpu.SemaphoreType.DMA
    members = replicas * plan.capacity
    refreshed, mass = pl.pallas_call(
        lambda *refs: fused_kernel(plan, *refs),
        out_shape=(
            jax.ShapeDtypeStruct(centroids.shape, jnp.bfloat16),
            jax.ShapeDtypeStruct((split, half, 8, plan.fine), jnp.float32),
        ),
        in_specs=[pl.BlockSpec(memory_space=pltpu.HBM)] * 6,
        out_specs=(any_space, any_space),
        scratch_shapes=[
            pltpu.SMEM((plan.lists,), jnp.int32),
            pltpu.VMEM((plan.moving, plan.features), jnp.bfloat16),
            pltpu.VMEM((1, plan.moving), jnp.int32),
            pltpu.SMEM((plan.lists,), jnp.float32),
            dma((4,)),
            pltpu.VMEM((half, plan.fine, plan.features), jnp.float32),
            pltpu.VMEM((half, plan.fine, LANES), jnp.float32),
            pltpu.VMEM((half, plan.fine, LANES), jnp.float32),
            pltpu.VMEM((half, replicas, plan.capacity, plan.features), jnp.bfloat16),
            pltpu.VMEM((replicas, plan.lists, members), jnp.int32),
            pltpu.VMEM((max(1, plan.groups - 1), plan.moving, plan.features), jnp.bfloat16),
            pltpu.VMEM((8, plan.moving_lanes), jnp.int32),
            pltpu.VMEM((max(1, plan.groups - 1), 8, plan.moving_lanes), jnp.int32),
            pltpu.VMEM((plan.blocks, plan.block, plan.width), jnp.bfloat16),
            pltpu.VMEM((plan.blocks, plan.block, plan.width), jnp.bfloat16),
            pltpu.VMEM((half, plan.fine, plan.features), jnp.bfloat16),
            pltpu.VMEM((half, plan.fine, plan.features), jnp.bfloat16),
            pltpu.VMEM((half, 8, plan.fine), jnp.float32),
            dma((half, replicas)), dma((half, replicas)),
            dma((replicas,)), dma((replicas,)),
            dma((plan.groups,)), dma((plan.groups,)),
            dma((plan.groups,)), dma((plan.groups,)),
            dma((plan.blocks,)), dma((plan.blocks,)),
            dma,
            dma((half, split)), dma((half, split)),
            dma((split,)), dma((split,)),
            dma,
        ],
        compiler_params=pltpu.CompilerParams(
            collective_id=0, has_side_effects=True, vmem_limit_bytes=VMEM_GRANT
        ),
    )(stay_rows, stay_count.reshape(-1), moving_rows, new_list.reshape(1, -1), centroids, sharpness)
    return pl.pallas_call(
        lambda *refs: deliver_kernel(plan, *refs),
        out_shape=(
            jax.ShapeDtypeStruct(centroids.shape, jnp.bfloat16),
            jax.ShapeDtypeStruct((plan.lists, plan.fine // replicas), jnp.float32),
        ),
        in_specs=[any_space, pl.BlockSpec(memory_space=pltpu.VMEM)],
        out_specs=(any_space, pl.BlockSpec(memory_space=pltpu.VMEM)),
        scratch_shapes=[
            pltpu.VMEM(centroids.shape, jnp.bfloat16), dma((plan.lists,)), dma((plan.lists,))
        ],
        compiler_params=pltpu.CompilerParams(vmem_limit_bytes=VMEM_GRANT),
    )(refreshed, mass)


def device_program(stay_rows, stay_count, moving_rows, new_list, centroids, sharpness):
    lists_here, capacity, features = stay_rows.shape
    plan = Plan(
        lax.axis_size("owner"), lax.axis_size("rep"), lists_here, capacity, features,
        centroids.shape[1], moving_rows.shape[0],
    )
    step = (lambda *a: fused(plan, *a)) if plan.fits() else local
    return step(stay_rows, stay_count, moving_rows, new_list, centroids, sharpness)


def solution(mesh):
    in_specs = (
        P("owner", "rep", None),
        P("owner", "rep"),
        P(("owner", "rep"), None),
        P(("owner", "rep")),
        P("owner", None, None),
        P("owner"),
    )
    out_specs = (P("owner", None, None), P("owner", "rep"))
    return jax.shard_map(device_program, mesh=mesh, in_specs=in_specs, out_specs=out_specs, check_vma=False)
```

```python
import math

import jax
import jax.numpy as jnp
from jax import lax
from jax.experimental import pallas as pl
from jax.experimental.pallas import tpu as pltpu
from jax.sharding import PartitionSpec as P

SLOT_L = 2


prior_weight = 1.0


def partner(value, axis, stride):
    mask = 2**stride
    pairs = [(source, source ^ mask) for source in range(lax.axis_size(axis))]
    return lax.ppermute(value, axis, pairs)


def weigh(members, live_mask, centres, centre_norm, sharp, features):
    products = jnp.einsum("lrd,lfd->lrf", members, centres, preferred_element_type=jnp.float32)
    scores = sharp[:, None, None] * (2.0 * products - centre_norm[:, None, :]) / math.sqrt(features)
    weights = jax.nn.softmax(scores, axis=-1).astype(jnp.bfloat16) * live_mask[:, :, None]
    numerator = jnp.einsum("lrf,lrd->lfd", weights, members, preferred_element_type=jnp.float32)
    return (numerator, jnp.sum(weights.astype(jnp.float32), axis=1))


def local(stay_rows, stay_count, moving_rows, new_list, centroids, sharpness):
    owners = lax.axis_size("owner")
    replicas = lax.axis_size("rep")
    lists_here, capacity, features = stay_rows.shape
    fine_count = centroids.shape[1]
    centre_norm = jnp.sum(jnp.square(centroids.astype(jnp.float32)), axis=-1)
    outgoing_count = new_list.shape[0]
    order_index = jnp.arange(outgoing_count)
    earlier = (new_list[None, :] == new_list[:, None]) & (
        order_index[None, :] < order_index[:, None]
    )
    slot_index = jnp.sum(earlier.astype(jnp.int32), axis=1)
    local_list = new_list % lists_here
    target_owner = new_list // lists_here
    position = (local_list * owners + target_owner) * SLOT_L + slot_index
    slot_total = lists_here * owners * SLOT_L
    outgoing = (
        jnp.zeros((slot_total, features), jnp.bfloat16)
        .at[position]
        .set(moving_rows, unique_indices=True)
    )
    occupied = (
        jnp.zeros((slot_total,), jnp.bfloat16)
        .at[position]
        .set(jnp.ones((outgoing_count,), jnp.bfloat16), unique_indices=True)
    )
    arrived, present = (
        lax.all_to_all(
            outgoing.reshape(lists_here, owners, SLOT_L, features),
            "owner",
            split_axis=1,
            concat_axis=1,
            tiled=True,
        ),
        lax.all_to_all(
            occupied.reshape(lists_here, owners, SLOT_L),
            "owner",
            split_axis=1,
            concat_axis=1,
            tiled=True,
        ),
    )
    arrive_slots = owners * SLOT_L
    arrivals = arrived.reshape(lists_here, arrive_slots, features)
    present = present.reshape(lists_here, arrive_slots)
    live_count = stay_count[:, 0]
    replica = lax.axis_index("rep")
    fine_share = fine_count // replicas
    groups = max(1, replicas // lists_here)
    per_rep = max(1, lists_here // replicas)
    slot_mask = (jnp.arange(capacity)[None, :] < live_count[:, None]).astype(jnp.bfloat16)
    stay_pieces = stay_rows.reshape(lists_here * groups, capacity // groups, features)
    mask_pieces = slot_mask.reshape(lists_here * groups, capacity // groups)
    moved_stay, moved_mask = (
        lax.all_to_all(stay_pieces, "rep", split_axis=0, concat_axis=1, tiled=True),
        lax.all_to_all(mask_pieces, "rep", split_axis=0, concat_axis=1, tiled=True),
    )
    arrive_pieces = arrivals.reshape(lists_here * groups, arrive_slots // groups, features)
    present_pieces = present.reshape(lists_here * groups, arrive_slots // groups)
    moved_arrive, moved_present = (
        lax.all_to_all(arrive_pieces, "rep", split_axis=0, concat_axis=1, tiled=True),
        lax.all_to_all(present_pieces, "rep", split_axis=0, concat_axis=1, tiled=True),
    )
    members = jnp.concatenate([moved_stay, moved_arrive], axis=1)
    member_mask = jnp.concatenate([moved_mask, moved_present], axis=1)
    first_list = replica * per_rep // groups
    centres = lax.dynamic_slice_in_dim(centroids, first_list, per_rep, 0)
    norms = lax.dynamic_slice_in_dim(centre_norm, first_list, per_rep, 0)
    sharp = lax.dynamic_slice_in_dim(sharpness, first_list, per_rep, 0)
    numerator, mass_sum = weigh(members, member_mask, centres, norms, sharp, features)
    for bit_number in range(groups.bit_length() - 1):
        other_num, other_mass = partner((numerator, mass_sum), "rep", bit_number)
        numerator = numerator + other_num
        mass_sum = mass_sum + other_mass
    refreshed_all = (
        (numerator + prior_weight * centres.astype(jnp.float32))
        / (mass_sum[:, :, None] + prior_weight)
    ).astype(jnp.bfloat16)
    piece_rows = fine_count // groups
    part_index = replica % groups
    refreshed_piece = lax.dynamic_slice_in_dim(
        refreshed_all, part_index * piece_rows, piece_rows, 1
    ).reshape(per_rep * piece_rows, features)
    mass_piece = lax.dynamic_slice_in_dim(mass_sum, part_index * piece_rows, piece_rows, 1).reshape(
        per_rep * piece_rows
    )
    refreshed = lax.all_gather(refreshed_piece, "rep", axis=0, tiled=True).reshape(
        lists_here, fine_count, features
    )
    mass_whole = lax.all_gather(mass_piece, "rep", axis=0, tiled=True).reshape(
        lists_here, fine_count
    )
    return (refreshed, lax.dynamic_slice_in_dim(mass_whole, replica * fine_share, fine_share, 1))


LANES = 128
VMEM_BUDGET = 40 * 2**20
VMEM_GRANT = 48 * 2**20
MESH = pl.DeviceIdType.MESH


class Plan:
    def __init__(self, owners, replicas, lists, capacity, features, fine, moving):
        self.owners, self.replicas, self.lists = owners, replicas, lists
        self.capacity, self.features, self.fine, self.moving = capacity, features, fine, moving
        self.split = 2 if replicas % 2 == 0 and lists % 2 == 0 else 1
        self.groups = replicas // self.split
        self.half = lists // self.split
        self.per_source = self.half * SLOT_L
        self.block = self.groups * self.per_source
        self.blocks = owners * self.split
        self.width = features + LANES
        self.moving_lanes = -(-moving // LANES) * LANES

    def fits(self):
        slots = 2 * self.blocks * self.block * self.width
        held = self.half * self.replicas * self.capacity * self.features
        centres = 2 * self.half * self.fine * self.features
        gathered = self.groups * self.moving * self.features
        small = 2 * (slots + held + centres + gathered)
        return (
            small <= VMEM_BUDGET
            and self.block % 16 == 0
            and self.capacity % 16 == 0
            and self.moving % 16 == 0
            and self.features % LANES == 0
            and self.fine % LANES == 0
        )


def weigh_rows(plan, centres, norm, sharp, rows, mask):
    products = lax.dot_general(
        centres, rows, (((1,), (1,)), ((), ())), preferred_element_type=jnp.float32
    )
    scores = sharp * (2.0 * products - norm) / math.sqrt(plan.features)
    top = jnp.max(scores, axis=0, keepdims=True)
    raised = jnp.exp(scores - top)
    weights = (raised / jnp.sum(raised, axis=0, keepdims=True)).astype(jnp.bfloat16)
    weights = weights * mask.astype(jnp.bfloat16)
    numerator = jnp.dot(weights, rows, preferred_element_type=jnp.float32)
    mass = jnp.sum(weights.astype(jnp.float32), axis=1, keepdims=True)
    ones = jnp.ones((8, rows.shape[0]), jnp.bfloat16)
    mass_row = lax.dot_general(
        ones, weights, (((1,), (1,)), ((), ())), preferred_element_type=jnp.float32
    )
    return numerator, mass, mass_row


def fused_kernel(
    plan,
    stay_ref, count_in, moving_ref, list_in, centre_ref, sharp_in,
    out_ref, mass_ref,
    count_ref, moving_own, list_ref, sharp_ref, operand_sem, total_buf, mass_col, norm_buf,
    stay_buf, count_buf, moving_buf, pos_own, pos_buf, placed, arrived, centre_buf, result_buf, mass_buf,
    stay_send, stay_recv, count_send, count_recv, moving_send, moving_recv, pos_send, pos_recv,
    slot_send, slot_recv, centre_sem, result_send, result_recv, mass_send, mass_recv, local_sem,
):
    owners, split, groups, half = plan.owners, plan.split, plan.groups, plan.half
    replicas, capacity, features = plan.replicas, plan.capacity, plan.features
    owner = lax.axis_index("owner")
    replica = lax.axis_index("rep")
    core = replica % split
    group = replica // split

    def rep_at(k, dc):
        return lax.rem(group + k, groups) * split + lax.rem(core + dc, split)

    def owner_at(k):
        return lax.rem(owner + k, owners)

    peers = [(k, dc) for k in range(groups) for dc in range(split) if (k, dc) != (0, 0)]
    plane = [(k, dc) for k in range(1, owners) for dc in range(split)]
    barrier = pltpu.get_barrier_semaphore()
    for k, dc in peers:
        pl.semaphore_signal(barrier, inc=1, device_id=(owner, rep_at(k, dc)), device_id_type=MESH)
    for k, dc in plane:
        pl.semaphore_signal(
            barrier, inc=1, device_id=(owner_at(k), rep_at(0, dc)), device_id_type=MESH
        )

    small = [
        pltpu.make_async_copy(source, held, operand_sem.at[i])
        for i, (source, held) in enumerate([
            (list_in, list_ref), (count_in, count_ref), (moving_ref, moving_own), (sharp_in, sharp_ref),
        ])
    ]
    for copy in small:
        copy.start()
    centre_copy = pltpu.make_async_copy(
        centre_ref.at[pl.ds(core * half, half)], centre_buf, centre_sem
    )
    centre_copy.start()

    def own_copy(j):
        return pltpu.make_async_copy(
            stay_ref.at[core * half + j], stay_buf.at[j, 0], stay_recv.at[j, 0]
        )

    for j in range(half):
        own_copy(j).start()

    pl.semaphore_wait(barrier, len(peers) + len(plane))

    def moving_copy(k):
        return pltpu.make_async_remote_copy(
            src_ref=moving_ref, dst_ref=moving_buf.at[k - 1],
            send_sem=moving_send.at[k - 1], recv_sem=moving_recv.at[k - 1],
            device_id=(owner, rep_at(k, 0)), device_id_type=MESH,
        )

    def pos_copy(k):
        return pltpu.make_async_remote_copy(
            src_ref=pos_own, dst_ref=pos_buf.at[k - 1],
            send_sem=pos_send.at[k - 1], recv_sem=pos_recv.at[k - 1],
            device_id=(owner, rep_at(k, 0)), device_id_type=MESH,
        )

    for k in range(1, groups):
        moving_copy(k).start()

    def count_copy(k, dc):
        q = k * split + dc
        return pltpu.make_async_remote_copy(
            src_ref=count_buf.at[0], dst_ref=count_buf.at[q],
            send_sem=count_send.at[q], recv_sem=count_recv.at[q],
            device_id=(owner, rep_at(k, dc)), device_id_type=MESH,
        )

    def stay_copy(j, k, dc):
        q = k * split + dc
        return pltpu.make_async_remote_copy(
            src_ref=stay_ref.at[lax.rem(core + dc, split) * half + j], dst_ref=stay_buf.at[j, q],
            send_sem=stay_send.at[j, q], recv_sem=stay_recv.at[j, q],
            device_id=(owner, rep_at(k, dc)), device_id_type=MESH,
        )

    siblings = [(k, dc) for k, dc in peers if k == 0]
    distant = [(k, dc) for k, dc in peers if k > 0]
    ahead = min(len(distant) + 1, half * len(distant))
    for i in range(ahead):
        j, place = divmod(i, len(distant))
        stay_copy(j, *distant[place]).start()
    for j in range(half):
        for k, dc in siblings:
            stay_copy(j, k, dc).start()

    moving = plan.moving
    small[0].wait()
    small[1].wait()
    line = lax.broadcasted_iota(jnp.int32, count_buf.shape[1:], 0)
    live = jnp.zeros(count_buf.shape[1:], jnp.int32)
    for i in range(plan.lists):
        live = jnp.where(line == i, count_ref[i], live)
    count_buf[0] = live
    names = jnp.broadcast_to(list_ref[...], (moving, moving))
    row = lax.broadcasted_iota(jnp.int32, (moving, moving), 0)
    column = lax.broadcasted_iota(jnp.int32, (moving, moving), 1)
    down = jnp.sum(jnp.where(row == column, names, 0), axis=1, keepdims=True)
    earlier = jnp.where((names == down) & (row < column), 1, 0)
    slot = jnp.sum(earlier, axis=0, keepdims=True)
    target = list_ref[...]
    position = (
        (target // half) * plan.block + group * plan.per_source + (target % half) * SLOT_L + slot
    )
    pos_own[...] = jnp.full(pos_own.shape, -1, jnp.int32)
    pos_own[:, :moving] = jnp.broadcast_to(position, (8, moving))
    for k in range(1, groups):
        pos_copy(k).start()
    for k, dc in peers:
        count_copy(k, dc).start()
    small[2].wait()
    small[3].wait()

    total = plan.blocks * plan.block
    slot_row = lax.broadcasted_iota(jnp.int32, (total, moving), 0)

    def one_hot(positions):
        return jnp.where(slot_row == positions, 1.0, 0.0).astype(jnp.bfloat16)

    pick = one_hot(pos_own[0:1, :moving])
    ones = jnp.ones((moving, LANES), jnp.bfloat16)
    rows = jnp.dot(pick, moving_own[...], preferred_element_type=jnp.float32)
    flags = jnp.dot(pick, ones, preferred_element_type=jnp.float32)
    for k in range(1, groups):
        pos_copy(k).wait_send()
        moving_copy(k).wait_send()
    for k in range(1, groups):
        pos_copy(k).wait_recv()
        moving_copy(k).wait_recv()
        pick = one_hot(pos_buf[k - 1, 0:1, :moving])
        rows += jnp.dot(pick, moving_buf[k - 1], preferred_element_type=jnp.float32)
        flags += jnp.dot(pick, ones, preferred_element_type=jnp.float32)
    placed[:, :, :features] = rows.astype(jnp.bfloat16).reshape(plan.blocks, plan.block, features)
    placed[:, :, features:] = flags.astype(jnp.bfloat16).reshape(plan.blocks, plan.block, LANES)

    def slot_copy(k, dc):
        b = k * split + dc
        return pltpu.make_async_remote_copy(
            src_ref=placed.at[owner_at(k) * split + lax.rem(core + dc, split)],
            dst_ref=arrived.at[b],
            send_sem=slot_send.at[b], recv_sem=slot_recv.at[b],
            device_id=(owner_at(k), rep_at(0, dc)), device_id_type=MESH,
        )

    sent = [(k, dc) for k in range(owners) for dc in range(split) if (k, dc) != (0, 0)]
    for k, dc in sent:
        slot_copy(k, dc).start()
    arrived[0] = placed[owner * split + core]
    centre_copy.wait()
    for j in range(half):
        wide = centre_buf[j].astype(jnp.float32)
        norm_buf[j] = jnp.broadcast_to(
            jnp.sum(wide * wide, axis=1, keepdims=True), norm_buf.shape[1:]
        )
    for k, dc in peers:
        count_copy(k, dc).wait_recv()

    arrived_lane = lax.broadcasted_iota(jnp.int32, (1, total), 1)
    arrived_list = (arrived_lane % plan.per_source) // SLOT_L

    def result_copy(j, dc):
        return pltpu.make_async_remote_copy(
            src_ref=result_buf.at[j], dst_ref=out_ref.at[core * half + j],
            send_sem=result_send.at[j, dc], recv_sem=result_recv.at[j, dc],
            device_id=(owner, rep_at(0, dc)), device_id_type=MESH,
        )

    def result_own(j):
        return pltpu.make_async_copy(
            result_buf.at[j], out_ref.at[core * half + j], result_recv.at[j, 0]
        )

    def add_part(j, rows, mask):
        num, mass, mass_row = weigh_rows(
            plan, centre_buf[j], norm_buf[j][:, 0:1], sharp_ref[core * half + j], rows, mask
        )
        total_buf[j] += num
        mass_col[j] += jnp.broadcast_to(mass, mass_col.shape[1:])
        mass_buf[j] += mass_row

    def add_stay(j, first, last):
        lane = lax.broadcasted_iota(jnp.int32, (1, (last - first) * capacity), 1)
        counts = jnp.zeros(lane.shape, jnp.int32)
        for q in range(first, last):
            counts = jnp.where(
                lane // capacity == q - first,
                count_buf[q, pl.ds(core * half + j, 1), :][:, : lane.shape[1]], counts,
            )
        mask = jnp.where(lane % capacity < counts, 1.0, 0.0)
        members = stay_buf[j, first:last].reshape((last - first) * capacity, features)
        add_part(j, members, mask)

    def add_arrivals():
        fine = plan.fine
        rows = arrived[:, :, :features].reshape(total, features)
        marks = arrived[:, :, features:].reshape(total, LANES)
        spread = jnp.full((8, LANES), 1.0 / LANES, jnp.bfloat16)
        present = lax.dot_general(
            spread, marks, (((1,), (1,)), ((), ())), preferred_element_type=jnp.float32
        )[0:1]
        products = lax.dot_general(
            centre_buf[...].reshape(half * fine, features), rows, (((1,), (1,)), ((), ())),
            preferred_element_type=jnp.float32,
        )
        parts = []
        for j in range(half):
            own = products[j * fine : (j + 1) * fine]
            sharp = sharp_ref[core * half + j]
            scores = sharp * (2.0 * own - norm_buf[j][:, 0:1]) / math.sqrt(features)
            raised = jnp.exp(scores - jnp.max(scores, axis=0, keepdims=True))
            weights = (raised / jnp.sum(raised, axis=0, keepdims=True)).astype(jnp.bfloat16)
            here = jnp.where(arrived_list == j, present, 0.0)
            weights = weights * here.astype(jnp.bfloat16)
            mass = jnp.sum(weights.astype(jnp.float32), axis=1, keepdims=True)
            mass_col[j] += jnp.broadcast_to(mass, mass_col.shape[1:])
            parts.append(weights)
        stacked = jnp.concatenate(parts, axis=0)
        ones = jnp.ones((8, total), jnp.bfloat16)
        mass_row = lax.dot_general(
            ones, stacked, (((1,), (1,)), ((), ())), preferred_element_type=jnp.float32
        )
        numerator = jnp.dot(stacked, rows, preferred_element_type=jnp.float32)
        for j in range(half):
            mass_buf[j] += mass_row[:, j * fine : (j + 1) * fine]
            total_buf[j] += numerator[j * fine : (j + 1) * fine]

    def add_near(j):
        total_buf[j] = prior_weight * centre_buf[j].astype(jnp.float32)
        mass_col[j] = jnp.zeros(mass_col.shape[1:], jnp.float32)
        mass_buf[j] = jnp.zeros(mass_buf.shape[1:], jnp.float32)
        own_copy(j).wait()
        for k, dc in siblings:
            stay_copy(j, k, dc).wait_recv()
        add_stay(j, 0, split)

    def pass_on(j):
        for i, (k, dc) in enumerate(distant):
            stay_copy(j, k, dc).wait_send()
            step, place = divmod(i + ahead, len(distant))

            @pl.when(j + step < half)
            def _():
                stay_copy(j + step, *distant[place]).start()

    def add_far(j):
        for k, dc in distant:
            stay_copy(j, k, dc).wait_recv()
        if groups > 1:
            add_stay(j, split, replicas)

    def finish(j):
        share = 1.0 / (mass_col[j][:, 0:1] + prior_weight)
        result_buf[j] = (total_buf[j] * share).astype(jnp.bfloat16)
        result_own(j).start()
        for dc in range(1, split):
            result_copy(j, dc).start()

    def early(j, carry):
        add_near(j)
        pass_on(j)
        add_far(j)
        return carry

    def settle(j, carry):
        finish(j)
        return carry

    last = half - 1
    lax.fori_loop(0, last, early, 0)
    add_near(last)
    for k, dc in sent:
        slot_copy(k, dc).wait_recv()
    add_arrivals()
    lax.fori_loop(0, last, settle, 0)
    add_far(last)
    finish(last)

    def mass_copy(dc):
        return pltpu.make_async_remote_copy(
            src_ref=mass_buf, dst_ref=mass_ref.at[core],
            send_sem=mass_send.at[dc], recv_sem=mass_recv.at[dc],
            device_id=(owner, rep_at(0, dc)), device_id_type=MESH,
        )

    mass_own = pltpu.make_async_copy(mass_buf, mass_ref.at[core], local_sem)
    mass_own.start()
    for dc in range(1, split):
        mass_copy(dc).start()

    for k, dc in peers:
        count_copy(k, dc).wait_send()
    for k, dc in distant:
        stay_copy(last, k, dc).wait_send()
    for j in range(half):
        for k, dc in siblings:
            stay_copy(j, k, dc).wait_send()
    for k, dc in sent:
        slot_copy(k, dc).wait_send()
    for j in range(half):
        result_own(j).wait()
        for dc in range(1, split):
            result_copy(j, dc).wait()
    mass_own.wait()
    for dc in range(1, split):
        mass_copy(dc).wait()


def fused(plan, stay_rows, stay_count, moving_rows, new_list, centroids, sharpness):
    half, split, replicas = plan.half, plan.split, plan.replicas
    any_space = pl.BlockSpec(memory_space=pl.ANY)
    dma = pltpu.SemaphoreType.DMA
    members = replicas * plan.capacity
    refreshed, mass = pl.pallas_call(
        lambda *refs: fused_kernel(plan, *refs),
        out_shape=(
            pltpu.VMEM(centroids.shape, jnp.bfloat16),
            pltpu.VMEM((split, half, 8, plan.fine), jnp.float32),
        ),
        in_specs=[pl.BlockSpec(memory_space=pltpu.HBM)] * 6,
        out_specs=(any_space, any_space),
        scratch_shapes=[
            pltpu.SMEM((plan.lists,), jnp.int32),
            pltpu.VMEM((plan.moving, plan.features), jnp.bfloat16),
            pltpu.VMEM((1, plan.moving), jnp.int32),
            pltpu.SMEM((plan.lists,), jnp.float32),
            dma((4,)),
            pltpu.VMEM((half, plan.fine, plan.features), jnp.float32),
            pltpu.VMEM((half, plan.fine, LANES), jnp.float32),
            pltpu.VMEM((half, plan.fine, LANES), jnp.float32),
            pltpu.VMEM((half, replicas, plan.capacity, plan.features), jnp.bfloat16),
            pltpu.VMEM((replicas, plan.lists, members), jnp.int32),
            pltpu.VMEM((max(1, plan.groups - 1), plan.moving, plan.features), jnp.bfloat16),
            pltpu.VMEM((8, plan.moving_lanes), jnp.int32),
            pltpu.VMEM((max(1, plan.groups - 1), 8, plan.moving_lanes), jnp.int32),
            pltpu.VMEM((plan.blocks, plan.block, plan.width), jnp.bfloat16),
            pltpu.VMEM((plan.blocks, plan.block, plan.width), jnp.bfloat16),
            pltpu.VMEM((half, plan.fine, plan.features), jnp.bfloat16),
            pltpu.VMEM((half, plan.fine, plan.features), jnp.bfloat16),
            pltpu.VMEM((half, 8, plan.fine), jnp.float32),
            dma((half, replicas)), dma((half, replicas)),
            dma((replicas,)), dma((replicas,)),
            dma((plan.groups,)), dma((plan.groups,)),
            dma((plan.groups,)), dma((plan.groups,)),
            dma((plan.blocks,)), dma((plan.blocks,)),
            dma,
            dma((half, split)), dma((half, split)),
            dma((split,)), dma((split,)),
            dma,
        ],
        compiler_params=pltpu.CompilerParams(
            collective_id=0, has_side_effects=True, vmem_limit_bytes=VMEM_GRANT
        ),
    )(*[
        pltpu.with_memory_space_constraint(x, pltpu.HBM)
        for x in (
            stay_rows, stay_count.reshape(-1), moving_rows, new_list.reshape(1, -1), centroids,
            sharpness,
        )
    ])
    fine_share = plan.fine // replicas
    whole = mass[:, :, 0, :].reshape(plan.lists, plan.fine)
    share = lax.dynamic_slice_in_dim(whole, lax.axis_index("rep") * fine_share, fine_share, 1)
    return refreshed, share


def device_program(stay_rows, stay_count, moving_rows, new_list, centroids, sharpness):
    lists_here, capacity, features = stay_rows.shape
    plan = Plan(
        lax.axis_size("owner"), lax.axis_size("rep"), lists_here, capacity, features,
        centroids.shape[1], moving_rows.shape[0],
    )
    step = (lambda *a: fused(plan, *a)) if plan.fits() else local
    return step(stay_rows, stay_count, moving_rows, new_list, centroids, sharpness)


def solution(mesh):
    in_specs = (
        P("owner", "rep", None),
        P("owner", "rep"),
        P(("owner", "rep"), None),
        P(("owner", "rep")),
        P("owner", None, None),
        P("owner"),
    )
    out_specs = (P("owner", None, None), P("owner", "rep"))
    return jax.shard_map(device_program, mesh=mesh, in_specs=in_specs, out_specs=out_specs, check_vma=False)
```

```python
import math

import jax
import jax.numpy as jnp
from jax import lax
from jax.experimental import pallas as pl
from jax.experimental.pallas import tpu as pltpu
from jax.sharding import PartitionSpec as P

SLOT_L = 2


prior_weight = 1.0


def partner(value, axis, stride):
    mask = 2**stride
    pairs = [(source, source ^ mask) for source in range(lax.axis_size(axis))]
    return lax.ppermute(value, axis, pairs)


def weigh(members, live_mask, centres, centre_norm, sharp, features):
    products = jnp.einsum("lrd,lfd->lrf", members, centres, preferred_element_type=jnp.float32)
    scores = sharp[:, None, None] * (2.0 * products - centre_norm[:, None, :]) / math.sqrt(features)
    weights = jax.nn.softmax(scores, axis=-1).astype(jnp.bfloat16) * live_mask[:, :, None]
    numerator = jnp.einsum("lrf,lrd->lfd", weights, members, preferred_element_type=jnp.float32)
    return (numerator, jnp.sum(weights.astype(jnp.float32), axis=1))


def local(stay_rows, stay_count, moving_rows, new_list, centroids, sharpness):
    owners = lax.axis_size("owner")
    replicas = lax.axis_size("rep")
    lists_here, capacity, features = stay_rows.shape
    fine_count = centroids.shape[1]
    centre_norm = jnp.sum(jnp.square(centroids.astype(jnp.float32)), axis=-1)
    outgoing_count = new_list.shape[0]
    order_index = jnp.arange(outgoing_count)
    earlier = (new_list[None, :] == new_list[:, None]) & (
        order_index[None, :] < order_index[:, None]
    )
    slot_index = jnp.sum(earlier.astype(jnp.int32), axis=1)
    local_list = new_list % lists_here
    target_owner = new_list // lists_here
    position = (local_list * owners + target_owner) * SLOT_L + slot_index
    slot_total = lists_here * owners * SLOT_L
    outgoing = (
        jnp.zeros((slot_total, features), jnp.bfloat16)
        .at[position]
        .set(moving_rows, unique_indices=True)
    )
    occupied = (
        jnp.zeros((slot_total,), jnp.bfloat16)
        .at[position]
        .set(jnp.ones((outgoing_count,), jnp.bfloat16), unique_indices=True)
    )
    arrived, present = (
        lax.all_to_all(
            outgoing.reshape(lists_here, owners, SLOT_L, features),
            "owner",
            split_axis=1,
            concat_axis=1,
            tiled=True,
        ),
        lax.all_to_all(
            occupied.reshape(lists_here, owners, SLOT_L),
            "owner",
            split_axis=1,
            concat_axis=1,
            tiled=True,
        ),
    )
    arrive_slots = owners * SLOT_L
    arrivals = arrived.reshape(lists_here, arrive_slots, features)
    present = present.reshape(lists_here, arrive_slots)
    live_count = stay_count[:, 0]
    replica = lax.axis_index("rep")
    fine_share = fine_count // replicas
    groups = max(1, replicas // lists_here)
    per_rep = max(1, lists_here // replicas)
    slot_mask = (jnp.arange(capacity)[None, :] < live_count[:, None]).astype(jnp.bfloat16)
    stay_pieces = stay_rows.reshape(lists_here * groups, capacity // groups, features)
    mask_pieces = slot_mask.reshape(lists_here * groups, capacity // groups)
    moved_stay, moved_mask = (
        lax.all_to_all(stay_pieces, "rep", split_axis=0, concat_axis=1, tiled=True),
        lax.all_to_all(mask_pieces, "rep", split_axis=0, concat_axis=1, tiled=True),
    )
    arrive_pieces = arrivals.reshape(lists_here * groups, arrive_slots // groups, features)
    present_pieces = present.reshape(lists_here * groups, arrive_slots // groups)
    moved_arrive, moved_present = (
        lax.all_to_all(arrive_pieces, "rep", split_axis=0, concat_axis=1, tiled=True),
        lax.all_to_all(present_pieces, "rep", split_axis=0, concat_axis=1, tiled=True),
    )
    members = jnp.concatenate([moved_stay, moved_arrive], axis=1)
    member_mask = jnp.concatenate([moved_mask, moved_present], axis=1)
    first_list = replica * per_rep // groups
    centres = lax.dynamic_slice_in_dim(centroids, first_list, per_rep, 0)
    norms = lax.dynamic_slice_in_dim(centre_norm, first_list, per_rep, 0)
    sharp = lax.dynamic_slice_in_dim(sharpness, first_list, per_rep, 0)
    numerator, mass_sum = weigh(members, member_mask, centres, norms, sharp, features)
    for bit_number in range(groups.bit_length() - 1):
        other_num, other_mass = partner((numerator, mass_sum), "rep", bit_number)
        numerator = numerator + other_num
        mass_sum = mass_sum + other_mass
    refreshed_all = (
        (numerator + prior_weight * centres.astype(jnp.float32))
        / (mass_sum[:, :, None] + prior_weight)
    ).astype(jnp.bfloat16)
    piece_rows = fine_count // groups
    part_index = replica % groups
    refreshed_piece = lax.dynamic_slice_in_dim(
        refreshed_all, part_index * piece_rows, piece_rows, 1
    ).reshape(per_rep * piece_rows, features)
    mass_piece = lax.dynamic_slice_in_dim(mass_sum, part_index * piece_rows, piece_rows, 1).reshape(
        per_rep * piece_rows
    )
    refreshed = lax.all_gather(refreshed_piece, "rep", axis=0, tiled=True).reshape(
        lists_here, fine_count, features
    )
    mass_whole = lax.all_gather(mass_piece, "rep", axis=0, tiled=True).reshape(
        lists_here, fine_count
    )
    return (refreshed, lax.dynamic_slice_in_dim(mass_whole, replica * fine_share, fine_share, 1))


LANES = 128
VMEM_BUDGET = 40 * 2**20
VMEM_GRANT = 48 * 2**20
MESH = pl.DeviceIdType.MESH


class Plan:
    def __init__(self, owners, replicas, lists, capacity, features, fine, moving):
        self.owners, self.replicas, self.lists = owners, replicas, lists
        self.capacity, self.features, self.fine, self.moving = capacity, features, fine, moving
        self.split = 2 if replicas % 2 == 0 and lists % 2 == 0 else 1
        self.groups = replicas // self.split
        self.half = lists // self.split
        self.per_source = self.half * SLOT_L
        self.block = self.groups * self.per_source
        self.blocks = owners * self.split
        self.width = features + LANES
        self.moving_lanes = -(-moving // LANES) * LANES

    def fits(self):
        slots = 2 * self.blocks * self.block * self.width
        held = self.half * self.replicas * self.capacity * self.features
        centres = 2 * self.half * self.fine * self.features
        gathered = self.groups * self.moving * self.features
        small = 2 * (slots + held + centres + gathered)
        return (
            small <= VMEM_BUDGET
            and self.per_source % 8 == 0
            and self.capacity % 16 == 0
            and self.moving % 16 == 0
            and self.features % LANES == 0
            and self.fine % LANES == 0
        )


def weigh_rows(plan, centres, norm, sharp, rows, mask):
    products = lax.dot_general(
        centres, rows, (((1,), (1,)), ((), ())), preferred_element_type=jnp.float32
    )
    scores = sharp * (2.0 * products - norm) / math.sqrt(plan.features)
    top = jnp.max(scores, axis=0, keepdims=True)
    raised = jnp.exp(scores - top)
    weights = (raised / jnp.sum(raised, axis=0, keepdims=True)).astype(jnp.bfloat16)
    weights = weights * mask.astype(jnp.bfloat16)
    numerator = jnp.dot(weights, rows, preferred_element_type=jnp.float32)
    mass = jnp.sum(weights.astype(jnp.float32), axis=1, keepdims=True)
    ones = jnp.ones((8, rows.shape[0]), jnp.bfloat16)
    mass_row = lax.dot_general(
        ones, weights, (((1,), (1,)), ((), ())), preferred_element_type=jnp.float32
    )
    return numerator, mass, mass_row


def fused_kernel(
    plan,
    stay_ref, count_in, moving_ref, list_in, centre_ref, sharp_in,
    out_ref, mass_ref,
    count_ref, moving_own, list_ref, sharp_ref, operand_sem, total_buf, mass_col, norm_buf,
    stay_buf, count_buf, moving_buf, pos_own, pos_buf, placed, arrived, centre_buf, result_buf, mass_buf,
    stay_send, stay_recv, count_send, count_recv, moving_send, moving_recv, pos_send, pos_recv,
    slot_send, slot_recv, centre_sem, result_send, result_recv, mass_send, mass_recv, local_sem,
):
    owners, split, groups, half = plan.owners, plan.split, plan.groups, plan.half
    replicas, capacity, features = plan.replicas, plan.capacity, plan.features
    owner = lax.axis_index("owner")
    replica = lax.axis_index("rep")
    core = replica % split
    group = replica // split

    def rep_at(k, dc):
        return lax.rem(group + k, groups) * split + lax.rem(core + dc, split)

    def owner_at(k):
        return lax.rem(owner + k, owners)

    peers = [(k, dc) for k in range(groups) for dc in range(split) if (k, dc) != (0, 0)]
    plane = [(k, dc) for k in range(1, owners) for dc in range(split)]
    barrier = pltpu.get_barrier_semaphore()
    for k, dc in peers:
        pl.semaphore_signal(barrier, inc=1, device_id=(owner, rep_at(k, dc)), device_id_type=MESH)
    for k, dc in plane:
        pl.semaphore_signal(
            barrier, inc=1, device_id=(owner_at(k), rep_at(0, dc)), device_id_type=MESH
        )

    small = [
        pltpu.make_async_copy(source, held, operand_sem.at[i])
        for i, (source, held) in enumerate([
            (list_in, list_ref), (count_in, count_ref), (moving_ref, moving_own), (sharp_in, sharp_ref),
        ])
    ]
    for copy in small:
        copy.start()
    centre_copy = pltpu.make_async_copy(
        centre_ref.at[pl.ds(core * half, half)], centre_buf, centre_sem
    )
    centre_copy.start()

    def own_copy(j):
        return pltpu.make_async_copy(
            stay_ref.at[core * half + j], stay_buf.at[j, 0], stay_recv.at[j, 0]
        )

    for j in range(half):
        own_copy(j).start()

    pl.semaphore_wait(barrier, len(peers) + len(plane))

    def moving_copy(k):
        return pltpu.make_async_remote_copy(
            src_ref=moving_ref, dst_ref=moving_buf.at[k - 1],
            send_sem=moving_send.at[k - 1], recv_sem=moving_recv.at[k - 1],
            device_id=(owner, rep_at(k, 0)), device_id_type=MESH,
        )

    def pos_copy(k):
        return pltpu.make_async_remote_copy(
            src_ref=pos_own, dst_ref=pos_buf.at[k - 1],
            send_sem=pos_send.at[k - 1], recv_sem=pos_recv.at[k - 1],
            device_id=(owner, rep_at(k, 0)), device_id_type=MESH,
        )

    for k in range(1, groups):
        moving_copy(k).start()

    def count_copy(k, dc):
        q = k * split + dc
        return pltpu.make_async_remote_copy(
            src_ref=count_buf.at[0], dst_ref=count_buf.at[q],
            send_sem=count_send.at[q], recv_sem=count_recv.at[q],
            device_id=(owner, rep_at(k, dc)), device_id_type=MESH,
        )

    def stay_copy(j, k, dc):
        q = k * split + dc
        return pltpu.make_async_remote_copy(
            src_ref=stay_ref.at[lax.rem(core + dc, split) * half + j], dst_ref=stay_buf.at[j, q],
            send_sem=stay_send.at[j, q], recv_sem=stay_recv.at[j, q],
            device_id=(owner, rep_at(k, dc)), device_id_type=MESH,
        )

    siblings = [(k, dc) for k, dc in peers if k == 0]
    distant = [(k, dc) for k, dc in peers if k > 0]
    for j in range(half):
        for k, dc in siblings:
            stay_copy(j, k, dc).start()

    moving = plan.moving
    small[0].wait()
    small[1].wait()
    line = lax.broadcasted_iota(jnp.int32, count_buf.shape[1:], 0)
    live = jnp.zeros(count_buf.shape[1:], jnp.int32)
    for i in range(plan.lists):
        live = jnp.where(line == i, count_ref[i], live)
    count_buf[0] = live
    names = jnp.broadcast_to(list_ref[...], (moving, moving))
    row = lax.broadcasted_iota(jnp.int32, (moving, moving), 0)
    column = lax.broadcasted_iota(jnp.int32, (moving, moving), 1)
    down = jnp.sum(jnp.where(row == column, names, 0), axis=1, keepdims=True)
    earlier = jnp.where((names == down) & (row < column), 1, 0)
    slot = jnp.sum(earlier, axis=0, keepdims=True)
    target = list_ref[...]
    position = (
        (target // half) * plan.per_source + (target % half) * SLOT_L + slot
    )
    pos_own[...] = jnp.full(pos_own.shape, -1, jnp.int32)
    pos_own[:, :moving] = jnp.broadcast_to(position, (8, moving))
    for k in range(1, groups):
        pos_copy(k).start()
    for k, dc in peers:
        count_copy(k, dc).start()
    small[2].wait()
    small[3].wait()

    sent = [(k, dc) for k in range(owners) for dc in range(split) if (k, dc) != (0, 0)]
    slots = plan.blocks * plan.per_source
    slot_row = lax.broadcasted_iota(jnp.int32, (slots, moving), 0)
    ones = jnp.ones((moving, LANES), jnp.bfloat16)

    def slot_copy(g, k, dc):
        b = k * split + dc
        return pltpu.make_async_remote_copy(
            src_ref=placed.at[g, owner_at(k) * split + lax.rem(core + dc, split)],
            dst_ref=arrived.at[g, b],
            send_sem=slot_send.at[g, b], recv_sem=slot_recv.at[g, b],
            device_id=(owner_at(k), rep_at(0, dc)), device_id_type=MESH,
        )

    def place_group(g, positions, source):
        pick = jnp.where(slot_row == positions, 1.0, 0.0).astype(jnp.bfloat16)
        rows = jnp.dot(pick, source, preferred_element_type=jnp.float32)
        flags = jnp.dot(pick, ones, preferred_element_type=jnp.float32)
        shape = (plan.blocks, plan.per_source)
        placed[g, :, :, :features] = rows.reshape(*shape, features).astype(jnp.bfloat16)
        placed[g, :, :, features:] = flags.reshape(*shape, LANES).astype(jnp.bfloat16)
        for k, dc in sent:
            slot_copy(g, k, dc).start()
        arrived[g, 0] = placed[g, owner * split + core]

    place_group(0, pos_own[0:1, :moving], moving_own[...])
    for k in range(1, groups):
        pos_copy(k).wait_send()
        moving_copy(k).wait_send()
    ahead = min(len(distant) + 1, half * len(distant))
    for i in range(ahead):
        j, place = divmod(i, len(distant))
        stay_copy(j, *distant[place]).start()
    for k in range(1, groups):
        pos_copy(k).wait_recv()
        moving_copy(k).wait_recv()
        place_group(k, pos_buf[k - 1, 0:1, :moving], moving_buf[k - 1])
    total = groups * slots
    centre_copy.wait()
    for j in range(half):
        wide = centre_buf[j].astype(jnp.float32)
        norm_buf[j] = jnp.broadcast_to(
            jnp.sum(wide * wide, axis=1, keepdims=True), norm_buf.shape[1:]
        )
    for k, dc in peers:
        count_copy(k, dc).wait_recv()

    arrived_lane = lax.broadcasted_iota(jnp.int32, (1, total), 1)
    arrived_list = (arrived_lane % plan.per_source) // SLOT_L

    def result_copy(j, dc):
        return pltpu.make_async_remote_copy(
            src_ref=result_buf.at[j], dst_ref=out_ref.at[core * half + j],
            send_sem=result_send.at[j, dc], recv_sem=result_recv.at[j, dc],
            device_id=(owner, rep_at(0, dc)), device_id_type=MESH,
        )

    def result_own(j):
        return pltpu.make_async_copy(
            result_buf.at[j], out_ref.at[core * half + j], result_recv.at[j, 0]
        )

    def add_part(j, rows, mask):
        num, mass, mass_row = weigh_rows(
            plan, centre_buf[j], norm_buf[j][:, 0:1], sharp_ref[core * half + j], rows, mask
        )
        total_buf[j] += num
        mass_col[j] += jnp.broadcast_to(mass, mass_col.shape[1:])
        mass_buf[j] += mass_row

    def add_stay(j, first, last):
        lane = lax.broadcasted_iota(jnp.int32, (1, (last - first) * capacity), 1)
        counts = jnp.zeros(lane.shape, jnp.int32)
        for q in range(first, last):
            counts = jnp.where(
                lane // capacity == q - first,
                count_buf[q, pl.ds(core * half + j, 1), :][:, : lane.shape[1]], counts,
            )
        mask = jnp.where(lane % capacity < counts, 1.0, 0.0)
        members = stay_buf[j, first:last].reshape((last - first) * capacity, features)
        add_part(j, members, mask)

    def add_arrivals():
        fine = plan.fine
        rows = arrived[:, :, :, :features].reshape(total, features)
        marks = arrived[:, :, :, features:].reshape(total, LANES)
        spread = jnp.full((8, LANES), 1.0 / LANES, jnp.bfloat16)
        present = lax.dot_general(
            spread, marks, (((1,), (1,)), ((), ())), preferred_element_type=jnp.float32
        )[0:1]
        products = lax.dot_general(
            centre_buf[...].reshape(half * fine, features), rows, (((1,), (1,)), ((), ())),
            preferred_element_type=jnp.float32,
        )
        parts = []
        for j in range(half):
            own = products[j * fine : (j + 1) * fine]
            sharp = sharp_ref[core * half + j]
            scores = sharp * (2.0 * own - norm_buf[j][:, 0:1]) / math.sqrt(features)
            raised = jnp.exp(scores - jnp.max(scores, axis=0, keepdims=True))
            weights = (raised / jnp.sum(raised, axis=0, keepdims=True)).astype(jnp.bfloat16)
            here = jnp.where(arrived_list == j, present, 0.0)
            weights = weights * here.astype(jnp.bfloat16)
            mass = jnp.sum(weights.astype(jnp.float32), axis=1, keepdims=True)
            mass_col[j] += jnp.broadcast_to(mass, mass_col.shape[1:])
            parts.append(weights)
        stacked = jnp.concatenate(parts, axis=0)
        ones = jnp.ones((8, total), jnp.bfloat16)
        mass_row = lax.dot_general(
            ones, stacked, (((1,), (1,)), ((), ())), preferred_element_type=jnp.float32
        )
        numerator = jnp.dot(stacked, rows, preferred_element_type=jnp.float32)
        for j in range(half):
            mass_buf[j] += mass_row[:, j * fine : (j + 1) * fine]
            total_buf[j] += numerator[j * fine : (j + 1) * fine]

    def add_near(j):
        total_buf[j] = prior_weight * centre_buf[j].astype(jnp.float32)
        mass_col[j] = jnp.zeros(mass_col.shape[1:], jnp.float32)
        mass_buf[j] = jnp.zeros(mass_buf.shape[1:], jnp.float32)
        own_copy(j).wait()
        for k, dc in siblings:
            stay_copy(j, k, dc).wait_recv()
        add_stay(j, 0, split)

    def pass_on(j):
        for i, (k, dc) in enumerate(distant):
            stay_copy(j, k, dc).wait_send()
            step, place = divmod(i + ahead, len(distant))

            @pl.when(j + step < half)
            def _():
                stay_copy(j + step, *distant[place]).start()

    def add_far(j):
        for k, dc in distant:
            stay_copy(j, k, dc).wait_recv()
        if groups > 1:
            add_stay(j, split, replicas)

    def finish(j):
        share = 1.0 / (mass_col[j][:, 0:1] + prior_weight)
        result_buf[j] = (total_buf[j] * share).astype(jnp.bfloat16)
        result_own(j).start()
        for dc in range(1, split):
            result_copy(j, dc).start()

    def early(j, carry):
        add_near(j)
        pass_on(j)
        add_far(j)
        return carry

    def settle(j, carry):
        finish(j)
        return carry

    last = half - 1
    lax.fori_loop(0, last, early, 0)
    add_near(last)
    for g in range(groups):
        for k, dc in sent:
            slot_copy(g, k, dc).wait_recv()
    add_arrivals()
    lax.fori_loop(0, last, settle, 0)
    add_far(last)
    finish(last)

    def mass_copy(dc):
        return pltpu.make_async_remote_copy(
            src_ref=mass_buf, dst_ref=mass_ref.at[core],
            send_sem=mass_send.at[dc], recv_sem=mass_recv.at[dc],
            device_id=(owner, rep_at(0, dc)), device_id_type=MESH,
        )

    mass_own = pltpu.make_async_copy(mass_buf, mass_ref.at[core], local_sem)
    mass_own.start()
    for dc in range(1, split):
        mass_copy(dc).start()

    for k, dc in peers:
        count_copy(k, dc).wait_send()
    for k, dc in distant:
        stay_copy(last, k, dc).wait_send()
    for j in range(half):
        for k, dc in siblings:
            stay_copy(j, k, dc).wait_send()
    for g in range(groups):
        for k, dc in sent:
            slot_copy(g, k, dc).wait_send()
    for j in range(half):
        result_own(j).wait()
        for dc in range(1, split):
            result_copy(j, dc).wait()
    mass_own.wait()
    for dc in range(1, split):
        mass_copy(dc).wait()


def fused(plan, stay_rows, stay_count, moving_rows, new_list, centroids, sharpness):
    half, split, replicas = plan.half, plan.split, plan.replicas
    any_space = pl.BlockSpec(memory_space=pl.ANY)
    dma = pltpu.SemaphoreType.DMA
    members = replicas * plan.capacity
    refreshed, mass = pl.pallas_call(
        lambda *refs: fused_kernel(plan, *refs),
        out_shape=(
            pltpu.VMEM(centroids.shape, jnp.bfloat16),
            pltpu.VMEM((split, half, 8, plan.fine), jnp.float32),
        ),
        in_specs=[pl.BlockSpec(memory_space=pltpu.HBM)] * 6,
        out_specs=(any_space, any_space),
        scratch_shapes=[
            pltpu.SMEM((plan.lists,), jnp.int32),
            pltpu.VMEM((plan.moving, plan.features), jnp.bfloat16),
            pltpu.VMEM((1, plan.moving), jnp.int32),
            pltpu.SMEM((plan.lists,), jnp.float32),
            dma((4,)),
            pltpu.VMEM((half, plan.fine, plan.features), jnp.float32),
            pltpu.VMEM((half, plan.fine, LANES), jnp.float32),
            pltpu.VMEM((half, plan.fine, LANES), jnp.float32),
            pltpu.VMEM((half, replicas, plan.capacity, plan.features), jnp.bfloat16),
            pltpu.VMEM((replicas, plan.lists, members), jnp.int32),
            pltpu.VMEM((max(1, plan.groups - 1), plan.moving, plan.features), jnp.bfloat16),
            pltpu.VMEM((8, plan.moving_lanes), jnp.int32),
            pltpu.VMEM((max(1, plan.groups - 1), 8, plan.moving_lanes), jnp.int32),
            pltpu.VMEM((plan.groups, plan.blocks, plan.per_source, plan.width), jnp.bfloat16),
            pltpu.VMEM((plan.groups, plan.blocks, plan.per_source, plan.width), jnp.bfloat16),
            pltpu.VMEM((half, plan.fine, plan.features), jnp.bfloat16),
            pltpu.VMEM((half, plan.fine, plan.features), jnp.bfloat16),
            pltpu.VMEM((half, 8, plan.fine), jnp.float32),
            dma((half, replicas)), dma((half, replicas)),
            dma((replicas,)), dma((replicas,)),
            dma((plan.groups,)), dma((plan.groups,)),
            dma((plan.groups,)), dma((plan.groups,)),
            dma((plan.groups, plan.blocks)), dma((plan.groups, plan.blocks)),
            dma,
            dma((half, split)), dma((half, split)),
            dma((split,)), dma((split,)),
            dma,
        ],
        compiler_params=pltpu.CompilerParams(
            collective_id=0, has_side_effects=True, vmem_limit_bytes=VMEM_GRANT
        ),
    )(*[
        pltpu.with_memory_space_constraint(x, pltpu.HBM)
        for x in (
            stay_rows, stay_count.reshape(-1), moving_rows, new_list.reshape(1, -1), centroids,
            sharpness,
        )
    ])
    fine_share = plan.fine // replicas
    whole = mass[:, :, 0, :].reshape(plan.lists, plan.fine)
    share = lax.dynamic_slice_in_dim(whole, lax.axis_index("rep") * fine_share, fine_share, 1)
    return refreshed, share


def device_program(stay_rows, stay_count, moving_rows, new_list, centroids, sharpness):
    lists_here, capacity, features = stay_rows.shape
    plan = Plan(
        lax.axis_size("owner"), lax.axis_size("rep"), lists_here, capacity, features,
        centroids.shape[1], moving_rows.shape[0],
    )
    step = (lambda *a: fused(plan, *a)) if plan.fits() else local
    return step(stay_rows, stay_count, moving_rows, new_list, centroids, sharpness)


def solution(mesh):
    in_specs = (
        P("owner", "rep", None),
        P("owner", "rep"),
        P(("owner", "rep"), None),
        P(("owner", "rep")),
        P("owner", None, None),
        P("owner"),
    )
    out_specs = (P("owner", None, None), P("owner", "rep"))
    return jax.shard_map(device_program, mesh=mesh, in_specs=in_specs, out_specs=out_specs, check_vma=False)
```

```python
import math

import jax
import jax.numpy as jnp
from jax import lax
from jax.experimental import pallas as pl
from jax.experimental.pallas import tpu as pltpu
from jax.sharding import PartitionSpec as P

SLOT_L = 2


prior_weight = 1.0


def partner(value, axis, stride):
    mask = 2**stride
    pairs = [(source, source ^ mask) for source in range(lax.axis_size(axis))]
    return lax.ppermute(value, axis, pairs)


def weigh(members, live_mask, centres, centre_norm, sharp, features):
    products = jnp.einsum("lrd,lfd->lrf", members, centres, preferred_element_type=jnp.float32)
    scores = sharp[:, None, None] * (2.0 * products - centre_norm[:, None, :]) / math.sqrt(features)
    weights = jax.nn.softmax(scores, axis=-1).astype(jnp.bfloat16) * live_mask[:, :, None]
    numerator = jnp.einsum("lrf,lrd->lfd", weights, members, preferred_element_type=jnp.float32)
    return (numerator, jnp.sum(weights.astype(jnp.float32), axis=1))


def local(stay_rows, stay_count, moving_rows, new_list, centroids, sharpness):
    owners = lax.axis_size("owner")
    replicas = lax.axis_size("rep")
    lists_here, capacity, features = stay_rows.shape
    fine_count = centroids.shape[1]
    centre_norm = jnp.sum(jnp.square(centroids.astype(jnp.float32)), axis=-1)
    outgoing_count = new_list.shape[0]
    order_index = jnp.arange(outgoing_count)
    earlier = (new_list[None, :] == new_list[:, None]) & (
        order_index[None, :] < order_index[:, None]
    )
    slot_index = jnp.sum(earlier.astype(jnp.int32), axis=1)
    local_list = new_list % lists_here
    target_owner = new_list // lists_here
    position = (local_list * owners + target_owner) * SLOT_L + slot_index
    slot_total = lists_here * owners * SLOT_L
    outgoing = (
        jnp.zeros((slot_total, features), jnp.bfloat16)
        .at[position]
        .set(moving_rows, unique_indices=True)
    )
    occupied = (
        jnp.zeros((slot_total,), jnp.bfloat16)
        .at[position]
        .set(jnp.ones((outgoing_count,), jnp.bfloat16), unique_indices=True)
    )
    arrived, present = (
        lax.all_to_all(
            outgoing.reshape(lists_here, owners, SLOT_L, features),
            "owner",
            split_axis=1,
            concat_axis=1,
            tiled=True,
        ),
        lax.all_to_all(
            occupied.reshape(lists_here, owners, SLOT_L),
            "owner",
            split_axis=1,
            concat_axis=1,
            tiled=True,
        ),
    )
    arrive_slots = owners * SLOT_L
    arrivals = arrived.reshape(lists_here, arrive_slots, features)
    present = present.reshape(lists_here, arrive_slots)
    live_count = stay_count[:, 0]
    replica = lax.axis_index("rep")
    fine_share = fine_count // replicas
    groups = max(1, replicas // lists_here)
    per_rep = max(1, lists_here // replicas)
    slot_mask = (jnp.arange(capacity)[None, :] < live_count[:, None]).astype(jnp.bfloat16)
    stay_pieces = stay_rows.reshape(lists_here * groups, capacity // groups, features)
    mask_pieces = slot_mask.reshape(lists_here * groups, capacity // groups)
    moved_stay, moved_mask = (
        lax.all_to_all(stay_pieces, "rep", split_axis=0, concat_axis=1, tiled=True),
        lax.all_to_all(mask_pieces, "rep", split_axis=0, concat_axis=1, tiled=True),
    )
    arrive_pieces = arrivals.reshape(lists_here * groups, arrive_slots // groups, features)
    present_pieces = present.reshape(lists_here * groups, arrive_slots // groups)
    moved_arrive, moved_present = (
        lax.all_to_all(arrive_pieces, "rep", split_axis=0, concat_axis=1, tiled=True),
        lax.all_to_all(present_pieces, "rep", split_axis=0, concat_axis=1, tiled=True),
    )
    members = jnp.concatenate([moved_stay, moved_arrive], axis=1)
    member_mask = jnp.concatenate([moved_mask, moved_present], axis=1)
    first_list = replica * per_rep // groups
    centres = lax.dynamic_slice_in_dim(centroids, first_list, per_rep, 0)
    norms = lax.dynamic_slice_in_dim(centre_norm, first_list, per_rep, 0)
    sharp = lax.dynamic_slice_in_dim(sharpness, first_list, per_rep, 0)
    numerator, mass_sum = weigh(members, member_mask, centres, norms, sharp, features)
    for bit_number in range(groups.bit_length() - 1):
        other_num, other_mass = partner((numerator, mass_sum), "rep", bit_number)
        numerator = numerator + other_num
        mass_sum = mass_sum + other_mass
    refreshed_all = (
        (numerator + prior_weight * centres.astype(jnp.float32))
        / (mass_sum[:, :, None] + prior_weight)
    ).astype(jnp.bfloat16)
    piece_rows = fine_count // groups
    part_index = replica % groups
    refreshed_piece = lax.dynamic_slice_in_dim(
        refreshed_all, part_index * piece_rows, piece_rows, 1
    ).reshape(per_rep * piece_rows, features)
    mass_piece = lax.dynamic_slice_in_dim(mass_sum, part_index * piece_rows, piece_rows, 1).reshape(
        per_rep * piece_rows
    )
    refreshed = lax.all_gather(refreshed_piece, "rep", axis=0, tiled=True).reshape(
        lists_here, fine_count, features
    )
    mass_whole = lax.all_gather(mass_piece, "rep", axis=0, tiled=True).reshape(
        lists_here, fine_count
    )
    return (refreshed, lax.dynamic_slice_in_dim(mass_whole, replica * fine_share, fine_share, 1))


LANES = 128
VMEM_BUDGET = 40 * 2**20
VMEM_GRANT = 48 * 2**20
MESH = pl.DeviceIdType.MESH


class Plan:
    def __init__(self, owners, replicas, lists, capacity, features, fine, moving):
        self.owners, self.replicas, self.lists = owners, replicas, lists
        self.capacity, self.features, self.fine, self.moving = capacity, features, fine, moving
        self.split = 2 if replicas % 2 == 0 and lists % 2 == 0 else 1
        self.groups = replicas // self.split
        self.half = lists // self.split
        self.per_source = self.half * SLOT_L
        self.block = self.groups * self.per_source
        self.blocks = owners * self.split
        self.width = features + LANES
        self.moving_lanes = -(-moving // LANES) * LANES

    def fits(self):
        slots = 2 * self.blocks * self.block * self.width
        held = self.half * self.replicas * self.capacity * self.features
        centres = 2 * self.half * self.fine * self.features
        gathered = self.groups * self.moving * self.features
        small = 2 * (slots + held + centres + gathered)
        return (
            small <= VMEM_BUDGET
            and self.per_source % 8 == 0
            and self.capacity % 16 == 0
            and self.moving % 16 == 0
            and self.features % LANES == 0
            and self.fine % LANES == 0
        )


def weigh_rows(plan, centres, norm, sharp, rows, mask):
    products = lax.dot_general(
        centres, rows, (((1,), (1,)), ((), ())), preferred_element_type=jnp.float32
    )
    scores = sharp * (2.0 * products - norm) / math.sqrt(plan.features)
    top = jnp.max(scores, axis=0, keepdims=True)
    raised = jnp.exp(scores - top)
    weights = (raised / jnp.sum(raised, axis=0, keepdims=True)).astype(jnp.bfloat16)
    weights = weights * mask.astype(jnp.bfloat16)
    numerator = jnp.dot(weights, rows, preferred_element_type=jnp.float32)
    mass = jnp.sum(weights.astype(jnp.float32), axis=1, keepdims=True)
    ones = jnp.ones((8, rows.shape[0]), jnp.bfloat16)
    mass_row = lax.dot_general(
        ones, weights, (((1,), (1,)), ((), ())), preferred_element_type=jnp.float32
    )
    return numerator, mass, mass_row


def fused_kernel(
    plan,
    stay_ref, count_in, moving_ref, list_in, centre_ref, sharp_in,
    out_ref, mass_ref,
    count_ref, moving_own, list_ref, sharp_ref, operand_sem, total_buf, mass_col, norm_buf,
    stay_buf, count_buf, moving_buf, pos_own, pos_buf, placed, arrived, centre_buf, result_buf, mass_buf,
    stay_send, stay_recv, count_send, count_recv, moving_send, moving_recv, pos_send, pos_recv,
    slot_send, slot_recv, centre_sem, result_send, result_recv, mass_send, mass_recv, local_sem,
):
    owners, split, groups, half = plan.owners, plan.split, plan.groups, plan.half
    replicas, capacity, features = plan.replicas, plan.capacity, plan.features
    owner = lax.axis_index("owner")
    replica = lax.axis_index("rep")
    core = replica % split
    group = replica // split

    def rep_at(k, dc):
        return lax.rem(group + k, groups) * split + lax.rem(core + dc, split)

    def owner_at(k):
        return lax.rem(owner + k, owners)

    peers = [(k, dc) for k in range(groups) for dc in range(split) if (k, dc) != (0, 0)]
    plane = [(k, dc) for k in range(1, owners) for dc in range(split)]
    barrier = pltpu.get_barrier_semaphore()
    for k, dc in peers:
        pl.semaphore_signal(barrier, inc=1, device_id=(owner, rep_at(k, dc)), device_id_type=MESH)
    for k, dc in plane:
        pl.semaphore_signal(
            barrier, inc=1, device_id=(owner_at(k), rep_at(0, dc)), device_id_type=MESH
        )

    small = [
        pltpu.make_async_copy(source, held, operand_sem.at[i])
        for i, (source, held) in enumerate([
            (list_in, list_ref), (count_in, count_ref), (moving_ref, moving_own), (sharp_in, sharp_ref),
        ])
    ]
    for copy in small:
        copy.start()
    centre_copy = pltpu.make_async_copy(
        centre_ref.at[pl.ds(core * half, half)], centre_buf, centre_sem
    )
    centre_copy.start()

    def own_copy(j):
        return pltpu.make_async_copy(
            stay_ref.at[core * half + j], stay_buf.at[j, 0], stay_recv.at[j, 0]
        )

    for j in range(half):
        own_copy(j).start()

    pl.semaphore_wait(barrier, len(peers) + len(plane))

    def moving_copy(k):
        return pltpu.make_async_remote_copy(
            src_ref=moving_ref, dst_ref=moving_buf.at[k - 1],
            send_sem=moving_send.at[k - 1], recv_sem=moving_recv.at[k - 1],
            device_id=(owner, rep_at(k, 0)), device_id_type=MESH,
        )

    def pos_copy(k):
        return pltpu.make_async_remote_copy(
            src_ref=pos_own, dst_ref=pos_buf.at[k - 1],
            send_sem=pos_send.at[k - 1], recv_sem=pos_recv.at[k - 1],
            device_id=(owner, rep_at(k, 0)), device_id_type=MESH,
        )

    for k in range(1, groups):
        moving_copy(k).start()

    def count_copy(k, dc):
        q = k * split + dc
        return pltpu.make_async_remote_copy(
            src_ref=count_buf.at[0], dst_ref=count_buf.at[q],
            send_sem=count_send.at[q], recv_sem=count_recv.at[q],
            device_id=(owner, rep_at(k, dc)), device_id_type=MESH,
        )

    def stay_copy(j, k, dc):
        q = k * split + dc
        return pltpu.make_async_remote_copy(
            src_ref=stay_ref.at[lax.rem(core + dc, split) * half + j], dst_ref=stay_buf.at[j, q],
            send_sem=stay_send.at[j, q], recv_sem=stay_recv.at[j, q],
            device_id=(owner, rep_at(k, dc)), device_id_type=MESH,
        )

    siblings = [(k, dc) for k, dc in peers if k == 0]
    distant = [(k, dc) for k, dc in peers if k > 0]
    ahead = min(len(distant) + 1, half * len(distant))
    if distant:
        stay_copy(0, *distant[0]).start()
    for j in range(half):
        for k, dc in siblings:
            stay_copy(j, k, dc).start()

    moving = plan.moving
    small[0].wait()
    small[1].wait()
    line = lax.broadcasted_iota(jnp.int32, count_buf.shape[1:], 0)
    live = jnp.zeros(count_buf.shape[1:], jnp.int32)
    for i in range(plan.lists):
        live = jnp.where(line == i, count_ref[i], live)
    count_buf[0] = live
    names = jnp.broadcast_to(list_ref[...], (moving, moving))
    row = lax.broadcasted_iota(jnp.int32, (moving, moving), 0)
    column = lax.broadcasted_iota(jnp.int32, (moving, moving), 1)
    down = jnp.sum(jnp.where(row == column, names, 0), axis=1, keepdims=True)
    earlier = jnp.where((names == down) & (row < column), 1, 0)
    slot = jnp.sum(earlier, axis=0, keepdims=True)
    target = list_ref[...]
    position = (
        (target // half) * plan.per_source + (target % half) * SLOT_L + slot
    )
    pos_own[...] = jnp.full(pos_own.shape, -1, jnp.int32)
    pos_own[:, :moving] = jnp.broadcast_to(position, (8, moving))
    for k in range(1, groups):
        pos_copy(k).start()
    for k, dc in peers:
        count_copy(k, dc).start()
    small[2].wait()
    small[3].wait()

    sent = [(k, dc) for k in range(owners) for dc in range(split) if (k, dc) != (0, 0)]
    slots = plan.blocks * plan.per_source
    slot_row = lax.broadcasted_iota(jnp.int32, (slots, moving), 0)
    ones = jnp.ones((moving, LANES), jnp.bfloat16)

    def slot_copy(g, k, dc):
        b = k * split + dc
        return pltpu.make_async_remote_copy(
            src_ref=placed.at[g, owner_at(k) * split + lax.rem(core + dc, split)],
            dst_ref=arrived.at[g, b],
            send_sem=slot_send.at[g, b], recv_sem=slot_recv.at[g, b],
            device_id=(owner_at(k), rep_at(0, dc)), device_id_type=MESH,
        )

    def place_group(g, positions, source):
        pick = jnp.where(slot_row == positions, 1.0, 0.0).astype(jnp.bfloat16)
        rows = jnp.dot(pick, source, preferred_element_type=jnp.float32)
        flags = jnp.dot(pick, ones, preferred_element_type=jnp.float32)
        shape = (plan.blocks, plan.per_source)
        placed[g, :, :, :features] = rows.reshape(*shape, features).astype(jnp.bfloat16)
        placed[g, :, :, features:] = flags.reshape(*shape, LANES).astype(jnp.bfloat16)
        for k, dc in sent:
            slot_copy(g, k, dc).start()
        arrived[g, 0] = placed[g, owner * split + core]

    place_group(0, pos_own[0:1, :moving], moving_own[...])
    for i in range(1, ahead):
        j, place = divmod(i, len(distant))
        stay_copy(j, *distant[place]).start()
    for k in range(1, groups):
        pos_copy(k).wait_recv()
        moving_copy(k).wait_recv()
        place_group(k, pos_buf[k - 1, 0:1, :moving], moving_buf[k - 1])
    total = groups * slots
    centre_copy.wait()
    for j in range(half):
        wide = centre_buf[j].astype(jnp.float32)
        norm_buf[j] = jnp.broadcast_to(
            jnp.sum(wide * wide, axis=1, keepdims=True), norm_buf.shape[1:]
        )
    for k, dc in peers:
        count_copy(k, dc).wait_recv()

    arrived_lane = lax.broadcasted_iota(jnp.int32, (1, total), 1)
    arrived_list = (arrived_lane % plan.per_source) // SLOT_L

    def result_copy(j, dc):
        return pltpu.make_async_remote_copy(
            src_ref=result_buf.at[j], dst_ref=out_ref.at[core * half + j],
            send_sem=result_send.at[j, dc], recv_sem=result_recv.at[j, dc],
            device_id=(owner, rep_at(0, dc)), device_id_type=MESH,
        )

    def result_own(j):
        return pltpu.make_async_copy(
            result_buf.at[j], out_ref.at[core * half + j], result_recv.at[j, 0]
        )

    def add_part(j, rows, mask):
        num, mass, mass_row = weigh_rows(
            plan, centre_buf[j], norm_buf[j][:, 0:1], sharp_ref[core * half + j], rows, mask
        )
        total_buf[j] += num
        mass_col[j] += jnp.broadcast_to(mass, mass_col.shape[1:])
        mass_buf[j] += mass_row

    def add_stay(j, first, last):
        lane = lax.broadcasted_iota(jnp.int32, (1, (last - first) * capacity), 1)
        counts = jnp.zeros(lane.shape, jnp.int32)
        for q in range(first, last):
            counts = jnp.where(
                lane // capacity == q - first,
                count_buf[q, pl.ds(core * half + j, 1), :][:, : lane.shape[1]], counts,
            )
        mask = jnp.where(lane % capacity < counts, 1.0, 0.0)
        members = stay_buf[j, first:last].reshape((last - first) * capacity, features)
        add_part(j, members, mask)

    def add_arrivals():
        fine = plan.fine
        rows = arrived[:, :, :, :features].reshape(total, features)
        marks = arrived[:, :, :, features:].reshape(total, LANES)
        spread = jnp.full((8, LANES), 1.0 / LANES, jnp.bfloat16)
        present = lax.dot_general(
            spread, marks, (((1,), (1,)), ((), ())), preferred_element_type=jnp.float32
        )[0:1]
        products = lax.dot_general(
            centre_buf[...].reshape(half * fine, features), rows, (((1,), (1,)), ((), ())),
            preferred_element_type=jnp.float32,
        )
        parts = []
        for j in range(half):
            own = products[j * fine : (j + 1) * fine]
            sharp = sharp_ref[core * half + j]
            scores = sharp * (2.0 * own - norm_buf[j][:, 0:1]) / math.sqrt(features)
            raised = jnp.exp(scores - jnp.max(scores, axis=0, keepdims=True))
            weights = (raised / jnp.sum(raised, axis=0, keepdims=True)).astype(jnp.bfloat16)
            here = jnp.where(arrived_list == j, present, 0.0)
            weights = weights * here.astype(jnp.bfloat16)
            mass = jnp.sum(weights.astype(jnp.float32), axis=1, keepdims=True)
            mass_col[j] += jnp.broadcast_to(mass, mass_col.shape[1:])
            parts.append(weights)
        stacked = jnp.concatenate(parts, axis=0)
        ones = jnp.ones((8, total), jnp.bfloat16)
        mass_row = lax.dot_general(
            ones, stacked, (((1,), (1,)), ((), ())), preferred_element_type=jnp.float32
        )
        numerator = jnp.dot(stacked, rows, preferred_element_type=jnp.float32)
        for j in range(half):
            mass_buf[j] += mass_row[:, j * fine : (j + 1) * fine]
            total_buf[j] += numerator[j * fine : (j + 1) * fine]

    def add_near(j):
        total_buf[j] = prior_weight * centre_buf[j].astype(jnp.float32)
        mass_col[j] = jnp.zeros(mass_col.shape[1:], jnp.float32)
        mass_buf[j] = jnp.zeros(mass_buf.shape[1:], jnp.float32)
        own_copy(j).wait()
        for k, dc in siblings:
            stay_copy(j, k, dc).wait_recv()
        add_stay(j, 0, split)

    def pass_on(j):
        for i, (k, dc) in enumerate(distant):
            stay_copy(j, k, dc).wait_send()
            step, place = divmod(i + ahead, len(distant))

            @pl.when(j + step < half)
            def _():
                stay_copy(j + step, *distant[place]).start()

    def add_far(j):
        for k, dc in distant:
            stay_copy(j, k, dc).wait_recv()
        if groups > 1:
            add_stay(j, split, replicas)

    def finish(j):
        share = 1.0 / (mass_col[j][:, 0:1] + prior_weight)
        result_buf[j] = (total_buf[j] * share).astype(jnp.bfloat16)
        result_own(j).start()
        for dc in range(1, split):
            result_copy(j, dc).start()

    def early(j, carry):
        add_near(j)
        pass_on(j)
        add_far(j)
        return carry

    def settle(j, carry):
        finish(j)
        return carry

    last = half - 1
    lax.fori_loop(0, last, early, 0)
    add_near(last)
    for g in range(groups):
        for k, dc in sent:
            slot_copy(g, k, dc).wait_recv()
    add_arrivals()
    lax.fori_loop(0, last, settle, 0)
    add_far(last)
    finish(last)

    def mass_copy(dc):
        return pltpu.make_async_remote_copy(
            src_ref=mass_buf, dst_ref=mass_ref.at[core],
            send_sem=mass_send.at[dc], recv_sem=mass_recv.at[dc],
            device_id=(owner, rep_at(0, dc)), device_id_type=MESH,
        )

    mass_own = pltpu.make_async_copy(mass_buf, mass_ref.at[core], local_sem)
    mass_own.start()
    for dc in range(1, split):
        mass_copy(dc).start()

    for k in range(1, groups):
        pos_copy(k).wait_send()
        moving_copy(k).wait_send()
    for k, dc in peers:
        count_copy(k, dc).wait_send()
    for k, dc in distant:
        stay_copy(last, k, dc).wait_send()
    for j in range(half):
        for k, dc in siblings:
            stay_copy(j, k, dc).wait_send()
    for g in range(groups):
        for k, dc in sent:
            slot_copy(g, k, dc).wait_send()
    for j in range(half):
        result_own(j).wait()
        for dc in range(1, split):
            result_copy(j, dc).wait()
    mass_own.wait()
    for dc in range(1, split):
        mass_copy(dc).wait()


def fused(plan, stay_rows, stay_count, moving_rows, new_list, centroids, sharpness):
    half, split, replicas = plan.half, plan.split, plan.replicas
    any_space = pl.BlockSpec(memory_space=pl.ANY)
    dma = pltpu.SemaphoreType.DMA
    members = replicas * plan.capacity
    refreshed, mass = pl.pallas_call(
        lambda *refs: fused_kernel(plan, *refs),
        out_shape=(
            pltpu.VMEM(centroids.shape, jnp.bfloat16),
            pltpu.VMEM((split, half, 8, plan.fine), jnp.float32),
        ),
        in_specs=[pl.BlockSpec(memory_space=pltpu.HBM)] * 6,
        out_specs=(any_space, any_space),
        scratch_shapes=[
            pltpu.SMEM((plan.lists,), jnp.int32),
            pltpu.VMEM((plan.moving, plan.features), jnp.bfloat16),
            pltpu.VMEM((1, plan.moving), jnp.int32),
            pltpu.SMEM((plan.lists,), jnp.float32),
            dma((4,)),
            pltpu.VMEM((half, plan.fine, plan.features), jnp.float32),
            pltpu.VMEM((half, plan.fine, LANES), jnp.float32),
            pltpu.VMEM((half, plan.fine, LANES), jnp.float32),
            pltpu.VMEM((half, replicas, plan.capacity, plan.features), jnp.bfloat16),
            pltpu.VMEM((replicas, plan.lists, members), jnp.int32),
            pltpu.VMEM((max(1, plan.groups - 1), plan.moving, plan.features), jnp.bfloat16),
            pltpu.VMEM((8, plan.moving_lanes), jnp.int32),
            pltpu.VMEM((max(1, plan.groups - 1), 8, plan.moving_lanes), jnp.int32),
            pltpu.VMEM((plan.groups, plan.blocks, plan.per_source, plan.width), jnp.bfloat16),
            pltpu.VMEM((plan.groups, plan.blocks, plan.per_source, plan.width), jnp.bfloat16),
            pltpu.VMEM((half, plan.fine, plan.features), jnp.bfloat16),
            pltpu.VMEM((half, plan.fine, plan.features), jnp.bfloat16),
            pltpu.VMEM((half, 8, plan.fine), jnp.float32),
            dma((half, replicas)), dma((half, replicas)),
            dma((replicas,)), dma((replicas,)),
            dma((plan.groups,)), dma((plan.groups,)),
            dma((plan.groups,)), dma((plan.groups,)),
            dma((plan.groups, plan.blocks)), dma((plan.groups, plan.blocks)),
            dma,
            dma((half, split)), dma((half, split)),
            dma((split,)), dma((split,)),
            dma,
        ],
        compiler_params=pltpu.CompilerParams(
            collective_id=0, has_side_effects=True, vmem_limit_bytes=VMEM_GRANT
        ),
    )(*[
        pltpu.with_memory_space_constraint(x, pltpu.HBM)
        for x in (
            stay_rows, stay_count.reshape(-1), moving_rows, new_list.reshape(1, -1), centroids,
            sharpness,
        )
    ])
    fine_share = plan.fine // replicas
    whole = mass[:, :, 0, :].reshape(plan.lists, plan.fine)
    share = lax.dynamic_slice_in_dim(whole, lax.axis_index("rep") * fine_share, fine_share, 1)
    return refreshed, share


def device_program(stay_rows, stay_count, moving_rows, new_list, centroids, sharpness):
    lists_here, capacity, features = stay_rows.shape
    plan = Plan(
        lax.axis_size("owner"), lax.axis_size("rep"), lists_here, capacity, features,
        centroids.shape[1], moving_rows.shape[0],
    )
    step = (lambda *a: fused(plan, *a)) if plan.fits() else local
    return step(stay_rows, stay_count, moving_rows, new_list, centroids, sharpness)


def solution(mesh):
    in_specs = (
        P("owner", "rep", None),
        P("owner", "rep"),
        P(("owner", "rep"), None),
        P(("owner", "rep")),
        P("owner", None, None),
        P("owner"),
    )
    out_specs = (P("owner", None, None), P("owner", "rep"))
    return jax.shard_map(device_program, mesh=mesh, in_specs=in_specs, out_specs=out_specs, check_vma=False)
```

```python
import math

import jax
import jax.numpy as jnp
from jax import lax
from jax.experimental import pallas as pl
from jax.experimental.pallas import tpu as pltpu
from jax.sharding import PartitionSpec as P

SLOT_L = 2


prior_weight = 1.0


def partner(value, axis, stride):
    mask = 2**stride
    pairs = [(source, source ^ mask) for source in range(lax.axis_size(axis))]
    return lax.ppermute(value, axis, pairs)


def weigh(members, live_mask, centres, centre_norm, sharp, features):
    products = jnp.einsum("lrd,lfd->lrf", members, centres, preferred_element_type=jnp.float32)
    scores = sharp[:, None, None] * (2.0 * products - centre_norm[:, None, :]) / math.sqrt(features)
    weights = jax.nn.softmax(scores, axis=-1).astype(jnp.bfloat16) * live_mask[:, :, None]
    numerator = jnp.einsum("lrf,lrd->lfd", weights, members, preferred_element_type=jnp.float32)
    return (numerator, jnp.sum(weights.astype(jnp.float32), axis=1))


def local(stay_rows, stay_count, moving_rows, new_list, centroids, sharpness):
    owners = lax.axis_size("owner")
    replicas = lax.axis_size("rep")
    lists_here, capacity, features = stay_rows.shape
    fine_count = centroids.shape[1]
    centre_norm = jnp.sum(jnp.square(centroids.astype(jnp.float32)), axis=-1)
    outgoing_count = new_list.shape[0]
    order_index = jnp.arange(outgoing_count)
    earlier = (new_list[None, :] == new_list[:, None]) & (
        order_index[None, :] < order_index[:, None]
    )
    slot_index = jnp.sum(earlier.astype(jnp.int32), axis=1)
    local_list = new_list % lists_here
    target_owner = new_list // lists_here
    position = (local_list * owners + target_owner) * SLOT_L + slot_index
    slot_total = lists_here * owners * SLOT_L
    outgoing = (
        jnp.zeros((slot_total, features), jnp.bfloat16)
        .at[position]
        .set(moving_rows, unique_indices=True)
    )
    occupied = (
        jnp.zeros((slot_total,), jnp.bfloat16)
        .at[position]
        .set(jnp.ones((outgoing_count,), jnp.bfloat16), unique_indices=True)
    )
    arrived, present = (
        lax.all_to_all(
            outgoing.reshape(lists_here, owners, SLOT_L, features),
            "owner",
            split_axis=1,
            concat_axis=1,
            tiled=True,
        ),
        lax.all_to_all(
            occupied.reshape(lists_here, owners, SLOT_L),
            "owner",
            split_axis=1,
            concat_axis=1,
            tiled=True,
        ),
    )
    arrive_slots = owners * SLOT_L
    arrivals = arrived.reshape(lists_here, arrive_slots, features)
    present = present.reshape(lists_here, arrive_slots)
    live_count = stay_count[:, 0]
    replica = lax.axis_index("rep")
    fine_share = fine_count // replicas
    groups = max(1, replicas // lists_here)
    per_rep = max(1, lists_here // replicas)
    slot_mask = (jnp.arange(capacity)[None, :] < live_count[:, None]).astype(jnp.bfloat16)
    stay_pieces = stay_rows.reshape(lists_here * groups, capacity // groups, features)
    mask_pieces = slot_mask.reshape(lists_here * groups, capacity // groups)
    moved_stay, moved_mask = (
        lax.all_to_all(stay_pieces, "rep", split_axis=0, concat_axis=1, tiled=True),
        lax.all_to_all(mask_pieces, "rep", split_axis=0, concat_axis=1, tiled=True),
    )
    arrive_pieces = arrivals.reshape(lists_here * groups, arrive_slots // groups, features)
    present_pieces = present.reshape(lists_here * groups, arrive_slots // groups)
    moved_arrive, moved_present = (
        lax.all_to_all(arrive_pieces, "rep", split_axis=0, concat_axis=1, tiled=True),
        lax.all_to_all(present_pieces, "rep", split_axis=0, concat_axis=1, tiled=True),
    )
    members = jnp.concatenate([moved_stay, moved_arrive], axis=1)
    member_mask = jnp.concatenate([moved_mask, moved_present], axis=1)
    first_list = replica * per_rep // groups
    centres = lax.dynamic_slice_in_dim(centroids, first_list, per_rep, 0)
    norms = lax.dynamic_slice_in_dim(centre_norm, first_list, per_rep, 0)
    sharp = lax.dynamic_slice_in_dim(sharpness, first_list, per_rep, 0)
    numerator, mass_sum = weigh(members, member_mask, centres, norms, sharp, features)
    for bit_number in range(groups.bit_length() - 1):
        other_num, other_mass = partner((numerator, mass_sum), "rep", bit_number)
        numerator = numerator + other_num
        mass_sum = mass_sum + other_mass
    refreshed_all = (
        (numerator + prior_weight * centres.astype(jnp.float32))
        / (mass_sum[:, :, None] + prior_weight)
    ).astype(jnp.bfloat16)
    piece_rows = fine_count // groups
    part_index = replica % groups
    refreshed_piece = lax.dynamic_slice_in_dim(
        refreshed_all, part_index * piece_rows, piece_rows, 1
    ).reshape(per_rep * piece_rows, features)
    mass_piece = lax.dynamic_slice_in_dim(mass_sum, part_index * piece_rows, piece_rows, 1).reshape(
        per_rep * piece_rows
    )
    refreshed = lax.all_gather(refreshed_piece, "rep", axis=0, tiled=True).reshape(
        lists_here, fine_count, features
    )
    mass_whole = lax.all_gather(mass_piece, "rep", axis=0, tiled=True).reshape(
        lists_here, fine_count
    )
    return (refreshed, lax.dynamic_slice_in_dim(mass_whole, replica * fine_share, fine_share, 1))


LANES = 128
VMEM_BUDGET = 40 * 2**20
VMEM_GRANT = 48 * 2**20
MESH = pl.DeviceIdType.MESH


class Plan:
    def __init__(self, owners, replicas, lists, capacity, features, fine, moving):
        self.owners, self.replicas, self.lists = owners, replicas, lists
        self.capacity, self.features, self.fine, self.moving = capacity, features, fine, moving
        self.split = 2 if replicas % 2 == 0 and lists % 2 == 0 else 1
        self.groups = replicas // self.split
        self.half = lists // self.split
        self.per_source = self.half * SLOT_L
        self.block = self.groups * self.per_source
        self.blocks = owners * self.split
        self.width = features + LANES
        self.moving_lanes = -(-moving // LANES) * LANES

    def fits(self):
        slots = 2 * self.blocks * self.block * self.width
        held = self.half * self.replicas * self.capacity * self.features
        centres = 2 * self.half * self.fine * self.features
        gathered = self.groups * self.moving * self.features
        small = 2 * (slots + held + centres + gathered)
        return (
            small <= VMEM_BUDGET
            and self.per_source % 8 == 0
            and self.capacity % 16 == 0
            and self.moving % 16 == 0
            and self.features % LANES == 0
            and self.fine % LANES == 0
        )


def weigh_rows(plan, centres, norm, sharp, rows, mask):
    products = lax.dot_general(
        centres, rows, (((1,), (1,)), ((), ())), preferred_element_type=jnp.float32
    )
    scores = sharp * (2.0 * products - norm) / math.sqrt(plan.features)
    top = jnp.max(scores, axis=0, keepdims=True)
    raised = jnp.exp(scores - top)
    weights = (raised / jnp.sum(raised, axis=0, keepdims=True)).astype(jnp.bfloat16)
    weights = weights * mask.astype(jnp.bfloat16)
    numerator = jnp.dot(weights, rows, preferred_element_type=jnp.float32)
    mass = jnp.sum(weights.astype(jnp.float32), axis=1, keepdims=True)
    ones = jnp.ones((8, rows.shape[0]), jnp.bfloat16)
    mass_row = lax.dot_general(
        ones, weights, (((1,), (1,)), ((), ())), preferred_element_type=jnp.float32
    )
    return numerator, mass, mass_row


def fused_kernel(
    plan,
    stay_ref, count_in, moving_ref, list_in, centre_ref, sharp_in,
    out_ref, mass_ref,
    count_ref, moving_own, list_ref, sharp_ref, operand_sem, total_buf, mass_col, norm_buf,
    stay_buf, count_buf, moving_buf, pos_own, pos_buf, placed, arrived, centre_buf, result_buf, mass_buf,
    stay_send, stay_recv, count_send, count_recv, moving_send, moving_recv, pos_send, pos_recv,
    slot_send, slot_recv, centre_sem, result_send, result_recv, mass_send, mass_recv, local_sem,
):
    owners, split, groups, half = plan.owners, plan.split, plan.groups, plan.half
    replicas, capacity, features = plan.replicas, plan.capacity, plan.features
    owner = lax.axis_index("owner")
    replica = lax.axis_index("rep")
    core = replica % split
    group = replica // split

    def rep_at(k, dc):
        return lax.rem(group + k, groups) * split + lax.rem(core + dc, split)

    def owner_at(k):
        return lax.rem(owner + k, owners)

    peers = [(k, dc) for k in range(groups) for dc in range(split) if (k, dc) != (0, 0)]
    plane = [(k, dc) for k in range(1, owners) for dc in range(split)]
    barrier = pltpu.get_barrier_semaphore()
    for k, dc in peers:
        pl.semaphore_signal(barrier, inc=1, device_id=(owner, rep_at(k, dc)), device_id_type=MESH)
    for k, dc in plane:
        pl.semaphore_signal(
            barrier, inc=1, device_id=(owner_at(k), rep_at(0, dc)), device_id_type=MESH
        )

    small = [
        pltpu.make_async_copy(source, held, operand_sem.at[i])
        for i, (source, held) in enumerate([
            (list_in, list_ref), (count_in, count_ref), (moving_ref, moving_own), (sharp_in, sharp_ref),
        ])
    ]
    for copy in small:
        copy.start()
    centre_copy = pltpu.make_async_copy(
        centre_ref.at[pl.ds(core * half, half)], centre_buf, centre_sem
    )
    centre_copy.start()

    def own_copy(j):
        return pltpu.make_async_copy(
            stay_ref.at[core * half + j], stay_buf.at[j, 0], stay_recv.at[j, 0]
        )

    for j in range(half):
        own_copy(j).start()

    pl.semaphore_wait(barrier, len(peers) + len(plane))

    def moving_copy(k):
        return pltpu.make_async_remote_copy(
            src_ref=moving_ref, dst_ref=moving_buf.at[k - 1],
            send_sem=moving_send.at[k - 1], recv_sem=moving_recv.at[k - 1],
            device_id=(owner, rep_at(k, 0)), device_id_type=MESH,
        )

    def pos_copy(k):
        return pltpu.make_async_remote_copy(
            src_ref=pos_own, dst_ref=pos_buf.at[k - 1],
            send_sem=pos_send.at[k - 1], recv_sem=pos_recv.at[k - 1],
            device_id=(owner, rep_at(k, 0)), device_id_type=MESH,
        )

    for k in range(1, groups):
        moving_copy(k).start()

    def count_copy(k, dc):
        q = k * split + dc
        return pltpu.make_async_remote_copy(
            src_ref=count_buf.at[0], dst_ref=count_buf.at[q],
            send_sem=count_send.at[q], recv_sem=count_recv.at[q],
            device_id=(owner, rep_at(k, dc)), device_id_type=MESH,
        )

    def stay_copy(j, k, dc):
        q = k * split + dc
        return pltpu.make_async_remote_copy(
            src_ref=stay_ref.at[lax.rem(core + dc, split) * half + j], dst_ref=stay_buf.at[j, q],
            send_sem=stay_send.at[j, q], recv_sem=stay_recv.at[j, q],
            device_id=(owner, rep_at(k, dc)), device_id_type=MESH,
        )

    siblings = [(k, dc) for k, dc in peers if k == 0]
    distant = [(k, dc) for k, dc in peers if k > 0]
    ahead = min(len(distant) + 1, half * len(distant))
    if distant:
        stay_copy(0, *distant[0]).start()

    moving = plan.moving
    small[0].wait()
    small[1].wait()
    line = lax.broadcasted_iota(jnp.int32, count_buf.shape[1:], 0)
    live = jnp.zeros(count_buf.shape[1:], jnp.int32)
    for i in range(plan.lists):
        live = jnp.where(line == i, count_ref[i], live)
    count_buf[0] = live
    names = jnp.broadcast_to(list_ref[...], (moving, moving))
    row = lax.broadcasted_iota(jnp.int32, (moving, moving), 0)
    column = lax.broadcasted_iota(jnp.int32, (moving, moving), 1)
    down = jnp.sum(jnp.where(row == column, names, 0), axis=1, keepdims=True)
    earlier = jnp.where((names == down) & (row < column), 1, 0)
    slot = jnp.sum(earlier, axis=0, keepdims=True)
    target = list_ref[...]
    position = (
        (target // half) * plan.per_source + (target % half) * SLOT_L + slot
    )
    pos_own[...] = jnp.full(pos_own.shape, -1, jnp.int32)
    pos_own[:, :moving] = jnp.broadcast_to(position, (8, moving))
    for k in range(1, groups):
        pos_copy(k).start()
    for k, dc in peers:
        count_copy(k, dc).start()
    small[2].wait()
    small[3].wait()

    sent = [(k, dc) for k in range(owners) for dc in range(split) if (k, dc) != (0, 0)]
    slots = plan.blocks * plan.per_source
    slot_row = lax.broadcasted_iota(jnp.int32, (slots, moving), 0)
    ones = jnp.ones((moving, LANES), jnp.bfloat16)

    def slot_copy(g, k, dc):
        b = k * split + dc
        return pltpu.make_async_remote_copy(
            src_ref=placed.at[g, owner_at(k) * split + lax.rem(core + dc, split)],
            dst_ref=arrived.at[g, b],
            send_sem=slot_send.at[g, b], recv_sem=slot_recv.at[g, b],
            device_id=(owner_at(k), rep_at(0, dc)), device_id_type=MESH,
        )

    def place_group(g, positions, source):
        pick = jnp.where(slot_row == positions, 1.0, 0.0).astype(jnp.bfloat16)
        rows = jnp.dot(pick, source, preferred_element_type=jnp.float32)
        flags = jnp.dot(pick, ones, preferred_element_type=jnp.float32)
        shape = (plan.blocks, plan.per_source)
        placed[g, :, :, :features] = rows.reshape(*shape, features).astype(jnp.bfloat16)
        placed[g, :, :, features:] = flags.reshape(*shape, LANES).astype(jnp.bfloat16)
        for k, dc in sent:
            slot_copy(g, k, dc).start()
        arrived[g, 0] = placed[g, owner * split + core]

    place_group(0, pos_own[0:1, :moving], moving_own[...])
    for i in range(1, ahead):
        j, place = divmod(i, len(distant))
        stay_copy(j, *distant[place]).start()
    for k in range(1, groups):
        pos_copy(k).wait_recv()
        moving_copy(k).wait_recv()
        place_group(k, pos_buf[k - 1, 0:1, :moving], moving_buf[k - 1])
    for j in range(half):
        for k, dc in siblings:
            stay_copy(j, k, dc).start()
    total = groups * slots
    centre_copy.wait()
    for j in range(half):
        wide = centre_buf[j].astype(jnp.float32)
        norm_buf[j] = jnp.broadcast_to(
            jnp.sum(wide * wide, axis=1, keepdims=True), norm_buf.shape[1:]
        )
    for k, dc in peers:
        count_copy(k, dc).wait_recv()

    arrived_lane = lax.broadcasted_iota(jnp.int32, (1, total), 1)
    arrived_list = (arrived_lane % plan.per_source) // SLOT_L

    def result_copy(j, dc):
        return pltpu.make_async_remote_copy(
            src_ref=result_buf.at[j], dst_ref=out_ref.at[core * half + j],
            send_sem=result_send.at[j, dc], recv_sem=result_recv.at[j, dc],
            device_id=(owner, rep_at(0, dc)), device_id_type=MESH,
        )

    def result_own(j):
        return pltpu.make_async_copy(
            result_buf.at[j], out_ref.at[core * half + j], result_recv.at[j, 0]
        )

    def add_part(j, rows, mask):
        num, mass, mass_row = weigh_rows(
            plan, centre_buf[j], norm_buf[j][:, 0:1], sharp_ref[core * half + j], rows, mask
        )
        total_buf[j] += num
        mass_col[j] += jnp.broadcast_to(mass, mass_col.shape[1:])
        mass_buf[j] += mass_row

    def add_stay(j, first, last):
        lane = lax.broadcasted_iota(jnp.int32, (1, (last - first) * capacity), 1)
        counts = jnp.zeros(lane.shape, jnp.int32)
        for q in range(first, last):
            counts = jnp.where(
                lane // capacity == q - first,
                count_buf[q, pl.ds(core * half + j, 1), :][:, : lane.shape[1]], counts,
            )
        mask = jnp.where(lane % capacity < counts, 1.0, 0.0)
        members = stay_buf[j, first:last].reshape((last - first) * capacity, features)
        add_part(j, members, mask)

    def add_arrivals():
        fine = plan.fine
        rows = arrived[:, :, :, :features].reshape(total, features)
        marks = arrived[:, :, :, features:].reshape(total, LANES)
        spread = jnp.full((8, LANES), 1.0 / LANES, jnp.bfloat16)
        present = lax.dot_general(
            spread, marks, (((1,), (1,)), ((), ())), preferred_element_type=jnp.float32
        )[0:1]
        products = lax.dot_general(
            centre_buf[...].reshape(half * fine, features), rows, (((1,), (1,)), ((), ())),
            preferred_element_type=jnp.float32,
        )
        parts = []
        for j in range(half):
            own = products[j * fine : (j + 1) * fine]
            sharp = sharp_ref[core * half + j]
            scores = sharp * (2.0 * own - norm_buf[j][:, 0:1]) / math.sqrt(features)
            raised = jnp.exp(scores - jnp.max(scores, axis=0, keepdims=True))
            weights = (raised / jnp.sum(raised, axis=0, keepdims=True)).astype(jnp.bfloat16)
            here = jnp.where(arrived_list == j, present, 0.0)
            weights = weights * here.astype(jnp.bfloat16)
            mass = jnp.sum(weights.astype(jnp.float32), axis=1, keepdims=True)
            mass_col[j] += jnp.broadcast_to(mass, mass_col.shape[1:])
            parts.append(weights)
        stacked = jnp.concatenate(parts, axis=0)
        ones = jnp.ones((8, total), jnp.bfloat16)
        mass_row = lax.dot_general(
            ones, stacked, (((1,), (1,)), ((), ())), preferred_element_type=jnp.float32
        )
        numerator = jnp.dot(stacked, rows, preferred_element_type=jnp.float32)
        for j in range(half):
            mass_buf[j] += mass_row[:, j * fine : (j + 1) * fine]
            total_buf[j] += numerator[j * fine : (j + 1) * fine]

    def add_near(j):
        total_buf[j] = prior_weight * centre_buf[j].astype(jnp.float32)
        mass_col[j] = jnp.zeros(mass_col.shape[1:], jnp.float32)
        mass_buf[j] = jnp.zeros(mass_buf.shape[1:], jnp.float32)
        own_copy(j).wait()
        for k, dc in siblings:
            stay_copy(j, k, dc).wait_recv()
        add_stay(j, 0, split)

    def pass_on(j):
        for i, (k, dc) in enumerate(distant):
            stay_copy(j, k, dc).wait_send()
            step, place = divmod(i + ahead, len(distant))

            @pl.when(j + step < half)
            def _():
                stay_copy(j + step, *distant[place]).start()

    def add_far(j):
        for k, dc in distant:
            stay_copy(j, k, dc).wait_recv()
        if groups > 1:
            add_stay(j, split, replicas)

    def finish(j):
        share = 1.0 / (mass_col[j][:, 0:1] + prior_weight)
        result_buf[j] = (total_buf[j] * share).astype(jnp.bfloat16)
        result_own(j).start()
        for dc in range(1, split):
            result_copy(j, dc).start()

    def early(j, carry):
        add_near(j)
        pass_on(j)
        add_far(j)
        return carry

    def settle(j, carry):
        finish(j)
        return carry

    last = half - 1
    lax.fori_loop(0, last, early, 0)
    add_near(last)
    for g in range(groups):
        for k, dc in sent:
            slot_copy(g, k, dc).wait_recv()
    add_arrivals()
    lax.fori_loop(0, last, settle, 0)
    for k, dc in distant:
        stay_copy(last, k, dc).wait_recv()
        add_stay(last, k * split + dc, k * split + dc + 1)
    finish(last)

    def mass_copy(dc):
        return pltpu.make_async_remote_copy(
            src_ref=mass_buf, dst_ref=mass_ref.at[core],
            send_sem=mass_send.at[dc], recv_sem=mass_recv.at[dc],
            device_id=(owner, rep_at(0, dc)), device_id_type=MESH,
        )

    mass_own = pltpu.make_async_copy(mass_buf, mass_ref.at[core], local_sem)
    mass_own.start()
    for dc in range(1, split):
        mass_copy(dc).start()

    for k in range(1, groups):
        pos_copy(k).wait_send()
        moving_copy(k).wait_send()
    for k, dc in peers:
        count_copy(k, dc).wait_send()
    for k, dc in distant:
        stay_copy(last, k, dc).wait_send()
    for j in range(half):
        for k, dc in siblings:
            stay_copy(j, k, dc).wait_send()
    for g in range(groups):
        for k, dc in sent:
            slot_copy(g, k, dc).wait_send()
    for j in range(half):
        result_own(j).wait()
        for dc in range(1, split):
            result_copy(j, dc).wait()
    mass_own.wait()
    for dc in range(1, split):
        mass_copy(dc).wait()


def fused(plan, stay_rows, stay_count, moving_rows, new_list, centroids, sharpness):
    half, split, replicas = plan.half, plan.split, plan.replicas
    any_space = pl.BlockSpec(memory_space=pl.ANY)
    dma = pltpu.SemaphoreType.DMA
    members = replicas * plan.capacity
    refreshed, mass = pl.pallas_call(
        lambda *refs: fused_kernel(plan, *refs),
        out_shape=(
            pltpu.VMEM(centroids.shape, jnp.bfloat16),
            pltpu.VMEM((split, half, 8, plan.fine), jnp.float32),
        ),
        in_specs=[pl.BlockSpec(memory_space=pltpu.HBM)] * 6,
        out_specs=(any_space, any_space),
        scratch_shapes=[
            pltpu.SMEM((plan.lists,), jnp.int32),
            pltpu.VMEM((plan.moving, plan.features), jnp.bfloat16),
            pltpu.VMEM((1, plan.moving), jnp.int32),
            pltpu.SMEM((plan.lists,), jnp.float32),
            dma((4,)),
            pltpu.VMEM((half, plan.fine, plan.features), jnp.float32),
            pltpu.VMEM((half, plan.fine, LANES), jnp.float32),
            pltpu.VMEM((half, plan.fine, LANES), jnp.float32),
            pltpu.VMEM((half, replicas, plan.capacity, plan.features), jnp.bfloat16),
            pltpu.VMEM((replicas, plan.lists, members), jnp.int32),
            pltpu.VMEM((max(1, plan.groups - 1), plan.moving, plan.features), jnp.bfloat16),
            pltpu.VMEM((8, plan.moving_lanes), jnp.int32),
            pltpu.VMEM((max(1, plan.groups - 1), 8, plan.moving_lanes), jnp.int32),
            pltpu.VMEM((plan.groups, plan.blocks, plan.per_source, plan.width), jnp.bfloat16),
            pltpu.VMEM((plan.groups, plan.blocks, plan.per_source, plan.width), jnp.bfloat16),
            pltpu.VMEM((half, plan.fine, plan.features), jnp.bfloat16),
            pltpu.VMEM((half, plan.fine, plan.features), jnp.bfloat16),
            pltpu.VMEM((half, 8, plan.fine), jnp.float32),
            dma((half, replicas)), dma((half, replicas)),
            dma((replicas,)), dma((replicas,)),
            dma((plan.groups,)), dma((plan.groups,)),
            dma((plan.groups,)), dma((plan.groups,)),
            dma((plan.groups, plan.blocks)), dma((plan.groups, plan.blocks)),
            dma,
            dma((half, split)), dma((half, split)),
            dma((split,)), dma((split,)),
            dma,
        ],
        compiler_params=pltpu.CompilerParams(
            collective_id=0, has_side_effects=True, vmem_limit_bytes=VMEM_GRANT
        ),
    )(*[
        pltpu.with_memory_space_constraint(x, pltpu.HBM)
        for x in (
            stay_rows, stay_count.reshape(-1), moving_rows, new_list.reshape(1, -1), centroids,
            sharpness,
        )
    ])
    fine_share = plan.fine // replicas
    whole = mass[:, :, 0, :].reshape(plan.lists, plan.fine)
    share = lax.dynamic_slice_in_dim(whole, lax.axis_index("rep") * fine_share, fine_share, 1)
    return refreshed, share


def device_program(stay_rows, stay_count, moving_rows, new_list, centroids, sharpness):
    lists_here, capacity, features = stay_rows.shape
    plan = Plan(
        lax.axis_size("owner"), lax.axis_size("rep"), lists_here, capacity, features,
        centroids.shape[1], moving_rows.shape[0],
    )
    step = (lambda *a: fused(plan, *a)) if plan.fits() else local
    return step(stay_rows, stay_count, moving_rows, new_list, centroids, sharpness)


def solution(mesh):
    in_specs = (
        P("owner", "rep", None),
        P("owner", "rep"),
        P(("owner", "rep"), None),
        P(("owner", "rep")),
        P("owner", None, None),
        P("owner"),
    )
    out_specs = (P("owner", None, None), P("owner", "rep"))
    return jax.shard_map(device_program, mesh=mesh, in_specs=in_specs, out_specs=out_specs, check_vma=False)
```

```python
import math

import jax
import jax.numpy as jnp
from jax import lax
from jax.experimental import pallas as pl
from jax.experimental.pallas import tpu as pltpu
from jax.sharding import PartitionSpec as P

SLOT_L = 2


prior_weight = 1.0


def partner(value, axis, stride):
    mask = 2**stride
    pairs = [(source, source ^ mask) for source in range(lax.axis_size(axis))]
    return lax.ppermute(value, axis, pairs)


def weigh(members, live_mask, centres, centre_norm, sharp, features):
    products = jnp.einsum("lrd,lfd->lrf", members, centres, preferred_element_type=jnp.float32)
    scores = sharp[:, None, None] * (2.0 * products - centre_norm[:, None, :]) / math.sqrt(features)
    weights = jax.nn.softmax(scores, axis=-1).astype(jnp.bfloat16) * live_mask[:, :, None]
    numerator = jnp.einsum("lrf,lrd->lfd", weights, members, preferred_element_type=jnp.float32)
    return (numerator, jnp.sum(weights.astype(jnp.float32), axis=1))


def local(stay_rows, stay_count, moving_rows, new_list, centroids, sharpness):
    owners = lax.axis_size("owner")
    replicas = lax.axis_size("rep")
    lists_here, capacity, features = stay_rows.shape
    fine_count = centroids.shape[1]
    centre_norm = jnp.sum(jnp.square(centroids.astype(jnp.float32)), axis=-1)
    outgoing_count = new_list.shape[0]
    order_index = jnp.arange(outgoing_count)
    earlier = (new_list[None, :] == new_list[:, None]) & (
        order_index[None, :] < order_index[:, None]
    )
    slot_index = jnp.sum(earlier.astype(jnp.int32), axis=1)
    local_list = new_list % lists_here
    target_owner = new_list // lists_here
    position = (local_list * owners + target_owner) * SLOT_L + slot_index
    slot_total = lists_here * owners * SLOT_L
    outgoing = (
        jnp.zeros((slot_total, features), jnp.bfloat16)
        .at[position]
        .set(moving_rows, unique_indices=True)
    )
    occupied = (
        jnp.zeros((slot_total,), jnp.bfloat16)
        .at[position]
        .set(jnp.ones((outgoing_count,), jnp.bfloat16), unique_indices=True)
    )
    arrived, present = (
        lax.all_to_all(
            outgoing.reshape(lists_here, owners, SLOT_L, features),
            "owner",
            split_axis=1,
            concat_axis=1,
            tiled=True,
        ),
        lax.all_to_all(
            occupied.reshape(lists_here, owners, SLOT_L),
            "owner",
            split_axis=1,
            concat_axis=1,
            tiled=True,
        ),
    )
    arrive_slots = owners * SLOT_L
    arrivals = arrived.reshape(lists_here, arrive_slots, features)
    present = present.reshape(lists_here, arrive_slots)
    live_count = stay_count[:, 0]
    replica = lax.axis_index("rep")
    fine_share = fine_count // replicas
    groups = max(1, replicas // lists_here)
    per_rep = max(1, lists_here // replicas)
    slot_mask = (jnp.arange(capacity)[None, :] < live_count[:, None]).astype(jnp.bfloat16)
    stay_pieces = stay_rows.reshape(lists_here * groups, capacity // groups, features)
    mask_pieces = slot_mask.reshape(lists_here * groups, capacity // groups)
    moved_stay, moved_mask = (
        lax.all_to_all(stay_pieces, "rep", split_axis=0, concat_axis=1, tiled=True),
        lax.all_to_all(mask_pieces, "rep", split_axis=0, concat_axis=1, tiled=True),
    )
    arrive_pieces = arrivals.reshape(lists_here * groups, arrive_slots // groups, features)
    present_pieces = present.reshape(lists_here * groups, arrive_slots // groups)
    moved_arrive, moved_present = (
        lax.all_to_all(arrive_pieces, "rep", split_axis=0, concat_axis=1, tiled=True),
        lax.all_to_all(present_pieces, "rep", split_axis=0, concat_axis=1, tiled=True),
    )
    members = jnp.concatenate([moved_stay, moved_arrive], axis=1)
    member_mask = jnp.concatenate([moved_mask, moved_present], axis=1)
    first_list = replica * per_rep // groups
    centres = lax.dynamic_slice_in_dim(centroids, first_list, per_rep, 0)
    norms = lax.dynamic_slice_in_dim(centre_norm, first_list, per_rep, 0)
    sharp = lax.dynamic_slice_in_dim(sharpness, first_list, per_rep, 0)
    numerator, mass_sum = weigh(members, member_mask, centres, norms, sharp, features)
    for bit_number in range(groups.bit_length() - 1):
        other_num, other_mass = partner((numerator, mass_sum), "rep", bit_number)
        numerator = numerator + other_num
        mass_sum = mass_sum + other_mass
    refreshed_all = (
        (numerator + prior_weight * centres.astype(jnp.float32))
        / (mass_sum[:, :, None] + prior_weight)
    ).astype(jnp.bfloat16)
    piece_rows = fine_count // groups
    part_index = replica % groups
    refreshed_piece = lax.dynamic_slice_in_dim(
        refreshed_all, part_index * piece_rows, piece_rows, 1
    ).reshape(per_rep * piece_rows, features)
    mass_piece = lax.dynamic_slice_in_dim(mass_sum, part_index * piece_rows, piece_rows, 1).reshape(
        per_rep * piece_rows
    )
    refreshed = lax.all_gather(refreshed_piece, "rep", axis=0, tiled=True).reshape(
        lists_here, fine_count, features
    )
    mass_whole = lax.all_gather(mass_piece, "rep", axis=0, tiled=True).reshape(
        lists_here, fine_count
    )
    return (refreshed, lax.dynamic_slice_in_dim(mass_whole, replica * fine_share, fine_share, 1))


LANES = 128
VMEM_BUDGET = 40 * 2**20
VMEM_GRANT = 48 * 2**20
MESH = pl.DeviceIdType.MESH


class Plan:
    def __init__(self, owners, replicas, lists, capacity, features, fine, moving):
        self.owners, self.replicas, self.lists = owners, replicas, lists
        self.capacity, self.features, self.fine, self.moving = capacity, features, fine, moving
        self.split = 2 if replicas % 2 == 0 and lists % 2 == 0 else 1
        self.groups = replicas // self.split
        self.half = lists // self.split
        self.per_source = self.half * SLOT_L
        self.block = self.groups * self.per_source
        self.blocks = owners * self.split
        self.width = features + LANES
        self.moving_lanes = -(-moving // LANES) * LANES

    def fits(self):
        slots = 2 * self.blocks * self.block * self.width
        held = self.half * self.replicas * self.capacity * self.features
        centres = 2 * self.half * self.fine * self.features
        gathered = self.groups * self.moving * self.features
        small = 2 * (slots + held + centres + gathered)
        return (
            small <= VMEM_BUDGET
            and self.per_source % 8 == 0
            and self.capacity % 16 == 0
            and self.moving % 16 == 0
            and self.features % LANES == 0
            and self.fine % LANES == 0
        )


def weigh_rows(plan, centres, norm, sharp, rows, mask):
    products = lax.dot_general(
        centres, rows, (((1,), (1,)), ((), ())), preferred_element_type=jnp.float32
    )
    scores = sharp * (2.0 * products - norm) / math.sqrt(plan.features)
    top = jnp.max(scores, axis=0, keepdims=True)
    raised = jnp.exp(scores - top)
    weights = (raised / jnp.sum(raised, axis=0, keepdims=True)).astype(jnp.bfloat16)
    weights = weights * mask.astype(jnp.bfloat16)
    numerator = jnp.dot(weights, rows, preferred_element_type=jnp.float32)
    mass = jnp.sum(weights.astype(jnp.float32), axis=1, keepdims=True)
    ones = jnp.ones((8, rows.shape[0]), jnp.bfloat16)
    mass_row = lax.dot_general(
        ones, weights, (((1,), (1,)), ((), ())), preferred_element_type=jnp.float32
    )
    return numerator, mass, mass_row


def fused_kernel(
    plan,
    stay_ref, count_in, moving_ref, list_in, centre_ref, sharp_in,
    out_ref, mass_ref,
    count_ref, moving_own, list_ref, sharp_ref, operand_sem, total_buf, mass_col, norm_buf,
    stay_buf, count_buf, moving_buf, pos_own, pos_buf, placed, arrived, centre_buf, result_buf, mass_buf,
    stay_send, stay_recv, count_send, count_recv, moving_send, moving_recv, pos_send, pos_recv,
    slot_send, slot_recv, centre_sem, result_send, result_recv, mass_send, mass_recv, local_sem,
):
    owners, split, groups, half = plan.owners, plan.split, plan.groups, plan.half
    replicas, capacity, features = plan.replicas, plan.capacity, plan.features
    owner = lax.axis_index("owner")
    replica = lax.axis_index("rep")
    core = replica % split
    group = replica // split

    def rep_at(k, dc):
        return lax.rem(group + k, groups) * split + lax.rem(core + dc, split)

    def owner_at(k):
        return lax.rem(owner + k, owners)

    peers = [(k, dc) for k in range(groups) for dc in range(split) if (k, dc) != (0, 0)]
    plane = [(k, dc) for k in range(1, owners) for dc in range(split)]
    barrier = pltpu.get_barrier_semaphore()
    for k, dc in peers:
        pl.semaphore_signal(barrier, inc=1, device_id=(owner, rep_at(k, dc)), device_id_type=MESH)
    for k, dc in plane:
        pl.semaphore_signal(
            barrier, inc=1, device_id=(owner_at(k), rep_at(0, dc)), device_id_type=MESH
        )

    small = [
        pltpu.make_async_copy(source, held, operand_sem.at[i])
        for i, (source, held) in enumerate([
            (list_in, list_ref), (count_in, count_ref), (moving_ref, moving_own), (sharp_in, sharp_ref),
        ])
    ]
    for copy in small:
        copy.start()
    centre_copy = pltpu.make_async_copy(
        centre_ref.at[pl.ds(core * half, half)], centre_buf, centre_sem
    )
    centre_copy.start()

    def own_copy(j):
        return pltpu.make_async_copy(
            stay_ref.at[core * half + j], stay_buf.at[j, 0], stay_recv.at[j, 0]
        )

    for j in range(half):
        own_copy(j).start()

    pl.semaphore_wait(barrier, len(peers) + len(plane))

    def moving_copy(k):
        return pltpu.make_async_remote_copy(
            src_ref=moving_ref, dst_ref=moving_buf.at[k - 1],
            send_sem=moving_send.at[k - 1], recv_sem=moving_recv.at[k - 1],
            device_id=(owner, rep_at(k, 0)), device_id_type=MESH,
        )

    def pos_copy(k):
        return pltpu.make_async_remote_copy(
            src_ref=pos_own, dst_ref=pos_buf.at[k - 1],
            send_sem=pos_send.at[k - 1], recv_sem=pos_recv.at[k - 1],
            device_id=(owner, rep_at(k, 0)), device_id_type=MESH,
        )

    for k in range(1, groups):
        moving_copy(k).start()

    def count_copy(k, dc):
        q = k * split + dc
        return pltpu.make_async_remote_copy(
            src_ref=count_buf.at[0], dst_ref=count_buf.at[q],
            send_sem=count_send.at[q], recv_sem=count_recv.at[q],
            device_id=(owner, rep_at(k, dc)), device_id_type=MESH,
        )

    def stay_copy(j, k, dc):
        q = k * split + dc
        return pltpu.make_async_remote_copy(
            src_ref=stay_ref.at[lax.rem(core + dc, split) * half + j], dst_ref=stay_buf.at[j, q],
            send_sem=stay_send.at[j, q], recv_sem=stay_recv.at[j, q],
            device_id=(owner, rep_at(k, dc)), device_id_type=MESH,
        )

    siblings = [(k, dc) for k, dc in peers if k == 0]
    distant = [(k, dc) for k, dc in peers if k > 0]
    ahead = min(2 * len(distant), half * len(distant))
    if distant:
        stay_copy(0, *distant[0]).start()

    moving = plan.moving
    small[0].wait()
    small[1].wait()
    line = lax.broadcasted_iota(jnp.int32, count_buf.shape[1:], 0)
    live = jnp.zeros(count_buf.shape[1:], jnp.int32)
    for i in range(plan.lists):
        live = jnp.where(line == i, count_ref[i], live)
    count_buf[0] = live
    names = jnp.broadcast_to(list_ref[...], (moving, moving))
    row = lax.broadcasted_iota(jnp.int32, (moving, moving), 0)
    column = lax.broadcasted_iota(jnp.int32, (moving, moving), 1)
    down = jnp.sum(jnp.where(row == column, names, 0), axis=1, keepdims=True)
    earlier = jnp.where((names == down) & (row < column), 1, 0)
    slot = jnp.sum(earlier, axis=0, keepdims=True)
    target = list_ref[...]
    position = (
        (target // half) * plan.per_source + (target % half) * SLOT_L + slot
    )
    pos_own[...] = jnp.full(pos_own.shape, -1, jnp.int32)
    pos_own[:, :moving] = jnp.broadcast_to(position, (8, moving))
    for k in range(1, groups):
        pos_copy(k).start()
    for k, dc in peers:
        count_copy(k, dc).start()
    small[2].wait()
    small[3].wait()

    sent = [(k, dc) for k in range(owners) for dc in range(split) if (k, dc) != (0, 0)]
    slots = plan.blocks * plan.per_source
    slot_row = lax.broadcasted_iota(jnp.int32, (slots, moving), 0)
    ones = jnp.ones((moving, LANES), jnp.bfloat16)

    def slot_copy(g, k, dc):
        b = k * split + dc
        return pltpu.make_async_remote_copy(
            src_ref=placed.at[g, owner_at(k) * split + lax.rem(core + dc, split)],
            dst_ref=arrived.at[g, b],
            send_sem=slot_send.at[g, b], recv_sem=slot_recv.at[g, b],
            device_id=(owner_at(k), rep_at(0, dc)), device_id_type=MESH,
        )

    def place_group(g, positions, source):
        pick = jnp.where(slot_row == positions, 1.0, 0.0).astype(jnp.bfloat16)
        rows = jnp.dot(pick, source, preferred_element_type=jnp.float32)
        flags = jnp.dot(pick, ones, preferred_element_type=jnp.float32)
        shape = (plan.blocks, plan.per_source)
        placed[g, :, :, :features] = rows.reshape(*shape, features).astype(jnp.bfloat16)
        placed[g, :, :, features:] = flags.reshape(*shape, LANES).astype(jnp.bfloat16)
        for k, dc in sent:
            slot_copy(g, k, dc).start()
        arrived[g, 0] = placed[g, owner * split + core]

    place_group(0, pos_own[0:1, :moving], moving_own[...])
    for i in range(1, ahead):
        j, place = divmod(i, len(distant))
        stay_copy(j, *distant[place]).start()
    for k in range(1, groups):
        pos_copy(k).wait_recv()
        moving_copy(k).wait_recv()
        place_group(k, pos_buf[k - 1, 0:1, :moving], moving_buf[k - 1])
    for j in range(half):
        for k, dc in siblings:
            stay_copy(j, k, dc).start()
    total = groups * slots
    centre_copy.wait()
    for j in range(half):
        wide = centre_buf[j].astype(jnp.float32)
        norm_buf[j] = jnp.broadcast_to(
            jnp.sum(wide * wide, axis=1, keepdims=True), norm_buf.shape[1:]
        )
    for k, dc in peers:
        count_copy(k, dc).wait_recv()

    arrived_lane = lax.broadcasted_iota(jnp.int32, (1, total), 1)
    arrived_list = (arrived_lane % plan.per_source) // SLOT_L

    def result_copy(j, dc):
        return pltpu.make_async_remote_copy(
            src_ref=result_buf.at[j], dst_ref=out_ref.at[core * half + j],
            send_sem=result_send.at[j, dc], recv_sem=result_recv.at[j, dc],
            device_id=(owner, rep_at(0, dc)), device_id_type=MESH,
        )

    def result_own(j):
        return pltpu.make_async_copy(
            result_buf.at[j], out_ref.at[core * half + j], result_recv.at[j, 0]
        )

    def add_part(j, rows, mask):
        num, mass, mass_row = weigh_rows(
            plan, centre_buf[j], norm_buf[j][:, 0:1], sharp_ref[core * half + j], rows, mask
        )
        total_buf[j] += num
        mass_col[j] += jnp.broadcast_to(mass, mass_col.shape[1:])
        mass_buf[j] += mass_row

    def add_stay(j, first, last):
        lane = lax.broadcasted_iota(jnp.int32, (1, (last - first) * capacity), 1)
        counts = jnp.zeros(lane.shape, jnp.int32)
        for q in range(first, last):
            counts = jnp.where(
                lane // capacity == q - first,
                count_buf[q, pl.ds(core * half + j, 1), :][:, : lane.shape[1]], counts,
            )
        mask = jnp.where(lane % capacity < counts, 1.0, 0.0)
        members = stay_buf[j, first:last].reshape((last - first) * capacity, features)
        add_part(j, members, mask)

    def add_arrivals():
        fine = plan.fine
        rows = arrived[:, :, :, :features].reshape(total, features)
        marks = arrived[:, :, :, features:].reshape(total, LANES)
        spread = jnp.full((8, LANES), 1.0 / LANES, jnp.bfloat16)
        present = lax.dot_general(
            spread, marks, (((1,), (1,)), ((), ())), preferred_element_type=jnp.float32
        )[0:1]
        products = lax.dot_general(
            centre_buf[...].reshape(half * fine, features), rows, (((1,), (1,)), ((), ())),
            preferred_element_type=jnp.float32,
        )
        parts = []
        for j in range(half):
            own = products[j * fine : (j + 1) * fine]
            sharp = sharp_ref[core * half + j]
            scores = sharp * (2.0 * own - norm_buf[j][:, 0:1]) / math.sqrt(features)
            raised = jnp.exp(scores - jnp.max(scores, axis=0, keepdims=True))
            weights = (raised / jnp.sum(raised, axis=0, keepdims=True)).astype(jnp.bfloat16)
            here = jnp.where(arrived_list == j, present, 0.0)
            weights = weights * here.astype(jnp.bfloat16)
            mass = jnp.sum(weights.astype(jnp.float32), axis=1, keepdims=True)
            mass_col[j] += jnp.broadcast_to(mass, mass_col.shape[1:])
            parts.append(weights)
        stacked = jnp.concatenate(parts, axis=0)
        ones = jnp.ones((8, total), jnp.bfloat16)
        mass_row = lax.dot_general(
            ones, stacked, (((1,), (1,)), ((), ())), preferred_element_type=jnp.float32
        )
        numerator = jnp.dot(stacked, rows, preferred_element_type=jnp.float32)
        for j in range(half):
            mass_buf[j] += mass_row[:, j * fine : (j + 1) * fine]
            total_buf[j] += numerator[j * fine : (j + 1) * fine]

    def add_near(j):
        total_buf[j] = prior_weight * centre_buf[j].astype(jnp.float32)
        mass_col[j] = jnp.zeros(mass_col.shape[1:], jnp.float32)
        mass_buf[j] = jnp.zeros(mass_buf.shape[1:], jnp.float32)
        own_copy(j).wait()
        for k, dc in siblings:
            stay_copy(j, k, dc).wait_recv()
        add_stay(j, 0, split)

    def pass_on(j):
        for i, (k, dc) in enumerate(distant):
            stay_copy(j, k, dc).wait_send()
            step, place = divmod(i + ahead, len(distant))

            @pl.when(j + step < half)
            def _():
                stay_copy(j + step, *distant[place]).start()

    def add_far(j):
        for k, dc in distant:
            stay_copy(j, k, dc).wait_recv()
        if groups > 1:
            add_stay(j, split, replicas)

    def finish(j):
        share = 1.0 / (mass_col[j][:, 0:1] + prior_weight)
        result_buf[j] = (total_buf[j] * share).astype(jnp.bfloat16)
        result_own(j).start()
        for dc in range(1, split):
            result_copy(j, dc).start()

    def early(j, carry):
        add_near(j)
        pass_on(j)
        add_far(j)
        return carry

    def settle(j, carry):
        finish(j)
        return carry

    last = half - 1
    lax.fori_loop(0, last, early, 0)
    add_near(last)
    for g in range(groups):
        for k, dc in sent:
            slot_copy(g, k, dc).wait_recv()
    add_arrivals()
    lax.fori_loop(0, last, settle, 0)
    for k, dc in distant:
        stay_copy(last, k, dc).wait_recv()
        add_stay(last, k * split + dc, k * split + dc + 1)
    finish(last)

    def mass_copy(dc):
        return pltpu.make_async_remote_copy(
            src_ref=mass_buf, dst_ref=mass_ref.at[core],
            send_sem=mass_send.at[dc], recv_sem=mass_recv.at[dc],
            device_id=(owner, rep_at(0, dc)), device_id_type=MESH,
        )

    mass_own = pltpu.make_async_copy(mass_buf, mass_ref.at[core], local_sem)
    mass_own.start()
    for dc in range(1, split):
        mass_copy(dc).start()

    for k in range(1, groups):
        pos_copy(k).wait_send()
        moving_copy(k).wait_send()
    for k, dc in peers:
        count_copy(k, dc).wait_send()
    for k, dc in distant:
        stay_copy(last, k, dc).wait_send()
    for j in range(half):
        for k, dc in siblings:
            stay_copy(j, k, dc).wait_send()
    for g in range(groups):
        for k, dc in sent:
            slot_copy(g, k, dc).wait_send()
    for j in range(half):
        result_own(j).wait()
        for dc in range(1, split):
            result_copy(j, dc).wait()
    mass_own.wait()
    for dc in range(1, split):
        mass_copy(dc).wait()


def fused(plan, stay_rows, stay_count, moving_rows, new_list, centroids, sharpness):
    half, split, replicas = plan.half, plan.split, plan.replicas
    any_space = pl.BlockSpec(memory_space=pl.ANY)
    dma = pltpu.SemaphoreType.DMA
    members = replicas * plan.capacity
    refreshed, mass = pl.pallas_call(
        lambda *refs: fused_kernel(plan, *refs),
        out_shape=(
            pltpu.VMEM(centroids.shape, jnp.bfloat16),
            pltpu.VMEM((split, half, 8, plan.fine), jnp.float32),
        ),
        in_specs=[pl.BlockSpec(memory_space=pltpu.HBM)] * 6,
        out_specs=(any_space, any_space),
        scratch_shapes=[
            pltpu.SMEM((plan.lists,), jnp.int32),
            pltpu.VMEM((plan.moving, plan.features), jnp.bfloat16),
            pltpu.VMEM((1, plan.moving), jnp.int32),
            pltpu.SMEM((plan.lists,), jnp.float32),
            dma((4,)),
            pltpu.VMEM((half, plan.fine, plan.features), jnp.float32),
            pltpu.VMEM((half, plan.fine, LANES), jnp.float32),
            pltpu.VMEM((half, plan.fine, LANES), jnp.float32),
            pltpu.VMEM((half, replicas, plan.capacity, plan.features), jnp.bfloat16),
            pltpu.VMEM((replicas, plan.lists, members), jnp.int32),
            pltpu.VMEM((max(1, plan.groups - 1), plan.moving, plan.features), jnp.bfloat16),
            pltpu.VMEM((8, plan.moving_lanes), jnp.int32),
            pltpu.VMEM((max(1, plan.groups - 1), 8, plan.moving_lanes), jnp.int32),
            pltpu.VMEM((plan.groups, plan.blocks, plan.per_source, plan.width), jnp.bfloat16),
            pltpu.VMEM((plan.groups, plan.blocks, plan.per_source, plan.width), jnp.bfloat16),
            pltpu.VMEM((half, plan.fine, plan.features), jnp.bfloat16),
            pltpu.VMEM((half, plan.fine, plan.features), jnp.bfloat16),
            pltpu.VMEM((half, 8, plan.fine), jnp.float32),
            dma((half, replicas)), dma((half, replicas)),
            dma((replicas,)), dma((replicas,)),
            dma((plan.groups,)), dma((plan.groups,)),
            dma((plan.groups,)), dma((plan.groups,)),
            dma((plan.groups, plan.blocks)), dma((plan.groups, plan.blocks)),
            dma,
            dma((half, split)), dma((half, split)),
            dma((split,)), dma((split,)),
            dma,
        ],
        compiler_params=pltpu.CompilerParams(
            collective_id=0, has_side_effects=True, vmem_limit_bytes=VMEM_GRANT
        ),
    )(*[
        pltpu.with_memory_space_constraint(x, pltpu.HBM)
        for x in (
            stay_rows, stay_count.reshape(-1), moving_rows, new_list.reshape(1, -1), centroids,
            sharpness,
        )
    ])
    fine_share = plan.fine // replicas
    whole = mass[:, :, 0, :].reshape(plan.lists, plan.fine)
    share = lax.dynamic_slice_in_dim(whole, lax.axis_index("rep") * fine_share, fine_share, 1)
    return refreshed, share


def device_program(stay_rows, stay_count, moving_rows, new_list, centroids, sharpness):
    lists_here, capacity, features = stay_rows.shape
    plan = Plan(
        lax.axis_size("owner"), lax.axis_size("rep"), lists_here, capacity, features,
        centroids.shape[1], moving_rows.shape[0],
    )
    step = (lambda *a: fused(plan, *a)) if plan.fits() else local
    return step(stay_rows, stay_count, moving_rows, new_list, centroids, sharpness)


def solution(mesh):
    in_specs = (
        P("owner", "rep", None),
        P("owner", "rep"),
        P(("owner", "rep"), None),
        P(("owner", "rep")),
        P("owner", None, None),
        P("owner"),
    )
    out_specs = (P("owner", None, None), P("owner", "rep"))
    return jax.shard_map(device_program, mesh=mesh, in_specs=in_specs, out_specs=out_specs, check_vma=False)
```
